32 devices in a mesh: groups: 2 (over y), seq: 4 (over z), head: 2 (over x), sub: 2 (over core).
Axes of the slice: x: 2, y: 2, z: 4, core: 2. Of those that a mesh axis runs over, the one named last changes fastest.
Arguments:
- hidden: bfloat16 [8, 4, 8192], P('groups', None, ('head', 'sub')), parts along dimension 0, may hold values from -2.5 to 2.5
- query: bfloat16 [8, 4, 64, 128], P('groups', None, ('head', 'sub')), parts along dimension 0, may hold values from -4096 to 4096
- key_new: bfloat16 [8, 4, 8, 128], P('groups', None, ('head', 'sub')), parts along dimension 0, may hold values from -16 to 16
- value_new: bfloat16 [8, 4, 8, 128], P('groups', None, ('head', 'sub')), parts along dimension 0, may hold values from -12 to 12
- kv_cache: bfloat16 [2, 8, 1024, 8, 128], P(None, 'groups', 'seq', ('head', 'sub')), parts along dimension 1, may hold values from -127 to 127, as said below
- kv_scale: float32 [2, 8, 8, 8], P(None, 'groups', ('head', 'sub'), 'seq'), parts along dimension 1, may hold values from 0.004 to 0.032
- context_len: int32 [8], P('groups'), parts along dimension 0, may hold values from 128 to 1024
- attn_out_weight: bfloat16 [8192, 8192], P('seq', ('head', 'sub')), may hold values from -0.0625 to 0.0625
- norm_gain: float32 [8192], P(('head', 'sub')), may hold values from 0.5 to 1.5
- in_weight: bfloat16 [2, 8192, 16384], P(None, ('head', 'sub'), 'seq'), may hold values from -0.0625 to 0.0625
- conv_weight: bfloat16 [16384, 4], P(('seq', 'head', 'sub')), may hold values from -3 to 3
- conv_bias: float32 [16384], P(('seq', 'head', 'sub')), may hold values from -3 to 3
- conv_state: bfloat16 [8, 3, 16384], P('groups', None, ('seq', 'head', 'sub')), parts along dimension 0, may hold values from -6 to 6
- xproj_weight: bfloat16 [16384, 544], P(('seq', 'head', 'sub')), may hold values from -0.046875 to 0.046875
- dt_weight: bfloat16 [512, 16384], P(None, ('seq', 'head', 'sub')), may hold values from -0.25 to 0.25
- dt_bias: float32 [16384], P(('seq', 'head', 'sub')), may hold values from -3 to 0
- decay_rate: float32 [16384, 16], P(('seq', 'head', 'sub')), may hold values from 0.05 to 8
- skip_gain: float32 [16384], P(('seq', 'head', 'sub')), may hold values from 0.5 to 1.5
- ssm_state: float32 [8, 16384, 16], P('groups', ('seq', 'head', 'sub')), parts along dimension 0, may hold values from -6 to 6
- mamba_out_weight: bfloat16 [16384, 8192], P('seq', ('head', 'sub')), may hold values from -0.046875 to 0.046875
Outputs:
- layer_out: bfloat16 [8, 4, 8192], P('groups', None, ('head', 'sub')), parts along dimension 0
- ssm_next: float32 [8, 16384, 16], P('groups', ('seq', 'head', 'sub')), parts along dimension 0
The draws below stay inside these ranges and needn't reach their ends.
There are 2 independent parts, one for each index of `groups`. The reference program is written for one: setup_inputs(seed, part) draws one part's arguments, and reference() takes and returns one part's arrays. A program takes and returns all parts, laid end to end along the dimension named above; an argument that names none is the same for every part. Nothing has to cross between parts.
Inputs may be any that keep to these rules, and one draw needn't show every extreme that they name: `kv_cache`: whole numbers.
All inputs are finite; a program needn't handle non-finite values.
Results may differ from the reference program's by a relative error of at most 0.015.
Values may be sent and summed in bfloat16 or wider, within the bound.
No kernel may reach another device: no remote copies, remote signals or barrier semaphores. Data moves between devices by JAX's collectives and lax.ppermute only.
A program may use at most 128 MiB of HBM per device.

```python
import math
import jax
import jax.numpy as jnp
from jax import lax

REQ = 4
NEW = 4
BLOCK = 128
D = 8192
QH = 64
KVH = 8
HD = 128
CH = 16384
NS = 16
RANK = 512
KC = 4
CTX = 1024
XD = 544


def shared_draw(key):
    base_key = jax.random.fold_in(key, 4101)
    key_ints, key_scale, key_query = jax.random.split(base_key, 3)
    cache_ints = jax.random.randint(key_ints, (2, REQ, CTX, KVH, HD), -127, 128).astype(jnp.float32)
    scales = jnp.exp(jax.random.uniform(key_scale, (2, REQ, KVH, CTX // BLOCK), minval=math.log(0.004), maxval=math.log(0.032)))
    queries = jax.random.normal(key_query, (REQ, NEW, QH, HD))
    return (cache_ints, scales, queries)


def draw_query(key, part):
    return shared_draw(key)[2].astype(jnp.bfloat16)


def draw_kv_cache(key, part):
    return shared_draw(key)[0].astype(jnp.bfloat16)


def draw_kv_scale(key, part):
    return shared_draw(key)[1].astype(jnp.float32)


def with_ends(drawn, key, smallest, high):
    longest = drawn.shape.index(max(drawn.shape))
    spots = []
    for shift in (0, 1):
        where = [jax.random.randint(jax.random.fold_in(key, axis), (), 0, length) for axis, length in enumerate(drawn.shape)]
        where[longest] = (where[longest] + shift) % drawn.shape[longest]
        spots.append(tuple(where))
    return drawn.at[spots[0]].set(smallest).at[spots[1]].set(high)


def shard_levels(own_key, extent, cuts, low, top_value):
    loudness = 1.0
    for dim, shards_of in cuts:
        steps = jax.random.uniform(jax.random.fold_in(jax.random.fold_in(own_key, 6), dim), (shards_of,), jnp.float32, low / len(cuts), top_value / len(cuts))
        loudness = loudness * jnp.repeat(jnp.exp(steps), extent[dim] // shards_of).reshape((-1,) + (1,) * (len(extent) - 1 - dim))
    return loudness


def bell_draw(stream_key, extent, width, limit, pieces=(), held_as=jnp.bfloat16):
    result = jax.random.normal(stream_key, extent, jnp.float32) * width
    if len(pieces) > 0:
        result = shard_levels(stream_key, extent, pieces, -0.22, 0.18) * result
    return jnp.clip(result, min=-limit, max=limit).astype(held_as)


def setup_inputs(seed: int = 0, part: int = 0) -> dict:
    keys = jax.random.split(jax.random.key(seed), 21)
    part_splits = jax.random.split(jax.random.fold_in(keys[20], part), 21)
    return {
        "hidden": bell_draw(part_splits[0], (REQ, NEW, D), 0.5, 2.5, ((2, 4),)),
        "query": draw_query(jax.random.fold_in(jax.random.fold_in(keys[20], part), 71), part),
        "key_new": bell_draw(part_splits[2], (REQ, NEW, KVH, HD), 3.0, 16.0, ((2, 4),)),
        "value_new": bell_draw(part_splits[3], (REQ, NEW, KVH, HD), 2.0, 12.0, ((2, 4),)),
        "kv_cache": draw_kv_cache(jax.random.fold_in(jax.random.fold_in(keys[20], part), 71), part),
        "kv_scale": draw_kv_scale(jax.random.fold_in(jax.random.fold_in(keys[20], part), 71), part),
        "context_len": with_ends(jax.random.randint(part_splits[6], (REQ,), BLOCK, CTX + 1), jax.random.fold_in(part_splits[6], 1), BLOCK, CTX).astype(jnp.int32),
        "attn_out_weight": bell_draw(keys[7], (QH * HD, D), (QH * HD) ** -0.5, 0.0625, ((0, 4), (1, 4))),
        "norm_gain": jnp.clip(1.0 + 0.1 * jax.random.normal(keys[8], (D,), jnp.float32), 0.5, 1.5),
        "in_weight": bell_draw(keys[9], (2, D, CH), D ** -0.5, 0.0625, ((1, 4), (2, 4))),
        "conv_weight": bell_draw(keys[10], (CH, KC), 0.5, 3.0, ((0, 16),)),
        "conv_bias": bell_draw(keys[11], (CH,), 0.5, 3.0, ((0, 16),), jnp.float32),
        "conv_state": bell_draw(part_splits[12], (REQ, KC - 1, CH), 1.0, 6.0, ((2, 16),)),
        "xproj_weight": bell_draw(keys[13], (CH, XD), CH ** -0.5, 0.046875, ((0, 16),)),
        "dt_weight": bell_draw(keys[14], (RANK, CH), RANK ** -0.5, 0.25, ((1, 16),)),
        "dt_bias": jnp.clip(-3.0 + 3.0 * jax.random.uniform(keys[15], (CH,), jnp.float32) ** shard_levels(keys[15], (CH,), ((0, 16),), -0.2, 0.2), -3.0, 0.0),
        "decay_rate": jnp.clip(jnp.exp(math.log(8.0) - 5.075174 * jax.random.uniform(keys[16], (CH, NS), jnp.float32) ** shard_levels(keys[16], (CH, NS), ((0, 16),), -0.2, 0.2)), 0.05, 8.0),
        "skip_gain": jnp.clip(0.5 + 1.0 * jax.random.uniform(keys[17], (CH,), jnp.float32) ** shard_levels(keys[17], (CH,), ((0, 16),), -0.2, 0.2), 0.5, 1.5),
        "ssm_state": bell_draw(part_splits[18], (REQ, CH, NS), 1.0, 6.0, ((1, 16),), jnp.float32),
        "mamba_out_weight": bell_draw(keys[19], (CH, D), CH ** -0.5, 0.046875, ((0, 4), (1, 4))),
    }


epsilon = 1e-06

def rms_unit(values):
    return values * lax.rsqrt(lax.optimization_barrier(jnp.mean(values * values, axis=-1, keepdims=True)) + epsilon)

def reference(hidden, query, key_new, value_new, kv_cache, kv_scale, context_len, attn_out_weight, norm_gain, in_weight, conv_weight, conv_bias, conv_state, xproj_weight, dt_weight, dt_bias, decay_rate, skip_gain, ssm_state, mamba_out_weight):
    group_size = QH // KVH
    inv_root = 1.0 / math.sqrt(HD)
    queries = query.astype(jnp.float32).reshape(REQ, NEW, KVH, group_size, HD)
    cache_keys = kv_cache[0].astype(jnp.float32)
    cache_values = kv_cache[1].astype(jnp.float32)
    key_scale = jnp.repeat(kv_scale[0], BLOCK, axis=2)
    value_scale = jnp.repeat(kv_scale[1], BLOCK, axis=2)
    scores = jnp.einsum('rtkgd,rpkd->rtkgp', queries, cache_keys)
    scores = scores * key_scale[:, None, :, None, :] * inv_root
    position = jnp.arange(CTX, dtype=jnp.int32)
    is_live = (position[None, :] < context_len[:, None])[:, None, None, None, :]
    scores = jnp.where(is_live, scores, -1e+30)
    recent = jnp.einsum('rtkgd,rjkd->rtkgj', queries, key_new.astype(jnp.float32)) * inv_root
    order_new = jnp.arange(NEW, dtype=jnp.int32)
    causal = (order_new[None, :] <= order_new[:, None])[None, :, None, None, :]
    recent = jnp.where(causal, recent, -1e+30)
    best_score = jnp.maximum(lax.optimization_barrier(jnp.max(scores, axis=-1)), lax.optimization_barrier(jnp.max(recent, axis=-1)))
    cache_weight = jnp.where(is_live, jnp.exp(scores - best_score[..., None]), 0.0)
    recent_weight = jnp.where(causal, jnp.exp(recent - best_score[..., None]), 0.0)
    weight_sum = lax.optimization_barrier(jnp.sum(cache_weight, axis=-1)) + lax.optimization_barrier(jnp.sum(recent_weight, axis=-1))
    scaled_weight = (cache_weight * value_scale[:, None, :, None, :]).astype(jnp.bfloat16)
    recent_weight = recent_weight.astype(jnp.bfloat16)
    blended = jnp.einsum('rtkgp,rpkd->rtkgd', scaled_weight.astype(jnp.float32), cache_values)
    blended = blended + jnp.einsum('rtkgj,rjkd->rtkgd', recent_weight.astype(jnp.float32), value_new.astype(jnp.float32))
    head_rows = (blended / weight_sum[..., None]).astype(jnp.bfloat16).reshape(REQ * NEW, QH * HD)
    attended = jnp.dot(head_rows, attn_out_weight, preferred_element_type=jnp.float32)
    residual = hidden.astype(jnp.float32).reshape(REQ * NEW, D) + attended
    mean_square = lax.optimization_barrier(jnp.sum(residual * residual, axis=-1, keepdims=True)) / D
    normed = (residual * lax.rsqrt(mean_square + epsilon) * norm_gain).astype(jnp.bfloat16)
    projected = jnp.einsum('nd,cde->cne', normed.astype(jnp.float32), in_weight.astype(jnp.float32))
    conv_in = projected[0].astype(jnp.bfloat16)
    gate_in = projected[1].astype(jnp.bfloat16)
    window = jnp.concatenate([conv_state.astype(jnp.float32), conv_in.astype(jnp.float32).reshape(REQ, NEW, CH)], axis=1)
    conv_sum = jnp.zeros((REQ, NEW, CH), jnp.float32) + conv_bias
    for tap in range(KC):
        conv_sum = conv_sum + conv_weight[:, tap].astype(jnp.float32) * window[:, tap:tap + NEW, :]
    conv_out = jax.nn.silu(conv_sum).astype(jnp.bfloat16).reshape(REQ * NEW, CH)
    mixing = jnp.dot(conv_out, xproj_weight, preferred_element_type=jnp.float32)
    low_rank = rms_unit(mixing[:, :RANK]).astype(jnp.bfloat16)
    input_mat = rms_unit(mixing[:, RANK:RANK + NS]).reshape(REQ, NEW, NS)
    output_mat = rms_unit(mixing[:, RANK + NS:]).reshape(REQ, NEW, NS)
    delta = jax.nn.softplus(jnp.dot(low_rank, dt_weight, preferred_element_type=jnp.float32) + dt_bias).reshape(REQ, NEW, CH)
    signal = conv_out.astype(jnp.float32).reshape(REQ, NEW, CH)
    memory = ssm_state
    outputs = []
    for moment in range(NEW):
        step_now = delta[:, moment]
        memory = jnp.exp(-step_now[..., None] * decay_rate) * memory + (step_now * signal[:, moment])[..., None] * input_mat[:, moment][:, None, :]
        outputs.append(lax.optimization_barrier(jnp.sum(memory * output_mat[:, moment][:, None, :], axis=-1)) + skip_gain * signal[:, moment])
    stacked = jnp.stack(outputs, axis=1).reshape(REQ * NEW, CH)
    gated_out = (stacked * jax.nn.silu(gate_in.astype(jnp.float32))).astype(jnp.bfloat16)
    final = residual + jnp.dot(gated_out, mamba_out_weight, preferred_element_type=jnp.float32)
    return (final.astype(jnp.bfloat16).reshape(REQ, NEW, D), memory)
```

```python
import math

import jax
import jax.numpy as jnp
from jax import lax
from jax.sharding import PartitionSpec as P

BLOCK = 128
EPS = 1e-06
HS = ("head", "sub")
DIRECT = 8


def shifted(value, axes, hop):
    count = lax.axis_size(axes)
    return lax.ppermute(value, axes, [(i, (i + hop) % count) for i in range(count)])


def paired_sum(terms):
    if len(terms) == 1:
        return terms[0]
    return paired_sum(terms[::2]) + paired_sum(terms[1::2])


def everyone(value, axes):
    return [value] + [shifted(value, axes, hop) for hop in range(1, lax.axis_size(axes))]


def sum_over(value, axes, kind=None):
    if lax.axis_size(axes) > DIRECT:
        return lax.psum(value, axes)
    if kind is not None:
        value = lax.optimization_barrier(value.astype(kind))
    return paired_sum([part.astype(jnp.float32) for part in everyone(value, axes)])


def split_pair(value):
    upper = lax.reduce_precision(value, 8, 7)
    return upper, lax.reduce_precision(value - upper, 8, 7)


def split_three(value):
    upper, middle = split_pair(value)
    return upper, middle, lax.reduce_precision(value - upper - middle, 8, 7)


def rms_unit(values):
    return values * lax.rsqrt(jnp.mean(values * values, axis=-1, keepdims=True) + EPS)


def attention(query, key_new, value_new, kv_cache, kv_scale, context_len):
    requests, steps, heads, dim = query.shape
    kv_heads = key_new.shape[2]
    group = heads // kv_heads
    cache_len = kv_cache.shape[2]
    width = cache_len * kv_heads
    inv_root = 1.0 / math.sqrt(dim)
    first = lax.axis_index("seq") == 0
    flat_query = query.reshape(requests, steps * heads, dim)
    flat_cache = kv_cache.reshape(2, requests, width, dim)
    column = jnp.arange(width, dtype=jnp.int32)
    row = jnp.arange(steps * heads, dtype=jnp.int32)
    row_kv = (row % heads) // group
    same = row_kv[:, None] == (column % kv_heads)[None, :]
    place = lax.axis_index("seq") * cache_len + column // kv_heads
    live = same[None] & (place[None, :] < context_len[:, None])[:, None, :]
    spread = jnp.repeat(kv_scale.transpose(0, 1, 3, 2), BLOCK, axis=2).reshape(2, requests, width)
    scores = jnp.einsum("rqd,rpd->rqp", flat_query, flat_cache[0], preferred_element_type=jnp.float32)
    scores = jnp.where(live, scores * spread[0][:, None, :] * inv_root, -1e30)
    flat_new_k = key_new.reshape(requests, steps * kv_heads, dim)
    flat_new_v = value_new.reshape(requests, steps * kv_heads, dim)
    new_column = jnp.arange(steps * kv_heads, dtype=jnp.int32)
    new_live = (
        (row_kv[:, None] == (new_column % kv_heads)[None, :])
        & ((new_column // kv_heads)[None, :] <= (row // heads)[:, None])
        & first
    )[None]
    recent = jnp.einsum("rqd,rjd->rqj", flat_query, flat_new_k, preferred_element_type=jnp.float32)
    recent = jnp.where(new_live, recent * inv_root, -1e30)
    top = jnp.maximum(jnp.max(scores, axis=-1), jnp.max(recent, axis=-1))
    weight = jnp.where(live, jnp.exp(scores - top[..., None]), 0.0)
    new_weight = jnp.where(new_live, jnp.exp(recent - top[..., None]), 0.0)
    total = jnp.sum(weight, axis=-1) + jnp.sum(new_weight, axis=-1)
    scaled = (weight * spread[1][:, None, :]).astype(jnp.bfloat16)
    mix = jnp.einsum("rqp,rpd->rqd", scaled, flat_cache[1], preferred_element_type=jnp.float32)
    mix = mix + jnp.einsum(
        "rqj,rjd->rqd", new_weight.astype(jnp.bfloat16), flat_new_v, preferred_element_type=jnp.float32
    )
    rows = requests * steps
    return mix.reshape(rows, heads, dim), top.reshape(rows, heads), total.reshape(rows, heads)


def merge(mixes, tops, totals):
    best = tops[0]
    for top in tops[1:]:
        best = jnp.maximum(best, top)
    factors = [jnp.exp(top - best) for top in tops]
    summed = paired_sum([total * factor for total, factor in zip(totals, factors)])
    mixed = paired_sum(
        [mix.astype(jnp.float32) * factor[..., None] for mix, factor in zip(mixes, factors)]
    )
    return (mixed / summed[..., None]).astype(jnp.bfloat16)


def local(
    hidden,
    query,
    key_new,
    value_new,
    kv_cache,
    kv_scale,
    context_len,
    attn_out_weight,
    norm_gain,
    in_weight,
    conv_weight,
    conv_bias,
    conv_state,
    xproj_weight,
    dt_weight,
    dt_bias,
    decay_rate,
    skip_gain,
    ssm_state,
    mamba_out_weight,
):
    requests, steps = hidden.shape[:2]
    rows = requests * steps
    seq_count = lax.axis_size("seq")
    hs_count = lax.axis_size(HS)
    hs_index = lax.axis_index(HS)
    heads = query.shape[2]
    dim = query.shape[3]
    mix, top, total = attention(query, key_new, value_new, kv_cache, kv_scale, context_len)
    if seq_count == hs_count:
        packed = jnp.concatenate(
            [mix.reshape(rows, heads * dim)] + list(split_three(top)) + list(split_three(total)), axis=1
        ).astype(jnp.bfloat16)
        swap = [(s * hs_count + j, j * hs_count + s) for s in range(seq_count) for j in range(hs_count)]
        swapped = lax.ppermute(packed, ("seq",) + HS, swap)
        parts = everyone(lax.optimization_barrier(swapped), HS)
        base = heads * dim
        piece = lambda part, k: part[:, base + k * heads : base + (k + 1) * heads].astype(jnp.float32)
        three = lambda part, k: piece(part, k) + piece(part, k + 1) + piece(part, k + 2)
        chosen = merge(
            [part[:, :base].reshape(rows, heads, dim) for part in parts],
            [three(part, 0) for part in parts],
            [three(part, 3) for part in parts],
        ).reshape(rows, base)
    else:
        mixes, tops, totals = (lax.all_gather(part, "seq") for part in (mix, top, total))
        every = range(seq_count)
        own_heads = merge([mixes[k] for k in every], [tops[k] for k in every], [totals[k] for k in every])
        every_head = lax.all_gather(own_heads.reshape(rows, heads * dim), HS, axis=1, tiled=True)
        width_in = attn_out_weight.shape[0]
        chosen = lax.dynamic_slice_in_dim(every_head, lax.axis_index("seq") * width_in, width_in, 1)
    attended = sum_over(
        jnp.dot(chosen, attn_out_weight, preferred_element_type=jnp.float32), "seq", jnp.bfloat16
    )
    residual = hidden.astype(jnp.float32).reshape(rows, -1) + attended
    features = residual.shape[1] * hs_count
    squares = jnp.sum(residual * residual, axis=-1, keepdims=True)
    gained = (residual * norm_gain).astype(jnp.bfloat16)
    projected = jnp.einsum("nd,cde->nce", gained, in_weight, preferred_element_type=jnp.float32)
    own_width = conv_weight.shape[0]
    upper, lower = split_pair(squares)

    def block_for(index):
        block = lax.dynamic_slice_in_dim(projected, index * own_width, own_width, 2)
        return block.reshape(rows, 2 * own_width)

    channels = block_for(hs_index)
    for hop in range(1, hs_count):
        block = jnp.concatenate([block_for((hs_index + hop) % hs_count), upper, lower], axis=1)
        part = shifted(block.astype(jnp.bfloat16), HS, hop).astype(jnp.float32)
        channels = channels + part[:, : 2 * own_width]
        squares = squares + part[:, 2 * own_width : 2 * own_width + 1] + part[:, 2 * own_width + 1 :]
    channels = channels * lax.rsqrt(squares / features + EPS)
    conv_in = channels[:, :own_width].astype(jnp.bfloat16)
    gate_in = channels[:, own_width:].astype(jnp.bfloat16)
    window = jnp.concatenate(
        [
            conv_state.astype(jnp.float32),
            conv_in.astype(jnp.float32).reshape(requests, steps, own_width),
        ],
        axis=1,
    )
    conv_sum = jnp.zeros((requests, steps, own_width), jnp.float32) + conv_bias
    for tap in range(conv_weight.shape[1]):
        conv_sum = conv_sum + conv_weight[:, tap].astype(jnp.float32) * window[:, tap : tap + steps, :]
    conv_out = jax.nn.silu(conv_sum).astype(jnp.bfloat16).reshape(rows, own_width)
    mixing = jnp.dot(conv_out, xproj_weight, preferred_element_type=jnp.float32)
    mixing = sum_over(sum_over(mixing, HS), "seq")
    low_width = dt_weight.shape[0]
    state_width = decay_rate.shape[1]
    low_rank = rms_unit(mixing[:, :low_width]).astype(jnp.bfloat16)
    input_mat = rms_unit(mixing[:, low_width : low_width + state_width]).reshape(
        requests, steps, state_width
    )
    output_mat = rms_unit(mixing[:, low_width + state_width :]).reshape(requests, steps, state_width)
    delta = jax.nn.softplus(
        jnp.dot(low_rank, dt_weight, preferred_element_type=jnp.float32) + dt_bias
    ).reshape(requests, steps, own_width)
    signal = conv_out.astype(jnp.float32).reshape(requests, steps, own_width)
    memory = ssm_state
    outputs = []
    for moment in range(steps):
        step_now = delta[:, moment]
        memory = (
            jnp.exp(-step_now[..., None] * decay_rate) * memory
            + (step_now * signal[:, moment])[..., None] * input_mat[:, moment][:, None, :]
        )
        outputs.append(
            jnp.sum(memory * output_mat[:, moment][:, None, :], axis=-1)
            + skip_gain * signal[:, moment]
        )
    stacked = jnp.stack(outputs, axis=1).reshape(rows, own_width)
    gated_out = (stacked * jax.nn.silu(gate_in.astype(jnp.float32))).astype(jnp.bfloat16)
    gated_block = lax.all_gather(gated_out, HS, axis=1, tiled=True)
    mamba_part = sum_over(
        jnp.dot(gated_block, mamba_out_weight, preferred_element_type=jnp.float32), "seq", jnp.bfloat16
    )
    final = (residual + mamba_part).astype(jnp.bfloat16).reshape(requests, steps, -1)
    return (final, memory)


def solution(mesh):
    return jax.shard_map(
        local,
        mesh=mesh,
        in_specs=(
            P("groups", None, HS),
            P("groups", None, HS, None),
            P("groups", None, HS, None),
            P("groups", None, HS, None),
            P(None, "groups", "seq", HS, None),
            P(None, "groups", HS, "seq"),
            P("groups"),
            P("seq", HS),
            P(HS),
            P(None, HS, "seq"),
            P(("seq",) + HS, None),
            P(("seq",) + HS),
            P("groups", None, ("seq",) + HS),
            P(("seq",) + HS, None),
            P(None, ("seq",) + HS),
            P(("seq",) + HS),
            P(("seq",) + HS, None),
            P(("seq",) + HS),
            P("groups", ("seq",) + HS, None),
            P("seq", HS),
        ),
        out_specs=(P("groups", None, HS), P("groups", ("seq",) + HS, None)),
        check_vma=False,
    )
```

```python
import math

import jax
import jax.numpy as jnp
from jax import lax
from jax.experimental import pallas as pl
from jax.experimental.pallas import tpu as pltpu
from jax.sharding import PartitionSpec as P

BLOCK = 128
EPS = 1e-06
HS = ("head", "sub")
DIRECT = 8
LANES = 128
MIB = 1024 * 1024
FLOPS_AHEAD = 20_000_000_000


def shifted(value, axes, hop):
    count = lax.axis_size(axes)
    return lax.ppermute(value, axes, [(i, (i + hop) % count) for i in range(count)])


def paired_sum(terms):
    if len(terms) == 1:
        return terms[0]
    return paired_sum(terms[::2]) + paired_sum(terms[1::2])


def everyone(value, axes):
    return [value] + [shifted(value, axes, hop) for hop in range(1, lax.axis_size(axes))]


def sum_over(value, axes, kind=None):
    if lax.axis_size(axes) > DIRECT:
        return lax.psum(value, axes)
    if kind is not None:
        value = lax.optimization_barrier(value.astype(kind))
    return paired_sum([part.astype(jnp.float32) for part in everyone(value, axes)])


def split_pair(value):
    upper = lax.reduce_precision(value, 8, 7)
    return upper, lax.reduce_precision(value - upper, 8, 7)


def rms_unit(values):
    return values * lax.rsqrt(jnp.mean(values * values, axis=-1, keepdims=True) + EPS)


def tile_of(width, limit):
    tile = width
    while tile > limit and tile % 2 == 0 and (tile // 2) % 128 == 0:
        tile //= 2
    return tile


def whole(count):
    return [pl.BlockSpec(memory_space=pltpu.VMEM)] * count


def attention(query, key_new, value_new, kv_cache, kv_scale, context_len):
    requests, steps, heads, dim = query.shape
    kv_heads = key_new.shape[2]
    group = heads // kv_heads
    cache_len = kv_cache.shape[2]
    width = cache_len * kv_heads
    blocks = kv_scale.shape[3]
    inv_root = 1.0 / math.sqrt(dim)
    lines = steps * heads
    total_rows = requests * lines
    news = steps * kv_heads

    def kernel(length_ref, scale_ref, query_ref, cache_ref, key_ref, value_ref, out_ref):
        shard = lax.axis_index("seq")
        row = lax.broadcasted_iota(jnp.int32, (lines, width), 0)
        column = lax.broadcasted_iota(jnp.int32, (lines, width), 1)
        same = (row % heads) // group == column % kv_heads
        place = shard * cache_len + column // kv_heads
        new_row = lax.broadcasted_iota(jnp.int32, (lines, news), 0)
        new_column = lax.broadcasted_iota(jnp.int32, (lines, news), 1)
        new_live = (
            ((new_row % heads) // group == new_column % kv_heads)
            & (new_column // kv_heads <= new_row // heads)
            & (shard == 0)
        )
        parity = lax.broadcasted_iota(jnp.int32, (1, kv_heads * BLOCK), 1) % kv_heads

        def spread(which, request):
            pieces = []
            for block in range(blocks):
                piece = jnp.full((1, kv_heads * BLOCK), scale_ref[which, request, 0, block])
                for head in range(1, kv_heads):
                    piece = jnp.where(parity == head, scale_ref[which, request, head, block], piece)
                pieces.append(piece)
            return jnp.concatenate(pieces, axis=1)

        tops, totals = [], []
        for request in range(requests):
            asked = query_ref[request]
            live = same & (place < length_ref[request])
            scores = lax.dot_general(
                asked, cache_ref[0, request], (((1,), (1,)), ((), ())), preferred_element_type=jnp.float32
            )
            scores = jnp.where(live, scores * spread(0, request) * inv_root, -1e30)
            recent = lax.dot_general(
                asked, key_ref[request], (((1,), (1,)), ((), ())), preferred_element_type=jnp.float32
            )
            recent = jnp.where(new_live, recent * inv_root, -1e30)
            top = jnp.maximum(
                jnp.max(scores, axis=1, keepdims=True), jnp.max(recent, axis=1, keepdims=True)
            )
            weight = jnp.where(live, jnp.exp(scores - top), 0.0)
            new_weight = jnp.where(new_live, jnp.exp(recent - top), 0.0)
            total = jnp.sum(weight, axis=1, keepdims=True) + jnp.sum(new_weight, axis=1, keepdims=True)
            mix = jnp.dot(
                (weight * spread(1, request)).astype(jnp.bfloat16),
                cache_ref[1, request],
                preferred_element_type=jnp.float32,
            ) + jnp.dot(
                new_weight.astype(jnp.bfloat16), value_ref[request], preferred_element_type=jnp.float32
            )
            for step in range(steps):
                start = (step * requests + request) * heads
                out_ref[start : start + heads, :] = mix[step * heads : (step + 1) * heads].astype(jnp.bfloat16)
            tops.append(top)
            totals.append(total)

        def by_step(values):
            return jnp.concatenate(
                [value[step * heads : (step + 1) * heads] for step in range(steps) for value in values], axis=0
            )

        lane = lax.broadcasted_iota(jnp.int32, (total_rows, LANES), 1)
        table = jnp.zeros((total_rows, LANES), jnp.float32)
        for start, value in ((0, by_step(tops)), (3, by_step(totals))):
            for k in range(3):
                piece = value.astype(jnp.bfloat16).astype(jnp.float32)
                table = jnp.where(lane == start + k, piece, table)
                value = value - piece
        turned = jnp.transpose(table)[:8]
        out_ref[total_rows:, :] = jnp.concatenate(
            [turned[:, k * LANES : (k + 1) * LANES] for k in range(total_rows // LANES)], axis=0
        ).astype(jnp.bfloat16)

    return pl.pallas_call(
        kernel,
        out_shape=jax.ShapeDtypeStruct((total_rows + total_rows // 16, dim), jnp.bfloat16),
        in_specs=[pl.BlockSpec(memory_space=pltpu.SMEM)] * 2 + whole(4),
        out_specs=whole(1)[0],
        compiler_params=pltpu.CompilerParams(vmem_limit_bytes=6 * 1024 * 1024),
        cost_estimate=pl.CostEstimate(flops=FLOPS_AHEAD, bytes_accessed=0, transcendentals=0),
    )(
        context_len,
        kv_scale,
        query.reshape(requests, lines, dim),
        kv_cache.reshape(2, requests, width, dim),
        key_new.reshape(requests, news, dim),
        value_new.reshape(requests, news, dim),
    )


def cost(flops):
    return pl.CostEstimate(flops=flops, bytes_accessed=0, transcendentals=0)


def merge_project(parts, weight, rows, heads, dim):
    lines = rows * heads
    count = len(parts)
    depth, width = weight.shape
    tile = tile_of(width, 512)

    def kernel(*refs):
        part_refs, weight_ref, out_ref, mixed, chosen = refs[:count], refs[count], refs[-3], refs[-2], refs[-1]
        tops, totals = [], []
        for ref in part_refs:
            stats = ref[lines:, :].astype(jnp.float32)
            wide = jnp.concatenate([stats[k * 8 : (k + 1) * 8] for k in range(lines // LANES)], axis=1)
            table = jnp.transpose(jnp.concatenate([wide, jnp.zeros((LANES - 8, lines), jnp.float32)], axis=0))
            tops.append(table[:, 0:1] + table[:, 1:2] + table[:, 2:3])
            totals.append(table[:, 3:4] + table[:, 4:5] + table[:, 5:6])
        best = tops[0]
        for top in tops[1:]:
            best = jnp.maximum(best, top)
        factors = [jnp.exp(top - best) for top in tops]
        summed = paired_sum([total * factor for total, factor in zip(totals, factors)])
        mixed[...] = (
            paired_sum([ref[:lines, :].astype(jnp.float32) * factor for ref, factor in zip(part_refs, factors)])
            / summed
        )
        for head in range(heads):
            chosen[:, head * dim : (head + 1) * dim] = mixed[pl.ds(head, rows, stride=heads), :].astype(
                jnp.bfloat16
            )
        for start in range(0, width, tile):
            out_ref[:, start : start + tile] = jnp.dot(
                chosen[...], weight_ref[:, start : start + tile], preferred_element_type=jnp.float32
            ).astype(out_ref.dtype)

    return pl.pallas_call(
        kernel,
        out_shape=jax.ShapeDtypeStruct((rows, width), jnp.bfloat16),
        in_specs=whole(count + 1),
        out_specs=whole(1)[0],
        scratch_shapes=[pltpu.VMEM((lines, dim), jnp.float32), pltpu.VMEM((rows, heads * dim), jnp.bfloat16)],
        compiler_params=pltpu.CompilerParams(vmem_limit_bytes=4 * MIB),
        cost_estimate=cost(FLOPS_AHEAD),
    )(*parts, weight)


def add_residual(hidden, parts, gain):
    rows, width = hidden.shape

    def kernel(hidden_ref, gain_ref, *refs):
        part_refs, (residual_ref, gained_ref, stats_ref) = refs[:-3], refs[-3:]
        residual = hidden_ref[...].astype(jnp.float32) + paired_sum(
            [ref[...].astype(jnp.float32) for ref in part_refs]
        )
        residual_ref[...] = residual
        gained_ref[...] = (residual * gain_ref[...]).astype(jnp.bfloat16)
        left = jnp.sum(residual * residual, axis=1, keepdims=True)
        lane = lax.broadcasted_iota(jnp.int32, (rows, LANES), 1)
        table = jnp.zeros((rows, LANES), jnp.float32)
        for k in range(3):
            piece = left.astype(jnp.bfloat16).astype(jnp.float32)
            table = jnp.where(lane == k, piece, table)
            left = left - piece
        stats_ref[...] = table.astype(jnp.bfloat16)

    return pl.pallas_call(
        kernel,
        out_shape=(
            jax.ShapeDtypeStruct((rows, width), jnp.float32),
            jax.ShapeDtypeStruct((rows, width), jnp.bfloat16),
            jax.ShapeDtypeStruct((rows, LANES), jnp.bfloat16),
        ),
        in_specs=whole(2 + len(parts)),
        out_specs=tuple(whole(3)),
        compiler_params=pltpu.CompilerParams(vmem_limit_bytes=4 * MIB),
        cost_estimate=cost(rows * width * 8),
    )(hidden, gain.reshape(1, width), *parts)


def hs_position():
    return lax.axis_index("head") * lax.axis_size("sub") + lax.axis_index("sub")


def project_block(gained, weight, stats, own_width, hop):
    rows, depth = gained.shape
    count = lax.axis_size(HS)
    width = 2 * own_width
    tile = tile_of(own_width, 512)
    kind = jnp.bfloat16 if hop else jnp.float32

    def kernel(gained_ref, weight_ref, stats_ref, out_ref):
        base = ((hs_position() + hop) % count) * own_width
        for part in range(2):
            for start in range(0, own_width, tile):
                columns = pl.ds(pl.multiple_of(base + start, tile), tile)
                out_ref[:, part * own_width + start : part * own_width + start + tile] = jnp.dot(
                    gained_ref[...], weight_ref[part, :, columns], preferred_element_type=jnp.float32
                ).astype(kind)
        if hop:
            out_ref[:, width:] = stats_ref[...]

    return pl.pallas_call(
        kernel,
        out_shape=jax.ShapeDtypeStruct((rows, width + (LANES if hop else 0)), kind),
        in_specs=whole(3),
        out_specs=whole(1)[0],
        compiler_params=pltpu.CompilerParams(vmem_limit_bytes=4 * MIB),
        cost_estimate=cost(2 * rows * depth * width),
    )(gained, weight, stats)


def convolve(own, received, stats, state, taps, bias, weight, features):
    rows, width = own.shape
    own_width = width // 2
    requests = state.shape[1]
    taps_count = taps.shape[0]
    mixed_width = weight.shape[0]
    count = len(received)

    def kernel(own_ref, stats_ref, state_ref, taps_ref, bias_ref, weight_ref, *refs):
        received_refs, (conv_ref, gate_ref, mixing_ref) = refs[:count], refs[count:]
        pieces = stats_ref[...].astype(jnp.float32)
        channels = own_ref[...]
        for ref in received_refs:
            channels = channels + ref[:, :width].astype(jnp.float32)
            pieces = pieces + ref[:, width:].astype(jnp.float32)
        squares = jnp.sum(pieces, axis=1, keepdims=True)
        channels = (channels * lax.rsqrt(squares / features + EPS)).astype(jnp.bfloat16)
        gate_ref[...] = channels[:, own_width:]
        window = jnp.concatenate(
            [state_ref[k].astype(jnp.float32) for k in range(taps_count - 1)]
            + [channels[:, :own_width].astype(jnp.float32)],
            axis=0,
        )
        total = bias_ref[...]
        for tap in range(taps_count):
            total = total + taps_ref[tap : tap + 1, :].astype(jnp.float32) * window[
                tap * requests : tap * requests + rows
            ]
        conv = (total * jax.nn.sigmoid(total)).astype(jnp.bfloat16)
        conv_ref[...] = conv
        mixing_ref[...] = lax.dot_general(
            conv, weight_ref[...], (((1,), (1,)), ((), ())), preferred_element_type=jnp.float32
        )

    return pl.pallas_call(
        kernel,
        out_shape=(
            jax.ShapeDtypeStruct((rows, own_width), jnp.bfloat16),
            jax.ShapeDtypeStruct((rows, own_width), jnp.bfloat16),
            jax.ShapeDtypeStruct((rows, mixed_width), jnp.float32),
        ),
        in_specs=whole(6 + count),
        out_specs=tuple(whole(3)),
        compiler_params=pltpu.CompilerParams(vmem_limit_bytes=8 * MIB),
        cost_estimate=cost(FLOPS_AHEAD),
    )(own, stats, state, taps, bias, weight, *received)


def scan_states(mixing, conv, gate, dt_weight, dt_bias, decay, skip, state):
    rows, own_width = conv.shape
    requests, state_width = state.shape[:2]
    low_width = dt_weight.shape[0]

    def kernel(mixing_ref, conv_ref, gate_ref, dt_ref, bias_ref, decay_ref, skip_ref, state_ref, *refs):
        gated_ref, next_ref, out = refs
        low = mixing_ref[:, :low_width]
        low_rank = (low * lax.rsqrt(jnp.mean(low * low, axis=1, keepdims=True) + EPS)).astype(jnp.bfloat16)
        step_size = jnp.dot(low_rank, dt_ref[...], preferred_element_type=jnp.float32) + bias_ref[...]
        step_size = jnp.maximum(step_size, 0.0) + jnp.log1p(jnp.exp(-jnp.abs(step_size)))
        mats = mixing_ref[:, low_width : low_width + 2 * state_width]
        lane = lax.broadcasted_iota(jnp.int32, mats.shape, 1)
        power = mats * mats
        first = jnp.sum(jnp.where(lane < state_width, power, 0.0), axis=1, keepdims=True)
        second = jnp.sum(jnp.where(lane < state_width, 0.0, power), axis=1, keepdims=True)
        mats = mats * lax.rsqrt(jnp.where(lane < state_width, first, second) / state_width + EPS)
        mats = jnp.concatenate([mats, jnp.zeros((rows, LANES - 2 * state_width), jnp.float32)], axis=1)
        turned = jnp.transpose(jnp.concatenate([mats, jnp.zeros((LANES - rows, LANES), jnp.float32)], axis=0))
        signal = conv_ref[...].astype(jnp.float32)
        drive = step_size * signal
        decay = decay_ref[...]
        for request in range(requests):
            memory = state_ref[request]
            for row in range(request, rows, requests):
                memory = (
                    jnp.exp(-step_size[row : row + 1] * decay) * memory
                    + drive[row : row + 1] * turned[:state_width, row : row + 1]
                )
                out[row : row + 1, :] = jnp.sum(
                    memory * turned[state_width : 2 * state_width, row : row + 1], axis=0, keepdims=True
                )
            next_ref[request] = memory
        gate = gate_ref[...].astype(jnp.float32)
        gated_ref[...] = ((out[...] + skip_ref[...] * signal) * (gate * jax.nn.sigmoid(gate))).astype(
            jnp.bfloat16
        )

    return pl.pallas_call(
        kernel,
        out_shape=(
            jax.ShapeDtypeStruct((rows, own_width), jnp.bfloat16),
            jax.ShapeDtypeStruct(state.shape, jnp.float32),
        ),
        in_specs=whole(8),
        out_specs=tuple(whole(2)),
        scratch_shapes=[pltpu.VMEM((rows, own_width), jnp.float32)],
        compiler_params=pltpu.CompilerParams(vmem_limit_bytes=8 * MIB),
        cost_estimate=cost(FLOPS_AHEAD // 4),
    )(mixing, conv, gate, dt_weight, dt_bias, decay, skip, state)


def project_out(blocks, hops, weight, before):
    rows, own_width = blocks[0].shape
    count = lax.axis_size(HS)
    width = weight.shape[1]
    tile = tile_of(width, 512)
    kind = jnp.float32 if before is None else jnp.bfloat16

    def kernel(*refs):
        block_refs, weight_ref, out_ref = refs[: len(hops)], refs[len(hops)], refs[-1]
        for start in range(0, width, tile):
            columns = slice(start, start + tile)
            terms = []
            for ref, hop in zip(block_refs, hops):
                base = pl.multiple_of(((hs_position() + count - hop) % count) * own_width, own_width)
                terms.append(
                    jnp.dot(
                        ref[...], weight_ref[pl.ds(base, own_width), columns], preferred_element_type=jnp.float32
                    )
                )
            total = terms[0]
            for term in terms[1:]:
                total = total + term
            if before is not None:
                total = total + refs[len(hops) + 1][:, columns]
            out_ref[:, columns] = total.astype(kind)

    extra = () if before is None else (before,)
    return pl.pallas_call(
        kernel,
        out_shape=jax.ShapeDtypeStruct((rows, width), kind),
        in_specs=whole(len(blocks) + 1 + len(extra)),
        out_specs=whole(1)[0],
        compiler_params=pltpu.CompilerParams(vmem_limit_bytes=4 * MIB),
        cost_estimate=cost(2 * rows * own_width * width * len(hops)),
    )(*blocks, weight, *extra)


def finish(residual, parts, requests):
    rows, width = residual.shape
    steps = rows // requests

    def kernel(residual_ref, *refs):
        part_refs, out_ref, total = refs[:-2], refs[-2], refs[-1]
        total[...] = residual_ref[...] + paired_sum([ref[...].astype(jnp.float32) for ref in part_refs])
        for request in range(requests):
            out_ref[request] = jnp.concatenate(
                [total[step * requests + request : step * requests + request + 1, :] for step in range(steps)],
                axis=0,
            ).astype(jnp.bfloat16)

    return pl.pallas_call(
        kernel,
        out_shape=jax.ShapeDtypeStruct((requests, steps, width), jnp.bfloat16),
        in_specs=whole(1 + len(parts)),
        out_specs=whole(1)[0],
        scratch_shapes=[pltpu.VMEM((rows, width), jnp.float32)],
        compiler_params=pltpu.CompilerParams(vmem_limit_bytes=4 * MIB),
        cost_estimate=cost(rows * width * 8),
    )(residual, *parts)


def plain_attention(query, key_new, value_new, kv_cache, kv_scale, context_len):
    requests, steps, heads, dim = query.shape
    kv_heads = key_new.shape[2]
    group = heads // kv_heads
    cache_len = kv_cache.shape[2]
    width = cache_len * kv_heads
    inv_root = 1.0 / math.sqrt(dim)
    first = lax.axis_index("seq") == 0
    flat_query = query.reshape(requests, steps * heads, dim)
    flat_cache = kv_cache.reshape(2, requests, width, dim)
    column = jnp.arange(width, dtype=jnp.int32)
    row = jnp.arange(steps * heads, dtype=jnp.int32)
    row_kv = (row % heads) // group
    same = row_kv[:, None] == (column % kv_heads)[None, :]
    place = lax.axis_index("seq") * cache_len + column // kv_heads
    live = same[None] & (place[None, :] < context_len[:, None])[:, None, :]
    spread = jnp.repeat(kv_scale.transpose(0, 1, 3, 2), BLOCK, axis=2).reshape(2, requests, width)
    scores = jnp.einsum("rqd,rpd->rqp", flat_query, flat_cache[0], preferred_element_type=jnp.float32)
    scores = jnp.where(live, scores * spread[0][:, None, :] * inv_root, -1e30)
    flat_new_k = key_new.reshape(requests, steps * kv_heads, dim)
    flat_new_v = value_new.reshape(requests, steps * kv_heads, dim)
    new_column = jnp.arange(steps * kv_heads, dtype=jnp.int32)
    new_live = (
        (row_kv[:, None] == (new_column % kv_heads)[None, :])
        & ((new_column // kv_heads)[None, :] <= (row // heads)[:, None])
        & first
    )[None]
    recent = jnp.einsum("rqd,rjd->rqj", flat_query, flat_new_k, preferred_element_type=jnp.float32)
    recent = jnp.where(new_live, recent * inv_root, -1e30)
    top = jnp.maximum(jnp.max(scores, axis=-1), jnp.max(recent, axis=-1))
    weight = jnp.where(live, jnp.exp(scores - top[..., None]), 0.0)
    new_weight = jnp.where(new_live, jnp.exp(recent - top[..., None]), 0.0)
    total = jnp.sum(weight, axis=-1) + jnp.sum(new_weight, axis=-1)
    scaled = (weight * spread[1][:, None, :]).astype(jnp.bfloat16)
    mix = jnp.einsum("rqp,rpd->rqd", scaled, flat_cache[1], preferred_element_type=jnp.float32)
    mix = mix + jnp.einsum(
        "rqj,rjd->rqd", new_weight.astype(jnp.bfloat16), flat_new_v, preferred_element_type=jnp.float32
    )
    rows = requests * steps
    return mix.reshape(rows, heads, dim), top.reshape(rows, heads), total.reshape(rows, heads)


def merge(mixes, tops, totals):
    best = tops[0]
    for top in tops[1:]:
        best = jnp.maximum(best, top)
    factors = [jnp.exp(top - best) for top in tops]
    summed = paired_sum([total * factor for total, factor in zip(totals, factors)])
    mixed = paired_sum(
        [mix.astype(jnp.float32) * factor[..., None] for mix, factor in zip(mixes, factors)]
    )
    return (mixed / summed[..., None]).astype(jnp.bfloat16)


def plain(
    hidden,
    query,
    key_new,
    value_new,
    kv_cache,
    kv_scale,
    context_len,
    attn_out_weight,
    norm_gain,
    in_weight,
    conv_weight,
    conv_bias,
    conv_state,
    xproj_weight,
    dt_weight,
    dt_bias,
    decay_rate,
    skip_gain,
    ssm_state,
    mamba_out_weight,
):
    requests, steps = hidden.shape[:2]
    rows = requests * steps
    seq_count = lax.axis_size("seq")
    hs_count = lax.axis_size(HS)
    hs_index = lax.axis_index(HS)
    heads = query.shape[2]
    dim = query.shape[3]
    mix, top, total = plain_attention(query, key_new, value_new, kv_cache, kv_scale, context_len)
    mixes, tops, totals = (lax.all_gather(part, "seq") for part in (mix, top, total))
    every = range(seq_count)
    own_heads = merge([mixes[k] for k in every], [tops[k] for k in every], [totals[k] for k in every])
    every_head = lax.all_gather(own_heads.reshape(rows, heads * dim), HS, axis=1, tiled=True)
    width_in = attn_out_weight.shape[0]
    chosen = lax.dynamic_slice_in_dim(every_head, lax.axis_index("seq") * width_in, width_in, 1)
    attended = sum_over(
        jnp.dot(chosen, attn_out_weight, preferred_element_type=jnp.float32), "seq", jnp.bfloat16
    )
    residual = hidden.astype(jnp.float32).reshape(rows, -1) + attended
    features = residual.shape[1] * hs_count
    squares = jnp.sum(residual * residual, axis=-1, keepdims=True)
    gained = (residual * norm_gain).astype(jnp.bfloat16)
    projected = jnp.einsum("nd,cde->nce", gained, in_weight, preferred_element_type=jnp.float32)
    own_width = conv_weight.shape[0]
    upper, lower = split_pair(squares)

    def block_for(index):
        block = lax.dynamic_slice_in_dim(projected, index * own_width, own_width, 2)
        return block.reshape(rows, 2 * own_width)

    channels = block_for(hs_index)
    for hop in range(1, hs_count):
        block = jnp.concatenate([block_for((hs_index + hop) % hs_count), upper, lower], axis=1)
        part = shifted(block.astype(jnp.bfloat16), HS, hop).astype(jnp.float32)
        channels = channels + part[:, : 2 * own_width]
        squares = squares + part[:, 2 * own_width : 2 * own_width + 1] + part[:, 2 * own_width + 1 :]
    channels = channels * lax.rsqrt(squares / features + EPS)
    conv_in = channels[:, :own_width].astype(jnp.bfloat16)
    gate_in = channels[:, own_width:].astype(jnp.bfloat16)
    window = jnp.concatenate(
        [
            conv_state.astype(jnp.float32),
            conv_in.astype(jnp.float32).reshape(requests, steps, own_width),
        ],
        axis=1,
    )
    conv_sum = jnp.zeros((requests, steps, own_width), jnp.float32) + conv_bias
    for tap in range(conv_weight.shape[1]):
        conv_sum = conv_sum + conv_weight[:, tap].astype(jnp.float32) * window[:, tap : tap + steps, :]
    conv_out = jax.nn.silu(conv_sum).astype(jnp.bfloat16).reshape(rows, own_width)
    mixing = jnp.dot(conv_out, xproj_weight, preferred_element_type=jnp.float32)
    mixing = sum_over(sum_over(mixing, HS), "seq")
    low_width = dt_weight.shape[0]
    state_width = decay_rate.shape[1]
    low_rank = rms_unit(mixing[:, :low_width]).astype(jnp.bfloat16)
    input_mat = rms_unit(mixing[:, low_width : low_width + state_width]).reshape(
        requests, steps, state_width
    )
    output_mat = rms_unit(mixing[:, low_width + state_width :]).reshape(requests, steps, state_width)
    delta = jax.nn.softplus(
        jnp.dot(low_rank, dt_weight, preferred_element_type=jnp.float32) + dt_bias
    ).reshape(requests, steps, own_width)
    signal = conv_out.astype(jnp.float32).reshape(requests, steps, own_width)
    memory = ssm_state
    outputs = []
    for moment in range(steps):
        step_now = delta[:, moment]
        memory = (
            jnp.exp(-step_now[..., None] * decay_rate) * memory
            + (step_now * signal[:, moment])[..., None] * input_mat[:, moment][:, None, :]
        )
        outputs.append(
            jnp.sum(memory * output_mat[:, moment][:, None, :], axis=-1)
            + skip_gain * signal[:, moment]
        )
    stacked = jnp.stack(outputs, axis=1).reshape(rows, own_width)
    gated_out = (stacked * jax.nn.silu(gate_in.astype(jnp.float32))).astype(jnp.bfloat16)
    gated_block = lax.all_gather(gated_out, HS, axis=1, tiled=True)
    mamba_part = sum_over(
        jnp.dot(gated_block, mamba_out_weight, preferred_element_type=jnp.float32), "seq", jnp.bfloat16
    )
    final = (residual + mamba_part).astype(jnp.bfloat16).reshape(requests, steps, -1)
    return (final, memory)


def local(
    hidden,
    query,
    key_new,
    value_new,
    kv_cache,
    kv_scale,
    context_len,
    attn_out_weight,
    norm_gain,
    in_weight,
    conv_weight,
    conv_bias,
    conv_state,
    xproj_weight,
    dt_weight,
    dt_bias,
    decay_rate,
    skip_gain,
    ssm_state,
    mamba_out_weight,
):
    requests, steps = hidden.shape[:2]
    rows = requests * steps
    seq_count = lax.axis_size("seq")
    hs_count = lax.axis_size(HS)
    heads, dim = query.shape[2:]
    own_width = conv_weight.shape[0]
    if (
        seq_count != hs_count
        or seq_count > DIRECT
        or own_width % LANES
        or dim != LANES
        or (rows * heads) % LANES
        or rows % 16
    ):
        return plain(
            hidden,
            query,
            key_new,
            value_new,
            kv_cache,
            kv_scale,
            context_len,
            attn_out_weight,
            norm_gain,
            in_weight,
            conv_weight,
            conv_bias,
            conv_state,
            xproj_weight,
            dt_weight,
            dt_bias,
            decay_rate,
            skip_gain,
            ssm_state,
            mamba_out_weight,
        )
    part = attention(query, key_new, value_new, kv_cache, kv_scale, context_len)
    parts = [
        lax.ppermute(
            part,
            ("seq",) + HS,
            [
                (s * hs_count + j, j * hs_count + (s + hop) % hs_count)
                for s in range(seq_count)
                for j in range(hs_count)
            ],
        )
        for hop in range(hs_count)
    ]
    partial = merge_project(parts, attn_out_weight, rows, heads, dim)
    step_hidden = hidden.transpose(1, 0, 2).reshape(rows, -1)
    features = step_hidden.shape[1] * hs_count
    residual, gained, stats = add_residual(step_hidden, everyone(partial, "seq"), norm_gain)
    received = []
    for hop in range(1, hs_count):
        block = project_block(gained, in_weight, stats, own_width, hop)
        received.append(shifted(block, HS, hop))
    own = project_block(gained, in_weight, stats, own_width, 0)
    conv, gate, mixing = convolve(
        own,
        received,
        stats,
        conv_state.transpose(1, 0, 2),
        conv_weight.T,
        conv_bias.reshape(1, -1),
        xproj_weight.T,
        features,
    )
    mixing = sum_over(sum_over(mixing, HS), "seq")
    gated, state = scan_states(
        mixing,
        conv,
        gate,
        dt_weight,
        dt_bias.reshape(1, -1),
        decay_rate.T,
        skip_gain.reshape(1, -1),
        ssm_state.transpose(0, 2, 1),
    )
    hops = range(1, hs_count)
    blocks = [shifted(gated, HS, hop) for hop in hops]
    first = project_out([gated], [0], mamba_out_weight, None)
    partial = project_out(blocks, hops, mamba_out_weight, first)
    final = finish(residual, everyone(partial, "seq"), requests)
    return final, state.transpose(0, 2, 1)


def solution(mesh):
    return jax.shard_map(
        local,
        mesh=mesh,
        in_specs=(
            P("groups", None, HS),
            P("groups", None, HS, None),
            P("groups", None, HS, None),
            P("groups", None, HS, None),
            P(None, "groups", "seq", HS, None),
            P(None, "groups", HS, "seq"),
            P("groups"),
            P("seq", HS),
            P(HS),
            P(None, HS, "seq"),
            P(("seq",) + HS, None),
            P(("seq",) + HS),
            P("groups", None, ("seq",) + HS),
            P(("seq",) + HS, None),
            P(None, ("seq",) + HS),
            P(("seq",) + HS),
            P(("seq",) + HS, None),
            P(("seq",) + HS),
            P("groups", ("seq",) + HS, None),
            P("seq", HS),
        ),
        out_specs=(P("groups", None, HS), P("groups", ("seq",) + HS, None)),
        check_vma=False,
    )
```

```python
import math

import jax
import jax.numpy as jnp
from jax import lax
from jax.experimental import pallas as pl
from jax.experimental.pallas import tpu as pltpu
from jax.sharding import PartitionSpec as P

BLOCK = 128
EPS = 1e-06
HS = ("head", "sub")
DIRECT = 8
LANES = 128
MIB = 1024 * 1024
PIECES = 8
ATT_LIMIT = 8
LOAD_LIMIT = 2
FLOPS_AHEAD = 20_000_000_000


def shifted(value, axes, hop):
    count = lax.axis_size(axes)
    return lax.ppermute(value, axes, [(i, (i + hop) % count) for i in range(count)])


def paired_sum(terms):
    if len(terms) == 1:
        return terms[0]
    return paired_sum(terms[::2]) + paired_sum(terms[1::2])


def crossed(value, axes, flip):
    return lax.ppermute(value, axes, [(i, i ^ flip) for i in range(lax.axis_size(axes))])


def crossed_all(value, axes):
    count = lax.axis_size(axes)
    far_first = {flip: crossed(value, axes, flip) for flip in range(count - 1, 0, -1)}
    return [value] + [far_first[flip] for flip in range(1, count)]


def everyone(value, axes):
    return [value] + [shifted(value, axes, hop) for hop in range(1, lax.axis_size(axes))]


def sum_over(value, axes, kind=None):
    if lax.axis_size(axes) > DIRECT:
        return lax.psum(value, axes)
    if kind is not None:
        value = lax.optimization_barrier(value.astype(kind))
    return paired_sum([part.astype(jnp.float32) for part in everyone(value, axes)])


def split_pair(value):
    upper = lax.reduce_precision(value, 8, 7)
    return upper, lax.reduce_precision(value - upper, 8, 7)


def rms_unit(values):
    return values * lax.rsqrt(jnp.mean(values * values, axis=-1, keepdims=True) + EPS)


def tile_of(width, limit):
    tile = width
    while tile > limit and tile % 2 == 0 and (tile // 2) % 128 == 0:
        tile //= 2
    return tile


def whole(count):
    return [pl.BlockSpec(memory_space=pltpu.VMEM)] * count


def pieces_of(source, target, ready):
    rows = target.shape[0] // PIECES
    return [
        pltpu.make_async_copy(
            source.at[k * rows : (k + 1) * rows], target.at[k * rows : (k + 1) * rows], ready.at[k]
        )
        for k in range(PIECES)
    ]


def bring(weight, part, after):
    shape = weight.shape if part is None else weight.shape[1:]

    def kernel(weight_ref, after_ref, out_ref, ready):
        copies = pieces_of(weight_ref if part is None else weight_ref.at[part], out_ref, ready)
        for copy in copies:
            copy.start()
        for copy in copies:
            copy.wait()

    return pl.pallas_call(
        kernel,
        out_shape=pltpu.VMEM(shape, weight.dtype),
        in_specs=[pl.BlockSpec(memory_space=pl.ANY)] * 2,
        out_specs=whole(1)[0],
        scratch_shapes=[pltpu.SemaphoreType.DMA((PIECES,))],
        compiler_params=pltpu.CompilerParams(vmem_limit_bytes=LOAD_LIMIT * MIB),
        cost_estimate=pl.CostEstimate(
            flops=0, bytes_accessed=2 * math.prod(shape) * weight.dtype.itemsize, transcendentals=0
        ),
    )(pltpu.with_memory_space_constraint(weight, pltpu.HBM), after)


def attention(query, key_new, value_new, kv_cache, kv_scale, context_len, weight):
    requests, steps, heads, dim = query.shape
    kv_heads = key_new.shape[2]
    group = heads // kv_heads
    cache_len = kv_cache.shape[2]
    width = cache_len * kv_heads
    blocks = kv_scale.shape[3]
    inv_root = 1.0 / math.sqrt(dim)
    lines = steps * heads
    total_rows = requests * lines
    news = steps * kv_heads

    def kernel(*refs):
        sources, weight_source, out_ref, weight_ref = refs[:6], refs[6], refs[7], refs[8]
        held, ready, weight_ready = refs[9:15], refs[15], refs[16]
        length_ref, scale_ref, query_ref, key_ref, value_ref, cache_ref = held
        copies = [
            pltpu.make_async_copy(sources[k], held[k], ready.at[k]) for k in range(5)
        ] + [
            pltpu.make_async_copy(sources[5].at[:, k], cache_ref.at[:, k], ready.at[5 + k])
            for k in range(requests)
        ]
        for copy in copies:
            copy.start()
        weight_copies = pieces_of(weight_source, weight_ref, weight_ready)
        for copy in weight_copies:
            copy.start()
        shard = lax.axis_index("seq")
        row = lax.broadcasted_iota(jnp.int32, (lines, width), 0)
        column = lax.broadcasted_iota(jnp.int32, (lines, width), 1)
        same = (row % heads) // group == column % kv_heads
        place = shard * cache_len + column // kv_heads
        new_row = lax.broadcasted_iota(jnp.int32, (lines, news), 0)
        new_column = lax.broadcasted_iota(jnp.int32, (lines, news), 1)
        new_live = (
            ((new_row % heads) // group == new_column % kv_heads)
            & (new_column // kv_heads <= new_row // heads)
            & (shard == 0)
        )
        parity = lax.broadcasted_iota(jnp.int32, (1, kv_heads * BLOCK), 1) % kv_heads

        def spread(which, request):
            pieces = []
            for block in range(blocks):
                piece = jnp.zeros((1, kv_heads * BLOCK), jnp.float32)
                for head in range(kv_heads):
                    piece = jnp.where(
                        parity == head, scale_ref[which, head, block : block + 1, request : request + 1], piece
                    )
                pieces.append(piece)
            return jnp.concatenate(pieces, axis=1)

        tops, totals = [], []
        for copy in copies[:5]:
            copy.wait()
        for request in range(requests):
            asked = query_ref[request]
            live = same & (place < length_ref[:, request : request + 1])
            copies[5 + request].wait()
            scores = lax.dot_general(
                asked, cache_ref[0, request], (((1,), (1,)), ((), ())), preferred_element_type=jnp.float32
            )
            scores = jnp.where(live, scores * spread(0, request) * inv_root, -1e30)
            recent = lax.dot_general(
                asked, key_ref[request], (((1,), (1,)), ((), ())), preferred_element_type=jnp.float32
            )
            recent = jnp.where(new_live, recent * inv_root, -1e30)
            top = jnp.maximum(
                jnp.max(scores, axis=1, keepdims=True), jnp.max(recent, axis=1, keepdims=True)
            )
            weight = jnp.where(live, jnp.exp(scores - top), 0.0)
            new_weight = jnp.where(new_live, jnp.exp(recent - top), 0.0)
            total = jnp.sum(weight, axis=1, keepdims=True) + jnp.sum(new_weight, axis=1, keepdims=True)
            mix = jnp.dot(
                (weight * spread(1, request)).astype(jnp.bfloat16),
                cache_ref[1, request],
                preferred_element_type=jnp.float32,
            ) + jnp.dot(
                new_weight.astype(jnp.bfloat16), value_ref[request], preferred_element_type=jnp.float32
            )
            for step in range(steps):
                start = (step * requests + request) * heads
                out_ref[start : start + heads, :] = mix[step * heads : (step + 1) * heads].astype(jnp.bfloat16)
            tops.append(top)
            totals.append(total)

        def by_step(values):
            return jnp.concatenate(
                [value[step * heads : (step + 1) * heads] for step in range(steps) for value in values], axis=0
            )

        lane = lax.broadcasted_iota(jnp.int32, (total_rows, LANES), 1)
        table = jnp.zeros((total_rows, LANES), jnp.float32)
        for start, value in ((0, by_step(tops)), (3, by_step(totals))):
            for k in range(3):
                piece = value.astype(jnp.bfloat16).astype(jnp.float32)
                table = jnp.where(lane == start + k, piece, table)
                value = value - piece
        turned = jnp.transpose(table)[:8]
        out_ref[total_rows:, :] = jnp.concatenate(
            [turned[:, k * LANES : (k + 1) * LANES] for k in range(total_rows // LANES)], axis=0
        ).astype(jnp.bfloat16)
        for copy in weight_copies:
            copy.wait()

    given_all = (
        context_len.reshape(1, requests),
        kv_scale.transpose(0, 2, 3, 1),
        query.reshape(requests, lines, dim),
        key_new.reshape(requests, news, dim),
        value_new.reshape(requests, news, dim),
        kv_cache.reshape(2, requests, width, dim),
    )
    return pl.pallas_call(
        kernel,
        out_shape=(
            jax.ShapeDtypeStruct((total_rows + total_rows // 16, dim), jnp.bfloat16),
            pltpu.VMEM(weight.shape, weight.dtype),
        ),
        in_specs=[pl.BlockSpec(memory_space=pl.ANY)] * 7,
        out_specs=tuple(whole(2)),
        scratch_shapes=[pltpu.VMEM(given.shape, given.dtype) for given in given_all]
        + [pltpu.SemaphoreType.DMA((5 + requests,)), pltpu.SemaphoreType.DMA((PIECES,))],
        compiler_params=pltpu.CompilerParams(vmem_limit_bytes=ATT_LIMIT * MIB),
        cost_estimate=cost(1_000_000_000),
    )(*[pltpu.with_memory_space_constraint(given, pltpu.HBM) for given in given_all + (weight,)])


def cost(flops):
    return pl.CostEstimate(flops=flops, bytes_accessed=0, transcendentals=0)


def merge_project(parts, weight, rows, heads, dim, brought):
    lines = rows * heads
    count = len(parts)
    depth, width = weight.shape
    tile = tile_of(width, 512)

    def kernel(*refs):
        part_refs, weight_ref, out_ref, mixed, chosen = refs[:count], refs[count], refs[-3], refs[-2], refs[-1]
        tops, totals = [], []
        for ref in part_refs:
            stats = ref[lines:, :].astype(jnp.float32)
            wide = jnp.concatenate([stats[k * 8 : (k + 1) * 8] for k in range(lines // LANES)], axis=1)
            table = jnp.transpose(jnp.concatenate([wide, jnp.zeros((LANES - 8, lines), jnp.float32)], axis=0))
            tops.append(table[:, 0:1] + table[:, 1:2] + table[:, 2:3])
            totals.append(table[:, 3:4] + table[:, 4:5] + table[:, 5:6])
        best = tops[0]
        for top in tops[1:]:
            best = jnp.maximum(best, top)
        factors = [jnp.exp(top - best) for top in tops]
        summed = paired_sum([total * factor for total, factor in zip(totals, factors)])
        mixed[...] = (
            paired_sum([ref[:lines, :].astype(jnp.float32) * factor for ref, factor in zip(part_refs, factors)])
            / summed
        )
        for head in range(heads):
            chosen[:, head * dim : (head + 1) * dim] = mixed[pl.ds(head, rows, stride=heads), :].astype(
                jnp.bfloat16
            )
        for start in range(0, width, tile):
            out_ref[:, start : start + tile] = jnp.dot(
                chosen[...], weight_ref[:, start : start + tile], preferred_element_type=jnp.float32
            ).astype(out_ref.dtype)

    return pl.pallas_call(
        kernel,
        out_shape=jax.ShapeDtypeStruct((rows, width), jnp.bfloat16),
        in_specs=whole(count + 1) + [pl.BlockSpec(memory_space=pl.ANY)],
        out_specs=whole(1)[0],
        scratch_shapes=[pltpu.VMEM((lines, dim), jnp.float32), pltpu.VMEM((rows, heads * dim), jnp.bfloat16)],
        compiler_params=pltpu.CompilerParams(vmem_limit_bytes=4 * MIB),
        cost_estimate=cost(FLOPS_AHEAD),
    )(*parts, weight, brought)


def in_three(left):
    rows = left.shape[0]
    lane = lax.broadcasted_iota(jnp.int32, (rows, LANES), 1)
    table = jnp.zeros((rows, LANES), jnp.float32)
    for k in range(3):
        piece = left.astype(jnp.bfloat16).astype(jnp.float32)
        table = jnp.where(lane == k, piece, table)
        left = left - piece
    return table.astype(jnp.bfloat16)


def add_residual(hidden, parts, gain):
    requests, steps, width = hidden.shape
    rows = requests * steps

    def kernel(hidden_ref, gain_ref, *refs):
        part_refs, (residual_ref, gained_ref, stats_ref) = refs[:-3], refs[-3:]
        wide = [hidden_ref[request].astype(jnp.float32) for request in range(requests)]
        by_step = jnp.concatenate([part[step : step + 1] for step in range(steps) for part in wide], axis=0)
        residual = by_step + paired_sum(
            [ref[...].astype(jnp.float32) for ref in part_refs]
        )
        residual_ref[...] = residual
        gained_ref[...] = (residual * gain_ref[...]).astype(jnp.bfloat16)
        stats_ref[...] = in_three(jnp.sum(residual * residual, axis=1, keepdims=True))

    return pl.pallas_call(
        kernel,
        out_shape=(
            jax.ShapeDtypeStruct((rows, width), jnp.float32),
            jax.ShapeDtypeStruct((rows, width), jnp.bfloat16),
            jax.ShapeDtypeStruct((rows, LANES), jnp.bfloat16),
        ),
        in_specs=whole(2 + len(parts)),
        out_specs=tuple(whole(3)),
        compiler_params=pltpu.CompilerParams(vmem_limit_bytes=4 * MIB),
        cost_estimate=cost(rows * width * 8),
    )(hidden, gain.reshape(1, width), *parts)


def hs_position():
    return lax.axis_index("head") * lax.axis_size("sub") + lax.axis_index("sub")


def project_block(gained, weights, stats, own_width, flip, arrived=None):
    rows, depth = gained.shape
    width = 2 * own_width
    tile = tile_of(own_width, 512)
    kind = jnp.bfloat16 if flip else jnp.float32
    extra = () if arrived is None else (arrived,)

    def kernel(gained_ref, stats_ref, *refs):
        weight_refs, refs, out_ref = refs[:2], refs[2:], refs[-1]
        base = (hs_position() ^ flip) * own_width
        for part in range(2):
            for start in range(0, own_width, tile):
                columns = pl.ds(pl.multiple_of(base + start, tile), tile)
                place = slice(part * own_width + start, part * own_width + start + tile)
                block = jnp.dot(
                    gained_ref[...], weight_refs[part][:, columns], preferred_element_type=jnp.float32
                )
                if extra:
                    block = block + refs[0][:, place].astype(jnp.float32)
                out_ref[:, place] = block.astype(kind)
        if flip and extra:
            both = stats_ref[...].astype(jnp.float32) + refs[0][:, width:].astype(jnp.float32)
            out_ref[:, width:] = in_three(jnp.sum(both, axis=1, keepdims=True))
        elif flip:
            out_ref[:, width:] = stats_ref[...]

    return pl.pallas_call(
        kernel,
        out_shape=jax.ShapeDtypeStruct((rows, width + (LANES if flip else 0)), kind),
        in_specs=whole(4 + len(extra)),
        out_specs=whole(1)[0],
        compiler_params=pltpu.CompilerParams(vmem_limit_bytes=4 * MIB),
        cost_estimate=cost(2 * rows * depth * width),
    )(gained, stats, *weights, *extra)


def convolve(own, received, squares, state, taps, bias, weight, features):
    rows, width = own.shape
    own_width = width // 2
    requests = state.shape[1]
    taps_count = taps.shape[0]
    mixed_width = weight.shape[0]
    count = len(squares)

    def kernel(own_ref, received_ref, state_ref, taps_ref, bias_ref, weight_ref, *refs):
        squares_refs, (conv_ref, gate_ref, mixing_ref) = refs[:count], refs[count:]
        pieces = received_ref[:, width:].astype(jnp.float32)
        for ref in squares_refs:
            pieces = pieces + ref[:, ref.shape[1] - LANES :].astype(jnp.float32)
        channels = own_ref[...] + received_ref[:, :width].astype(jnp.float32)
        squares = jnp.sum(pieces, axis=1, keepdims=True)
        channels = (channels * lax.rsqrt(squares / features + EPS)).astype(jnp.bfloat16)
        gate_ref[...] = channels[:, own_width:]
        window = jnp.concatenate(
            [state_ref[k].astype(jnp.float32) for k in range(taps_count - 1)]
            + [channels[:, :own_width].astype(jnp.float32)],
            axis=0,
        )
        total = bias_ref[...]
        for tap in range(taps_count):
            total = total + taps_ref[tap : tap + 1, :].astype(jnp.float32) * window[
                tap * requests : tap * requests + rows
            ]
        conv = (total * jax.nn.sigmoid(total)).astype(jnp.bfloat16)
        conv_ref[...] = conv
        mixing_ref[...] = lax.dot_general(
            conv, weight_ref[...], (((1,), (1,)), ((), ())), preferred_element_type=jnp.float32
        )

    return pl.pallas_call(
        kernel,
        out_shape=(
            jax.ShapeDtypeStruct((rows, own_width), jnp.bfloat16),
            jax.ShapeDtypeStruct((rows, own_width), jnp.bfloat16),
            jax.ShapeDtypeStruct((rows, mixed_width), jnp.float32),
        ),
        in_specs=whole(6 + count),
        out_specs=tuple(whole(3)),
        compiler_params=pltpu.CompilerParams(vmem_limit_bytes=8 * MIB),
        cost_estimate=cost(FLOPS_AHEAD),
    )(own, received, state, taps, bias, weight, *squares)


def scan_states(mixing, conv, gate, dt_weight, dt_bias, decay, skip, state, brought):
    rows, own_width = conv.shape
    requests, state_width = state.shape[:2]
    low_width = dt_weight.shape[0]

    def kernel(mixing_ref, conv_ref, gate_ref, dt_ref, bias_ref, decay_ref, skip_ref, state_ref, brought_ref, *refs):
        gated_ref, next_ref, out = refs
        low = mixing_ref[:, :low_width]
        low_rank = (low * lax.rsqrt(jnp.mean(low * low, axis=1, keepdims=True) + EPS)).astype(jnp.bfloat16)
        step_size = jnp.dot(low_rank, dt_ref[...], preferred_element_type=jnp.float32) + bias_ref[...]
        step_size = jnp.maximum(step_size, 0.0) + jnp.log1p(jnp.exp(-jnp.abs(step_size)))
        mats = mixing_ref[:, low_width : low_width + 2 * state_width]
        lane = lax.broadcasted_iota(jnp.int32, mats.shape, 1)
        power = mats * mats
        first = jnp.sum(jnp.where(lane < state_width, power, 0.0), axis=1, keepdims=True)
        second = jnp.sum(jnp.where(lane < state_width, 0.0, power), axis=1, keepdims=True)
        mats = mats * lax.rsqrt(jnp.where(lane < state_width, first, second) / state_width + EPS)
        mats = jnp.concatenate([mats, jnp.zeros((rows, LANES - 2 * state_width), jnp.float32)], axis=1)
        turned = jnp.transpose(jnp.concatenate([mats, jnp.zeros((LANES - rows, LANES), jnp.float32)], axis=0))
        signal = conv_ref[...].astype(jnp.float32)
        drive = step_size * signal
        decay = decay_ref[...]
        for request in range(requests):
            memory = state_ref[request]
            for row in range(request, rows, requests):
                memory = (
                    jnp.exp(-step_size[row : row + 1] * decay) * memory
                    + drive[row : row + 1] * turned[:state_width, row : row + 1]
                )
                out[row : row + 1, :] = jnp.sum(
                    memory * turned[state_width : 2 * state_width, row : row + 1], axis=0, keepdims=True
                )
            next_ref[request] = memory
        gate = gate_ref[...].astype(jnp.float32)
        gated_ref[...] = ((out[...] + skip_ref[...] * signal) * (gate * jax.nn.sigmoid(gate))).astype(
            jnp.bfloat16
        )

    return pl.pallas_call(
        kernel,
        out_shape=(
            jax.ShapeDtypeStruct((rows, own_width), jnp.bfloat16),
            jax.ShapeDtypeStruct(state.shape, jnp.float32),
        ),
        in_specs=whole(8) + [pl.BlockSpec(memory_space=pl.ANY)],
        out_specs=tuple(whole(2)),
        scratch_shapes=[pltpu.VMEM((rows, own_width), jnp.float32)],
        compiler_params=pltpu.CompilerParams(vmem_limit_bytes=8 * MIB),
        cost_estimate=cost(FLOPS_AHEAD // 4),
    )(mixing, conv, gate, dt_weight, dt_bias, decay, skip, state, brought)


def project_out(blocks, flips, weight, before):
    rows, own_width = blocks[0].shape
    width = weight.shape[1]
    tile = tile_of(width, 512)
    kind = jnp.float32 if before is None else jnp.bfloat16

    def kernel(*refs):
        block_refs, weight_ref, out_ref = refs[: len(flips)], refs[len(flips)], refs[-1]
        for start in range(0, width, tile):
            columns = slice(start, start + tile)
            terms = []
            for ref, flip in zip(block_refs, flips):
                base = pl.multiple_of((hs_position() ^ flip) * own_width, own_width)
                terms.append(
                    jnp.dot(
                        ref[...], weight_ref[pl.ds(base, own_width), columns], preferred_element_type=jnp.float32
                    )
                )
            total = terms[0]
            for term in terms[1:]:
                total = total + term
            if before is not None:
                total = total + refs[len(flips) + 1][:, columns]
            out_ref[:, columns] = total.astype(kind)

    extra = () if before is None else (before,)
    return pl.pallas_call(
        kernel,
        out_shape=jax.ShapeDtypeStruct((rows, width), kind),
        in_specs=whole(len(blocks) + 1 + len(extra)),
        out_specs=whole(1)[0],
        compiler_params=pltpu.CompilerParams(vmem_limit_bytes=4 * MIB),
        cost_estimate=cost(2 * rows * own_width * width * len(flips)),
    )(*blocks, weight, *extra)


def finish(residual, parts, requests):
    rows, width = residual.shape
    steps = rows // requests

    def kernel(residual_ref, *refs):
        part_refs, out_ref, total = refs[:-2], refs[-2], refs[-1]
        total[...] = residual_ref[...] + paired_sum([ref[...].astype(jnp.float32) for ref in part_refs])
        for request in range(requests):
            out_ref[request] = jnp.concatenate(
                [total[step * requests + request : step * requests + request + 1, :] for step in range(steps)],
                axis=0,
            ).astype(jnp.bfloat16)

    return pl.pallas_call(
        kernel,
        out_shape=jax.ShapeDtypeStruct((requests, steps, width), jnp.bfloat16),
        in_specs=whole(1 + len(parts)),
        out_specs=whole(1)[0],
        scratch_shapes=[pltpu.VMEM((rows, width), jnp.float32)],
        compiler_params=pltpu.CompilerParams(vmem_limit_bytes=4 * MIB),
        cost_estimate=cost(rows * width * 8),
    )(residual, *parts)


def plain_attention(query, key_new, value_new, kv_cache, kv_scale, context_len):
    requests, steps, heads, dim = query.shape
    kv_heads = key_new.shape[2]
    group = heads // kv_heads
    cache_len = kv_cache.shape[2]
    width = cache_len * kv_heads
    inv_root = 1.0 / math.sqrt(dim)
    first = lax.axis_index("seq") == 0
    flat_query = query.reshape(requests, steps * heads, dim)
    flat_cache = kv_cache.reshape(2, requests, width, dim)
    column = jnp.arange(width, dtype=jnp.int32)
    row = jnp.arange(steps * heads, dtype=jnp.int32)
    row_kv = (row % heads) // group
    same = row_kv[:, None] == (column % kv_heads)[None, :]
    place = lax.axis_index("seq") * cache_len + column // kv_heads
    live = same[None] & (place[None, :] < context_len[:, None])[:, None, :]
    spread = jnp.repeat(kv_scale.transpose(0, 1, 3, 2), BLOCK, axis=2).reshape(2, requests, width)
    scores = jnp.einsum("rqd,rpd->rqp", flat_query, flat_cache[0], preferred_element_type=jnp.float32)
    scores = jnp.where(live, scores * spread[0][:, None, :] * inv_root, -1e30)
    flat_new_k = key_new.reshape(requests, steps * kv_heads, dim)
    flat_new_v = value_new.reshape(requests, steps * kv_heads, dim)
    new_column = jnp.arange(steps * kv_heads, dtype=jnp.int32)
    new_live = (
        (row_kv[:, None] == (new_column % kv_heads)[None, :])
        & ((new_column // kv_heads)[None, :] <= (row // heads)[:, None])
        & first
    )[None]
    recent = jnp.einsum("rqd,rjd->rqj", flat_query, flat_new_k, preferred_element_type=jnp.float32)
    recent = jnp.where(new_live, recent * inv_root, -1e30)
    top = jnp.maximum(jnp.max(scores, axis=-1), jnp.max(recent, axis=-1))
    weight = jnp.where(live, jnp.exp(scores - top[..., None]), 0.0)
    new_weight = jnp.where(new_live, jnp.exp(recent - top[..., None]), 0.0)
    total = jnp.sum(weight, axis=-1) + jnp.sum(new_weight, axis=-1)
    scaled = (weight * spread[1][:, None, :]).astype(jnp.bfloat16)
    mix = jnp.einsum("rqp,rpd->rqd", scaled, flat_cache[1], preferred_element_type=jnp.float32)
    mix = mix + jnp.einsum(
        "rqj,rjd->rqd", new_weight.astype(jnp.bfloat16), flat_new_v, preferred_element_type=jnp.float32
    )
    rows = requests * steps
    return mix.reshape(rows, heads, dim), top.reshape(rows, heads), total.reshape(rows, heads)


def merge(mixes, tops, totals):
    best = tops[0]
    for top in tops[1:]:
        best = jnp.maximum(best, top)
    factors = [jnp.exp(top - best) for top in tops]
    summed = paired_sum([total * factor for total, factor in zip(totals, factors)])
    mixed = paired_sum(
        [mix.astype(jnp.float32) * factor[..., None] for mix, factor in zip(mixes, factors)]
    )
    return (mixed / summed[..., None]).astype(jnp.bfloat16)


def plain(
    hidden,
    query,
    key_new,
    value_new,
    kv_cache,
    kv_scale,
    context_len,
    attn_out_weight,
    norm_gain,
    in_weight,
    conv_weight,
    conv_bias,
    conv_state,
    xproj_weight,
    dt_weight,
    dt_bias,
    decay_rate,
    skip_gain,
    ssm_state,
    mamba_out_weight,
):
    requests, steps = hidden.shape[:2]
    rows = requests * steps
    seq_count = lax.axis_size("seq")
    hs_count = lax.axis_size(HS)
    hs_index = lax.axis_index(HS)
    heads = query.shape[2]
    dim = query.shape[3]
    mix, top, total = plain_attention(query, key_new, value_new, kv_cache, kv_scale, context_len)
    mixes, tops, totals = (lax.all_gather(part, "seq") for part in (mix, top, total))
    every = range(seq_count)
    own_heads = merge([mixes[k] for k in every], [tops[k] for k in every], [totals[k] for k in every])
    every_head = lax.all_gather(own_heads.reshape(rows, heads * dim), HS, axis=1, tiled=True)
    width_in = attn_out_weight.shape[0]
    chosen = lax.dynamic_slice_in_dim(every_head, lax.axis_index("seq") * width_in, width_in, 1)
    attended = sum_over(
        jnp.dot(chosen, attn_out_weight, preferred_element_type=jnp.float32), "seq", jnp.bfloat16
    )
    residual = hidden.astype(jnp.float32).reshape(rows, -1) + attended
    features = residual.shape[1] * hs_count
    squares = jnp.sum(residual * residual, axis=-1, keepdims=True)
    gained = (residual * norm_gain).astype(jnp.bfloat16)
    projected = jnp.einsum("nd,cde->nce", gained, in_weight, preferred_element_type=jnp.float32)
    own_width = conv_weight.shape[0]
    upper, lower = split_pair(squares)

    def block_for(index):
        block = lax.dynamic_slice_in_dim(projected, index * own_width, own_width, 2)
        return block.reshape(rows, 2 * own_width)

    channels = block_for(hs_index)
    for hop in range(1, hs_count):
        block = jnp.concatenate([block_for((hs_index + hop) % hs_count), upper, lower], axis=1)
        part = shifted(block.astype(jnp.bfloat16), HS, hop).astype(jnp.float32)
        channels = channels + part[:, : 2 * own_width]
        squares = squares + part[:, 2 * own_width : 2 * own_width + 1] + part[:, 2 * own_width + 1 :]
    channels = channels * lax.rsqrt(squares / features + EPS)
    conv_in = channels[:, :own_width].astype(jnp.bfloat16)
    gate_in = channels[:, own_width:].astype(jnp.bfloat16)
    window = jnp.concatenate(
        [
            conv_state.astype(jnp.float32),
            conv_in.astype(jnp.float32).reshape(requests, steps, own_width),
        ],
        axis=1,
    )
    conv_sum = jnp.zeros((requests, steps, own_width), jnp.float32) + conv_bias
    for tap in range(conv_weight.shape[1]):
        conv_sum = conv_sum + conv_weight[:, tap].astype(jnp.float32) * window[:, tap : tap + steps, :]
    conv_out = jax.nn.silu(conv_sum).astype(jnp.bfloat16).reshape(rows, own_width)
    mixing = jnp.dot(conv_out, xproj_weight, preferred_element_type=jnp.float32)
    mixing = sum_over(sum_over(mixing, HS), "seq")
    low_width = dt_weight.shape[0]
    state_width = decay_rate.shape[1]
    low_rank = rms_unit(mixing[:, :low_width]).astype(jnp.bfloat16)
    input_mat = rms_unit(mixing[:, low_width : low_width + state_width]).reshape(
        requests, steps, state_width
    )
    output_mat = rms_unit(mixing[:, low_width + state_width :]).reshape(requests, steps, state_width)
    delta = jax.nn.softplus(
        jnp.dot(low_rank, dt_weight, preferred_element_type=jnp.float32) + dt_bias
    ).reshape(requests, steps, own_width)
    signal = conv_out.astype(jnp.float32).reshape(requests, steps, own_width)
    memory = ssm_state
    outputs = []
    for moment in range(steps):
        step_now = delta[:, moment]
        memory = (
            jnp.exp(-step_now[..., None] * decay_rate) * memory
            + (step_now * signal[:, moment])[..., None] * input_mat[:, moment][:, None, :]
        )
        outputs.append(
            jnp.sum(memory * output_mat[:, moment][:, None, :], axis=-1)
            + skip_gain * signal[:, moment]
        )
    stacked = jnp.stack(outputs, axis=1).reshape(rows, own_width)
    gated_out = (stacked * jax.nn.silu(gate_in.astype(jnp.float32))).astype(jnp.bfloat16)
    gated_block = lax.all_gather(gated_out, HS, axis=1, tiled=True)
    mamba_part = sum_over(
        jnp.dot(gated_block, mamba_out_weight, preferred_element_type=jnp.float32), "seq", jnp.bfloat16
    )
    final = (residual + mamba_part).astype(jnp.bfloat16).reshape(requests, steps, -1)
    return (final, memory)


def local(
    hidden,
    query,
    key_new,
    value_new,
    kv_cache,
    kv_scale,
    context_len,
    attn_out_weight,
    norm_gain,
    in_weight,
    conv_weight,
    conv_bias,
    conv_state,
    xproj_weight,
    dt_weight,
    dt_bias,
    decay_rate,
    skip_gain,
    ssm_state,
    mamba_out_weight,
):
    requests, steps = hidden.shape[:2]
    rows = requests * steps
    seq_count = lax.axis_size("seq")
    hs_count = lax.axis_size(HS)
    heads, dim = query.shape[2:]
    own_width = conv_weight.shape[0]
    if (
        lax.axis_size("head") != 2
        or lax.axis_size("sub") != 2
        or seq_count != hs_count
        or own_width % LANES
        or dim != LANES
        or (rows * heads) % LANES
        or rows % 16
    ):
        return plain(
            hidden,
            query,
            key_new,
            value_new,
            kv_cache,
            kv_scale,
            context_len,
            attn_out_weight,
            norm_gain,
            in_weight,
            conv_weight,
            conv_bias,
            conv_state,
            xproj_weight,
            dt_weight,
            dt_bias,
            decay_rate,
            skip_gain,
            ssm_state,
            mamba_out_weight,
        )
    part, out_rows = attention(
        query, key_new, value_new, kv_cache, kv_scale, context_len, attn_out_weight
    )
    first_in = bring(in_weight, 0, part)
    place = range(hs_count)
    parts = [
        lax.ppermute(
            part,
            ("seq",) + HS,
            [
                (s * hs_count + j, j * hs_count + ((s // 2 + turn) % 2) * 2 + s % 2)
                for s in range(seq_count)
                for j in place
            ],
        )
        for turn in range(2)
    ]
    parts, first_in = lax.optimization_barrier((parts, first_in))
    parts = parts + [crossed(arrived, "sub", 1) for arrived in parts]
    partial = merge_project(parts, out_rows, rows, heads, dim, first_in)
    second_in = bring(in_weight, 1, partial)
    residual, gained, stats = add_residual(hidden, crossed_all(partial, "seq"), norm_gain)
    features = residual.shape[1] * hs_count
    give = lambda flip, arrived=None: project_block(gained, (first_in, second_in), stats, own_width, flip, arrived)
    for_far = crossed(give(3), "sub", 1)
    for_near = crossed(give(1), "sub", 1)
    received = crossed(give(2, for_far), "head", 1)
    own = give(0, for_near)
    conv, gate, mixing = convolve(
        own,
        received,
        [stats, for_far],
        conv_state.transpose(1, 0, 2),
        conv_weight.T,
        conv_bias.reshape(1, -1),
        xproj_weight.T,
        features,
    )
    mixing = mixing + crossed(mixing, "sub", 1)
    mamba_rows = bring(mamba_out_weight, None, mixing)
    base = lambda s, x, c: s * hs_count + x * 2 + c
    arrived = [
        lax.ppermute(
            mixing,
            ("seq",) + HS,
            [(base(s, x, 1), base(s ^ flip, x ^ 1, 1)) for s in range(seq_count) for x in range(2)]
            + [(base(s, x, 0), base(s ^ flip, x, 0)) for s in range(seq_count) for x in range(2) if flip],
        )
        for flip in range(seq_count - 1, -1, -1)
    ]
    arrived, mamba_rows = lax.optimization_barrier((arrived, mamba_rows))
    line = jnp.where(lax.axis_index("sub") == 0, mixing, 0.0) + paired_sum(arrived)
    mixing = line + crossed(line, "sub", 1)
    gated, state = scan_states(
        mixing,
        conv,
        gate,
        dt_weight,
        dt_bias.reshape(1, -1),
        decay_rate.T,
        skip_gain.reshape(1, -1),
        ssm_state.transpose(0, 2, 1),
        mamba_rows,
    )
    blocks = crossed_all(gated, HS)
    first = project_out(blocks[:1], [0], mamba_rows, None)
    partial = project_out(blocks[1:], list(place)[1:], mamba_rows, first)
    final = finish(residual, crossed_all(partial, "seq"), requests)
    return final, state.transpose(0, 2, 1)


def solution(mesh):
    return jax.shard_map(
        local,
        mesh=mesh,
        in_specs=(
            P("groups", None, HS),
            P("groups", None, HS, None),
            P("groups", None, HS, None),
            P("groups", None, HS, None),
            P(None, "groups", "seq", HS, None),
            P(None, "groups", HS, "seq"),
            P("groups"),
            P("seq", HS),
            P(HS),
            P(None, HS, "seq"),
            P(("seq",) + HS, None),
            P(("seq",) + HS),
            P("groups", None, ("seq",) + HS),
            P(("seq",) + HS, None),
            P(None, ("seq",) + HS),
            P(("seq",) + HS),
            P(("seq",) + HS, None),
            P(("seq",) + HS),
            P("groups", ("seq",) + HS, None),
            P("seq", HS),
        ),
        out_specs=(P("groups", None, HS), P("groups", ("seq",) + HS, None)),
        check_vma=False,
    )
```

```python
import math

import jax
import jax.numpy as jnp
from jax import lax
from jax.experimental import pallas as pl
from jax.experimental.pallas import tpu as pltpu
from jax.sharding import PartitionSpec as P

BLOCK = 128
EPS = 1e-06
HS = ("head", "sub")
DIRECT = 8
LANES = 128
MIB = 1024 * 1024
PIECES = 4
FLOPS_AHEAD = 20_000_000_000


def shifted(value, axes, hop):
    count = lax.axis_size(axes)
    return lax.ppermute(value, axes, [(i, (i + hop) % count) for i in range(count)])


def paired_sum(terms):
    if len(terms) == 1:
        return terms[0]
    return paired_sum(terms[::2]) + paired_sum(terms[1::2])


def crossed(value, axes, flip):
    return lax.ppermute(value, axes, [(i, i ^ flip) for i in range(lax.axis_size(axes))])


def crossed_all(value, axes):
    count = lax.axis_size(axes)
    far_first = {flip: crossed(value, axes, flip) for flip in range(count - 1, 0, -1)}
    return [value] + [far_first[flip] for flip in range(1, count)]


def everyone(value, axes):
    return [value] + [shifted(value, axes, hop) for hop in range(1, lax.axis_size(axes))]


def sum_over(value, axes, kind=None):
    if lax.axis_size(axes) > DIRECT:
        return lax.psum(value, axes)
    if kind is not None:
        value = lax.optimization_barrier(value.astype(kind))
    return paired_sum([part.astype(jnp.float32) for part in everyone(value, axes)])


def split_pair(value):
    upper = lax.reduce_precision(value, 8, 7)
    return upper, lax.reduce_precision(value - upper, 8, 7)


def rms_unit(values):
    return values * lax.rsqrt(jnp.mean(values * values, axis=-1, keepdims=True) + EPS)


def tile_of(width, limit):
    tile = width
    while tile > limit and tile % 2 == 0 and (tile // 2) % 128 == 0:
        tile //= 2
    return tile


def whole(count):
    return [pl.BlockSpec(memory_space=pltpu.VMEM)] * count


def in_pieces(source, target):
    rows = target.shape[0] // PIECES
    return [(source.at[k * rows : (k + 1) * rows], target.at[k * rows : (k + 1) * rows]) for k in range(PIECES)]


def hs_position():
    return lax.axis_index("head") * lax.axis_size("sub") + lax.axis_index("sub")


def whole_job(weight):
    return weight, weight.shape, in_pieces, PIECES


def block_job(weight, own_width, flip):
    def views(source, target):
        columns = pl.ds(pl.multiple_of((hs_position() ^ flip) * own_width, own_width), own_width)
        return [
            pair for part in range(2) for pair in in_pieces(source.at[part, :, columns], target.at[part])
        ]

    return weight, (2, weight.shape[1], own_width), views, 2 * PIECES


def rows_job(weight, own_width, flips):
    def views(source, target):
        pairs = []
        for place, flip in enumerate(flips):
            base = pl.multiple_of((hs_position() ^ flip) * own_width, own_width)
            pairs += in_pieces(source.at[pl.ds(base, own_width)], target.at[place])
        return pairs

    return weight, (len(flips), own_width, weight.shape[1]), views, len(flips) * PIECES


def job_shapes(jobs):
    return [pltpu.VMEM(job[1], job[0].dtype) for job in jobs]


def job_inputs(jobs):
    return [pltpu.with_memory_space_constraint(job[0], pltpu.HBM) for job in jobs]


def job_bytes(jobs):
    return sum(2 * math.prod(job[1]) * job[0].dtype.itemsize for job in jobs)


def job_sems(jobs):
    count = sum(job[3] for job in jobs)
    return [pltpu.SemaphoreType.DMA((count,))] if jobs else []


def start_jobs(jobs, sources, targets, ready):
    pairs = []
    for job, source, target in zip(jobs, sources, targets):
        pairs += job[2](source, target)
    copies = [pltpu.make_async_copy(source, target, ready.at[k]) for k, (source, target) in enumerate(pairs)]
    for copy in copies:
        copy.start()
    return copies


def anywhere(count):
    return [pl.BlockSpec(memory_space=pl.ANY)] * count


def bring(jobs, after):
    count = len(jobs)

    def kernel(*refs):
        for copy in start_jobs(jobs, refs[:count], refs[count + 1 : -1], refs[-1]):
            copy.wait()

    return pl.pallas_call(
        kernel,
        out_shape=tuple(job_shapes(jobs)),
        in_specs=anywhere(count + 1),
        out_specs=tuple(whole(count)),
        scratch_shapes=job_sems(jobs),
        compiler_params=pltpu.CompilerParams(vmem_limit_bytes=2 * MIB),
        cost_estimate=pl.CostEstimate(flops=0, bytes_accessed=job_bytes(jobs), transcendentals=0),
    )(*job_inputs(jobs), after)


def attention(query, key_new, value_new, kv_cache, kv_scale, context_len, jobs):
    requests, steps, heads, dim = query.shape
    kv_heads = key_new.shape[2]
    group = heads // kv_heads
    cache_len = kv_cache.shape[2]
    width = cache_len * kv_heads
    blocks = kv_scale.shape[3]
    inv_root = 1.0 / math.sqrt(dim)
    lines = steps * heads
    total_rows = requests * lines
    news = steps * kv_heads

    def kernel(*refs):
        count = len(jobs)
        sources, job_sources, refs = refs[:6], refs[6 : 6 + count], refs[6 + count :]
        out_ref, targets, held, ready = refs[0], refs[1 : 1 + count], refs[1 + count : 7 + count], refs[7 + count]
        length_ref, scale_ref, query_ref, key_ref, value_ref, cache_ref = held
        copies = [
            pltpu.make_async_copy(sources[k], held[k], ready.at[k]) for k in range(5)
        ] + [
            pltpu.make_async_copy(sources[5].at[:, k], cache_ref.at[:, k], ready.at[5 + k])
            for k in range(requests)
        ]
        for copy in copies:
            copy.start()
        job_copies = start_jobs(jobs, job_sources, targets, refs[-1])
        shard = lax.axis_index("seq")
        row = lax.broadcasted_iota(jnp.int32, (lines, width), 0)
        column = lax.broadcasted_iota(jnp.int32, (lines, width), 1)
        same = (row % heads) // group == column % kv_heads
        place = shard * cache_len + column // kv_heads
        new_row = lax.broadcasted_iota(jnp.int32, (lines, news), 0)
        new_column = lax.broadcasted_iota(jnp.int32, (lines, news), 1)
        new_live = (
            ((new_row % heads) // group == new_column % kv_heads)
            & (new_column // kv_heads <= new_row // heads)
            & (shard == 0)
        )
        parity = lax.broadcasted_iota(jnp.int32, (1, kv_heads * BLOCK), 1) % kv_heads

        def spread(which, request):
            pieces = []
            for block in range(blocks):
                piece = jnp.zeros((1, kv_heads * BLOCK), jnp.float32)
                for head in range(kv_heads):
                    piece = jnp.where(
                        parity == head, scale_ref[which, head, block : block + 1, request : request + 1], piece
                    )
                pieces.append(piece)
            return jnp.concatenate(pieces, axis=1)

        tops, totals = [], []
        for copy in copies[:5]:
            copy.wait()
        for request in range(requests):
            asked = query_ref[request]
            live = same & (place < length_ref[:, request : request + 1])
            copies[5 + request].wait()
            scores = lax.dot_general(
                asked, cache_ref[0, request], (((1,), (1,)), ((), ())), preferred_element_type=jnp.float32
            )
            scores = jnp.where(live, scores * spread(0, request) * inv_root, -1e30)
            recent = lax.dot_general(
                asked, key_ref[request], (((1,), (1,)), ((), ())), preferred_element_type=jnp.float32
            )
            recent = jnp.where(new_live, recent * inv_root, -1e30)
            top = jnp.maximum(
                jnp.max(scores, axis=1, keepdims=True), jnp.max(recent, axis=1, keepdims=True)
            )
            weight = jnp.where(live, jnp.exp(scores - top), 0.0)
            new_weight = jnp.where(new_live, jnp.exp(recent - top), 0.0)
            total = jnp.sum(weight, axis=1, keepdims=True) + jnp.sum(new_weight, axis=1, keepdims=True)
            mix = jnp.dot(
                (weight * spread(1, request)).astype(jnp.bfloat16),
                cache_ref[1, request],
                preferred_element_type=jnp.float32,
            ) + jnp.dot(
                new_weight.astype(jnp.bfloat16), value_ref[request], preferred_element_type=jnp.float32
            )
            for step in range(steps):
                start = (step * requests + request) * heads
                out_ref[start : start + heads, :] = mix[step * heads : (step + 1) * heads].astype(jnp.bfloat16)
            tops.append(top)
            totals.append(total)

        def by_step(values):
            return jnp.concatenate(
                [value[step * heads : (step + 1) * heads] for step in range(steps) for value in values], axis=0
            )

        lane = lax.broadcasted_iota(jnp.int32, (total_rows, LANES), 1)
        table = jnp.zeros((total_rows, LANES), jnp.float32)
        for start, value in ((0, by_step(tops)), (3, by_step(totals))):
            for k in range(3):
                piece = value.astype(jnp.bfloat16).astype(jnp.float32)
                table = jnp.where(lane == start + k, piece, table)
                value = value - piece
        turned = jnp.transpose(table)[:8]
        out_ref[total_rows:, :] = jnp.concatenate(
            [turned[:, k * LANES : (k + 1) * LANES] for k in range(total_rows // LANES)], axis=0
        ).astype(jnp.bfloat16)
        for copy in job_copies:
            copy.wait()

    given_all = (
        context_len.reshape(1, requests),
        kv_scale.transpose(0, 2, 3, 1),
        query.reshape(requests, lines, dim),
        key_new.reshape(requests, news, dim),
        value_new.reshape(requests, news, dim),
        kv_cache.reshape(2, requests, width, dim),
    )
    return pl.pallas_call(
        kernel,
        out_shape=tuple(
            [jax.ShapeDtypeStruct((total_rows + total_rows // 16, dim), jnp.bfloat16)] + job_shapes(jobs)
        ),
        in_specs=anywhere(6 + len(jobs)),
        out_specs=tuple(whole(1 + len(jobs))),
        scratch_shapes=[pltpu.VMEM(given.shape, given.dtype) for given in given_all]
        + [pltpu.SemaphoreType.DMA((5 + requests,))]
        + job_sems(jobs),
        compiler_params=pltpu.CompilerParams(vmem_limit_bytes=8 * MIB),
        cost_estimate=cost(1_000_000_000),
    )(*[pltpu.with_memory_space_constraint(given, pltpu.HBM) for given in given_all], *job_inputs(jobs))


def cost(flops):
    return pl.CostEstimate(flops=flops, bytes_accessed=0, transcendentals=0)


def merge_project(parts, weight, rows, heads, dim):
    lines = rows * heads
    count = len(parts)
    depth, width = weight.shape
    tile = tile_of(width, 512)

    def kernel(*refs):
        part_refs, weight_ref, out_ref, mixed, chosen = refs[:count], refs[count], refs[-3], refs[-2], refs[-1]
        tops, totals = [], []
        for ref in part_refs:
            stats = ref[lines:, :].astype(jnp.float32)
            wide = jnp.concatenate([stats[k * 8 : (k + 1) * 8] for k in range(lines // LANES)], axis=1)
            table = jnp.transpose(jnp.concatenate([wide, jnp.zeros((LANES - 8, lines), jnp.float32)], axis=0))
            tops.append(table[:, 0:1] + table[:, 1:2] + table[:, 2:3])
            totals.append(table[:, 3:4] + table[:, 4:5] + table[:, 5:6])
        best = tops[0]
        for top in tops[1:]:
            best = jnp.maximum(best, top)
        factors = [jnp.exp(top - best) for top in tops]
        summed = paired_sum([total * factor for total, factor in zip(totals, factors)])
        mixed[...] = (
            paired_sum([ref[:lines, :].astype(jnp.float32) * factor for ref, factor in zip(part_refs, factors)])
            / summed
        )
        for head in range(heads):
            chosen[:, head * dim : (head + 1) * dim] = mixed[pl.ds(head, rows, stride=heads), :].astype(
                jnp.bfloat16
            )
        for start in range(0, width, tile):
            out_ref[:, start : start + tile] = jnp.dot(
                chosen[...], weight_ref[:, start : start + tile], preferred_element_type=jnp.float32
            ).astype(out_ref.dtype)

    return pl.pallas_call(
        kernel,
        out_shape=jax.ShapeDtypeStruct((rows, width), jnp.bfloat16),
        in_specs=whole(count + 1),
        out_specs=whole(1)[0],
        scratch_shapes=[pltpu.VMEM((lines, dim), jnp.float32), pltpu.VMEM((rows, heads * dim), jnp.bfloat16)],
        compiler_params=pltpu.CompilerParams(vmem_limit_bytes=4 * MIB),
        cost_estimate=cost(FLOPS_AHEAD),
    )(*parts, weight)


def in_three(left):
    rows = left.shape[0]
    lane = lax.broadcasted_iota(jnp.int32, (rows, LANES), 1)
    table = jnp.zeros((rows, LANES), jnp.float32)
    for k in range(3):
        piece = left.astype(jnp.bfloat16).astype(jnp.float32)
        table = jnp.where(lane == k, piece, table)
        left = left - piece
    return table.astype(jnp.bfloat16)


def add_residual(hidden, parts, gain):
    requests, steps, width = hidden.shape
    rows = requests * steps

    def kernel(hidden_ref, gain_ref, *refs):
        part_refs, (residual_ref, gained_ref, stats_ref) = refs[:-3], refs[-3:]
        wide = [hidden_ref[request].astype(jnp.float32) for request in range(requests)]
        by_step = jnp.concatenate([part[step : step + 1] for step in range(steps) for part in wide], axis=0)
        residual = by_step + paired_sum(
            [ref[...].astype(jnp.float32) for ref in part_refs]
        )
        residual_ref[...] = residual
        gained_ref[...] = (residual * gain_ref[...]).astype(jnp.bfloat16)
        stats_ref[...] = in_three(jnp.sum(residual * residual, axis=1, keepdims=True))

    return pl.pallas_call(
        kernel,
        out_shape=(
            jax.ShapeDtypeStruct((rows, width), jnp.float32),
            jax.ShapeDtypeStruct((rows, width), jnp.bfloat16),
            jax.ShapeDtypeStruct((rows, LANES), jnp.bfloat16),
        ),
        in_specs=whole(2 + len(parts)),
        out_specs=tuple(whole(3)),
        compiler_params=pltpu.CompilerParams(vmem_limit_bytes=4 * MIB),
        cost_estimate=cost(rows * width * 8),
    )(hidden, gain.reshape(1, width), *parts)


def project_block(gained, weight, own_width, kind, stats):
    rows, depth = gained.shape
    width = 2 * own_width
    tile = tile_of(own_width, 512)
    riders = () if stats is None else (stats,)

    def kernel(gained_ref, weight_ref, *refs):
        out_ref = refs[-1]
        for part in range(2):
            for start in range(0, own_width, tile):
                out_ref[:, part * own_width + start : part * own_width + start + tile] = jnp.dot(
                    gained_ref[...], weight_ref[part, :, start : start + tile], preferred_element_type=jnp.float32
                ).astype(kind)
        if riders:
            out_ref[:, width:] = refs[0][...]

    return pl.pallas_call(
        kernel,
        out_shape=jax.ShapeDtypeStruct((rows, width + (LANES if riders else 0)), kind),
        in_specs=whole(2 + len(riders)),
        out_specs=whole(1)[0],
        compiler_params=pltpu.CompilerParams(vmem_limit_bytes=4 * MIB),
        cost_estimate=cost(2 * rows * depth * width),
    )(gained, weight, *riders)


def relay(block, arrived, stats):
    rows, width = block.shape

    def kernel(block_ref, arrived_ref, stats_ref, out_ref):
        out_ref[:, :width] = (block_ref[...] + arrived_ref[:, :width].astype(jnp.float32)).astype(jnp.bfloat16)
        both = stats_ref[...].astype(jnp.float32) + arrived_ref[:, width:].astype(jnp.float32)
        out_ref[:, width:] = in_three(jnp.sum(both, axis=1, keepdims=True))

    return pl.pallas_call(
        kernel,
        out_shape=jax.ShapeDtypeStruct((rows, width + LANES), jnp.bfloat16),
        in_specs=whole(3),
        out_specs=whole(1)[0],
        compiler_params=pltpu.CompilerParams(vmem_limit_bytes=4 * MIB),
        cost_estimate=cost(rows * width * 8),
    )(block, arrived, stats)


def convolve(own, near, received, squares, state, taps, bias, weight, features):
    rows, width = own.shape
    own_width = width // 2
    requests = state.shape[1]
    taps_count = taps.shape[0]
    mixed_width = weight.shape[0]
    count = len(squares)

    def kernel(own_ref, near_ref, received_ref, state_ref, taps_ref, bias_ref, weight_ref, *refs):
        squares_refs, (conv_ref, gate_ref, mixing_ref) = refs[:count], refs[count:]
        pieces = received_ref[:, width:].astype(jnp.float32)
        for ref in squares_refs:
            pieces = pieces + ref[:, ref.shape[1] - LANES :].astype(jnp.float32)
        channels = (own_ref[...] + near_ref[...].astype(jnp.float32)) + received_ref[:, :width].astype(jnp.float32)
        squares = jnp.sum(pieces, axis=1, keepdims=True)
        channels = (channels * lax.rsqrt(squares / features + EPS)).astype(jnp.bfloat16)
        gate_ref[...] = channels[:, own_width:]
        window = jnp.concatenate(
            [state_ref[k].astype(jnp.float32) for k in range(taps_count - 1)]
            + [channels[:, :own_width].astype(jnp.float32)],
            axis=0,
        )
        total = bias_ref[...]
        for tap in range(taps_count):
            total = total + taps_ref[tap : tap + 1, :].astype(jnp.float32) * window[
                tap * requests : tap * requests + rows
            ]
        conv = (total * jax.nn.sigmoid(total)).astype(jnp.bfloat16)
        conv_ref[...] = conv
        mixing_ref[...] = lax.dot_general(
            conv, weight_ref[...], (((1,), (1,)), ((), ())), preferred_element_type=jnp.float32
        )

    return pl.pallas_call(
        kernel,
        out_shape=(
            jax.ShapeDtypeStruct((rows, own_width), jnp.bfloat16),
            jax.ShapeDtypeStruct((rows, own_width), jnp.bfloat16),
            jax.ShapeDtypeStruct((rows, mixed_width), jnp.float32),
        ),
        in_specs=whole(7 + count),
        out_specs=tuple(whole(3)),
        compiler_params=pltpu.CompilerParams(vmem_limit_bytes=8 * MIB),
        cost_estimate=cost(FLOPS_AHEAD),
    )(own, near, received, state, taps, bias, weight, *squares)


def scan_states(mixing, conv, gate, dt_weight, dt_bias, decay, skip, state, brought):
    rows, own_width = conv.shape
    requests, state_width = state.shape[:2]
    low_width = dt_weight.shape[0]

    def kernel(mixing_ref, conv_ref, gate_ref, dt_ref, bias_ref, decay_ref, skip_ref, state_ref, brought_ref, *refs):
        gated_ref, next_ref, out = refs
        low = mixing_ref[:, :low_width]
        low_rank = (low * lax.rsqrt(jnp.mean(low * low, axis=1, keepdims=True) + EPS)).astype(jnp.bfloat16)
        step_size = jnp.dot(low_rank, dt_ref[...], preferred_element_type=jnp.float32) + bias_ref[...]
        step_size = jnp.maximum(step_size, 0.0) + jnp.log1p(jnp.exp(-jnp.abs(step_size)))
        mats = mixing_ref[:, low_width : low_width + 2 * state_width]
        lane = lax.broadcasted_iota(jnp.int32, mats.shape, 1)
        power = mats * mats
        first = jnp.sum(jnp.where(lane < state_width, power, 0.0), axis=1, keepdims=True)
        second = jnp.sum(jnp.where(lane < state_width, 0.0, power), axis=1, keepdims=True)
        mats = mats * lax.rsqrt(jnp.where(lane < state_width, first, second) / state_width + EPS)
        mats = jnp.concatenate([mats, jnp.zeros((rows, LANES - 2 * state_width), jnp.float32)], axis=1)
        turned = jnp.transpose(jnp.concatenate([mats, jnp.zeros((LANES - rows, LANES), jnp.float32)], axis=0))
        signal = conv_ref[...].astype(jnp.float32)
        drive = step_size * signal
        decay = decay_ref[...]
        for request in range(requests):
            memory = state_ref[request]
            for row in range(request, rows, requests):
                memory = (
                    jnp.exp(-step_size[row : row + 1] * decay) * memory
                    + drive[row : row + 1] * turned[:state_width, row : row + 1]
                )
                out[row : row + 1, :] = jnp.sum(
                    memory * turned[state_width : 2 * state_width, row : row + 1], axis=0, keepdims=True
                )
            next_ref[request] = memory
        gate = gate_ref[...].astype(jnp.float32)
        gated_ref[...] = ((out[...] + skip_ref[...] * signal) * (gate * jax.nn.sigmoid(gate))).astype(
            jnp.bfloat16
        )

    return pl.pallas_call(
        kernel,
        out_shape=(
            jax.ShapeDtypeStruct((rows, own_width), jnp.bfloat16),
            jax.ShapeDtypeStruct(state.shape, jnp.float32),
        ),
        in_specs=whole(8) + [pl.BlockSpec(memory_space=pl.ANY)],
        out_specs=tuple(whole(2)),
        scratch_shapes=[pltpu.VMEM((rows, own_width), jnp.float32)],
        compiler_params=pltpu.CompilerParams(vmem_limit_bytes=8 * MIB),
        cost_estimate=cost(FLOPS_AHEAD // 4),
    )(mixing, conv, gate, dt_weight, dt_bias, decay, skip, state, brought)


def project_out(blocks, weights, before):
    rows, own_width = blocks[0].shape
    width = weights[0].shape[2]
    count = len(blocks)
    end = count + len(weights)
    tile = tile_of(width, 512)
    kind = jnp.float32 if before is None else jnp.bfloat16
    places = [(k, place) for k, weight in enumerate(weights) for place in range(weight.shape[0])]

    def kernel(*refs):
        block_refs, weight_refs, out_ref = refs[:count], refs[count:end], refs[-1]
        for start in range(0, width, tile):
            columns = slice(start, start + tile)
            total = None if before is None else refs[end][:, columns]
            for ref, (k, place) in zip(block_refs, places):
                term = jnp.dot(ref[...], weight_refs[k][place, :, columns], preferred_element_type=jnp.float32)
                total = term if total is None else total + term
            out_ref[:, columns] = total.astype(kind)

    extra = () if before is None else (before,)
    return pl.pallas_call(
        kernel,
        out_shape=jax.ShapeDtypeStruct((rows, width), kind),
        in_specs=whole(end + len(extra)),
        out_specs=whole(1)[0],
        compiler_params=pltpu.CompilerParams(vmem_limit_bytes=4 * MIB),
        cost_estimate=cost(2 * rows * own_width * width * count),
    )(*blocks, *weights, *extra)


def finish(residual, parts, requests):
    rows, width = residual.shape
    steps = rows // requests

    def kernel(residual_ref, *refs):
        part_refs, out_ref, total = refs[:-2], refs[-2], refs[-1]
        total[...] = residual_ref[...] + paired_sum([ref[...].astype(jnp.float32) for ref in part_refs])
        for request in range(requests):
            out_ref[request] = jnp.concatenate(
                [total[step * requests + request : step * requests + request + 1, :] for step in range(steps)],
                axis=0,
            ).astype(jnp.bfloat16)

    return pl.pallas_call(
        kernel,
        out_shape=jax.ShapeDtypeStruct((requests, steps, width), jnp.bfloat16),
        in_specs=whole(1 + len(parts)),
        out_specs=whole(1)[0],
        scratch_shapes=[pltpu.VMEM((rows, width), jnp.float32)],
        compiler_params=pltpu.CompilerParams(vmem_limit_bytes=4 * MIB),
        cost_estimate=cost(rows * width * 8),
    )(residual, *parts)


def plain_attention(query, key_new, value_new, kv_cache, kv_scale, context_len):
    requests, steps, heads, dim = query.shape
    kv_heads = key_new.shape[2]
    group = heads // kv_heads
    cache_len = kv_cache.shape[2]
    width = cache_len * kv_heads
    inv_root = 1.0 / math.sqrt(dim)
    first = lax.axis_index("seq") == 0
    flat_query = query.reshape(requests, steps * heads, dim)
    flat_cache = kv_cache.reshape(2, requests, width, dim)
    column = jnp.arange(width, dtype=jnp.int32)
    row = jnp.arange(steps * heads, dtype=jnp.int32)
    row_kv = (row % heads) // group
    same = row_kv[:, None] == (column % kv_heads)[None, :]
    place = lax.axis_index("seq") * cache_len + column // kv_heads
    live = same[None] & (place[None, :] < context_len[:, None])[:, None, :]
    spread = jnp.repeat(kv_scale.transpose(0, 1, 3, 2), BLOCK, axis=2).reshape(2, requests, width)
    scores = jnp.einsum("rqd,rpd->rqp", flat_query, flat_cache[0], preferred_element_type=jnp.float32)
    scores = jnp.where(live, scores * spread[0][:, None, :] * inv_root, -1e30)
    flat_new_k = key_new.reshape(requests, steps * kv_heads, dim)
    flat_new_v = value_new.reshape(requests, steps * kv_heads, dim)
    new_column = jnp.arange(steps * kv_heads, dtype=jnp.int32)
    new_live = (
        (row_kv[:, None] == (new_column % kv_heads)[None, :])
        & ((new_column // kv_heads)[None, :] <= (row // heads)[:, None])
        & first
    )[None]
    recent = jnp.einsum("rqd,rjd->rqj", flat_query, flat_new_k, preferred_element_type=jnp.float32)
    recent = jnp.where(new_live, recent * inv_root, -1e30)
    top = jnp.maximum(jnp.max(scores, axis=-1), jnp.max(recent, axis=-1))
    weight = jnp.where(live, jnp.exp(scores - top[..., None]), 0.0)
    new_weight = jnp.where(new_live, jnp.exp(recent - top[..., None]), 0.0)
    total = jnp.sum(weight, axis=-1) + jnp.sum(new_weight, axis=-1)
    scaled = (weight * spread[1][:, None, :]).astype(jnp.bfloat16)
    mix = jnp.einsum("rqp,rpd->rqd", scaled, flat_cache[1], preferred_element_type=jnp.float32)
    mix = mix + jnp.einsum(
        "rqj,rjd->rqd", new_weight.astype(jnp.bfloat16), flat_new_v, preferred_element_type=jnp.float32
    )
    rows = requests * steps
    return mix.reshape(rows, heads, dim), top.reshape(rows, heads), total.reshape(rows, heads)


def merge(mixes, tops, totals):
    best = tops[0]
    for top in tops[1:]:
        best = jnp.maximum(best, top)
    factors = [jnp.exp(top - best) for top in tops]
    summed = paired_sum([total * factor for total, factor in zip(totals, factors)])
    mixed = paired_sum(
        [mix.astype(jnp.float32) * factor[..., None] for mix, factor in zip(mixes, factors)]
    )
    return (mixed / summed[..., None]).astype(jnp.bfloat16)


def plain(
    hidden,
    query,
    key_new,
    value_new,
    kv_cache,
    kv_scale,
    context_len,
    attn_out_weight,
    norm_gain,
    in_weight,
    conv_weight,
    conv_bias,
    conv_state,
    xproj_weight,
    dt_weight,
    dt_bias,
    decay_rate,
    skip_gain,
    ssm_state,
    mamba_out_weight,
):
    requests, steps = hidden.shape[:2]
    rows = requests * steps
    seq_count = lax.axis_size("seq")
    hs_count = lax.axis_size(HS)
    hs_index = lax.axis_index(HS)
    heads = query.shape[2]
    dim = query.shape[3]
    mix, top, total = plain_attention(query, key_new, value_new, kv_cache, kv_scale, context_len)
    mixes, tops, totals = (lax.all_gather(part, "seq") for part in (mix, top, total))
    every = range(seq_count)
    own_heads = merge([mixes[k] for k in every], [tops[k] for k in every], [totals[k] for k in every])
    every_head = lax.all_gather(own_heads.reshape(rows, heads * dim), HS, axis=1, tiled=True)
    width_in = attn_out_weight.shape[0]
    chosen = lax.dynamic_slice_in_dim(every_head, lax.axis_index("seq") * width_in, width_in, 1)
    attended = sum_over(
        jnp.dot(chosen, attn_out_weight, preferred_element_type=jnp.float32), "seq", jnp.bfloat16
    )
    residual = hidden.astype(jnp.float32).reshape(rows, -1) + attended
    features = residual.shape[1] * hs_count
    squares = jnp.sum(residual * residual, axis=-1, keepdims=True)
    gained = (residual * norm_gain).astype(jnp.bfloat16)
    projected = jnp.einsum("nd,cde->nce", gained, in_weight, preferred_element_type=jnp.float32)
    own_width = conv_weight.shape[0]
    upper, lower = split_pair(squares)

    def block_for(index):
        block = lax.dynamic_slice_in_dim(projected, index * own_width, own_width, 2)
        return block.reshape(rows, 2 * own_width)

    channels = block_for(hs_index)
    for hop in range(1, hs_count):
        block = jnp.concatenate([block_for((hs_index + hop) % hs_count), upper, lower], axis=1)
        part = shifted(block.astype(jnp.bfloat16), HS, hop).astype(jnp.float32)
        channels = channels + part[:, : 2 * own_width]
        squares = squares + part[:, 2 * own_width : 2 * own_width + 1] + part[:, 2 * own_width + 1 :]
    channels = channels * lax.rsqrt(squares / features + EPS)
    conv_in = channels[:, :own_width].astype(jnp.bfloat16)
    gate_in = channels[:, own_width:].astype(jnp.bfloat16)
    window = jnp.concatenate(
        [
            conv_state.astype(jnp.float32),
            conv_in.astype(jnp.float32).reshape(requests, steps, own_width),
        ],
        axis=1,
    )
    conv_sum = jnp.zeros((requests, steps, own_width), jnp.float32) + conv_bias
    for tap in range(conv_weight.shape[1]):
        conv_sum = conv_sum + conv_weight[:, tap].astype(jnp.float32) * window[:, tap : tap + steps, :]
    conv_out = jax.nn.silu(conv_sum).astype(jnp.bfloat16).reshape(rows, own_width)
    mixing = jnp.dot(conv_out, xproj_weight, preferred_element_type=jnp.float32)
    mixing = sum_over(sum_over(mixing, HS), "seq")
    low_width = dt_weight.shape[0]
    state_width = decay_rate.shape[1]
    low_rank = rms_unit(mixing[:, :low_width]).astype(jnp.bfloat16)
    input_mat = rms_unit(mixing[:, low_width : low_width + state_width]).reshape(
        requests, steps, state_width
    )
    output_mat = rms_unit(mixing[:, low_width + state_width :]).reshape(requests, steps, state_width)
    delta = jax.nn.softplus(
        jnp.dot(low_rank, dt_weight, preferred_element_type=jnp.float32) + dt_bias
    ).reshape(requests, steps, own_width)
    signal = conv_out.astype(jnp.float32).reshape(requests, steps, own_width)
    memory = ssm_state
    outputs = []
    for moment in range(steps):
        step_now = delta[:, moment]
        memory = (
            jnp.exp(-step_now[..., None] * decay_rate) * memory
            + (step_now * signal[:, moment])[..., None] * input_mat[:, moment][:, None, :]
        )
        outputs.append(
            jnp.sum(memory * output_mat[:, moment][:, None, :], axis=-1)
            + skip_gain * signal[:, moment]
        )
    stacked = jnp.stack(outputs, axis=1).reshape(rows, own_width)
    gated_out = (stacked * jax.nn.silu(gate_in.astype(jnp.float32))).astype(jnp.bfloat16)
    gated_block = lax.all_gather(gated_out, HS, axis=1, tiled=True)
    mamba_part = sum_over(
        jnp.dot(gated_block, mamba_out_weight, preferred_element_type=jnp.float32), "seq", jnp.bfloat16
    )
    final = (residual + mamba_part).astype(jnp.bfloat16).reshape(requests, steps, -1)
    return (final, memory)


def local(
    hidden,
    query,
    key_new,
    value_new,
    kv_cache,
    kv_scale,
    context_len,
    attn_out_weight,
    norm_gain,
    in_weight,
    conv_weight,
    conv_bias,
    conv_state,
    xproj_weight,
    dt_weight,
    dt_bias,
    decay_rate,
    skip_gain,
    ssm_state,
    mamba_out_weight,
):
    requests, steps = hidden.shape[:2]
    rows = requests * steps
    seq_count = lax.axis_size("seq")
    hs_count = lax.axis_size(HS)
    heads, dim = query.shape[2:]
    own_width = conv_weight.shape[0]
    if (
        lax.axis_size("head") != 2
        or lax.axis_size("sub") != 2
        or seq_count != hs_count
        or own_width % LANES
        or dim != LANES
        or (rows * heads) % LANES
        or rows % 16
    ):
        return plain(
            hidden,
            query,
            key_new,
            value_new,
            kv_cache,
            kv_scale,
            context_len,
            attn_out_weight,
            norm_gain,
            in_weight,
            conv_weight,
            conv_bias,
            conv_state,
            xproj_weight,
            dt_weight,
            dt_bias,
            decay_rate,
            skip_gain,
            ssm_state,
            mamba_out_weight,
        )
    part, out_rows = attention(
        query, key_new, value_new, kv_cache, kv_scale, context_len, [whole_job(attn_out_weight)]
    )
    columns = lambda flip: block_job(in_weight, own_width, flip)
    far_columns, chip_columns = bring([columns(3), columns(2)], part)
    place = range(hs_count)
    parts = [
        lax.ppermute(
            part,
            ("seq",) + HS,
            [
                (s * hs_count + j, j * hs_count + ((s // 2 + turn) % 2) * 2 + s % 2)
                for s in range(seq_count)
                for j in place
            ],
        )
        for turn in range(2)
    ]
    parts, far_columns, chip_columns = lax.optimization_barrier((parts, far_columns, chip_columns))
    parts = parts + [crossed(arrived, "sub", 1) for arrived in parts]
    partial = merge_project(parts, out_rows, rows, heads, dim)
    core_columns, own_columns = bring([columns(1), columns(0)], partial)
    terms, core_columns, own_columns = lax.optimization_barrier(
        (crossed_all(partial, "seq"), core_columns, own_columns)
    )
    residual, gained, stats = add_residual(hidden, terms, norm_gain)
    features = residual.shape[1] * hs_count
    for_far = crossed(project_block(gained, far_columns, own_width, jnp.bfloat16, stats), "sub", 1)
    block = relay(project_block(gained, chip_columns, own_width, jnp.float32, None), for_far, stats)
    received = crossed(block, "head", 1)
    late, block = lax.optimization_barrier((gained, block))
    near = crossed(project_block(late, core_columns, own_width, jnp.bfloat16, None), "sub", 1)
    own = project_block(late, own_columns, own_width, jnp.float32, None)
    conv, gate, mixing = convolve(
        own,
        near,
        received,
        [stats, for_far],
        conv_state.transpose(1, 0, 2),
        conv_weight.T,
        conv_bias.reshape(1, -1),
        xproj_weight.T,
        features,
    )
    mixing = mixing + crossed(mixing, "sub", 1)
    mamba_rows = lambda flips: rows_job(mamba_out_weight, own_width, flips)
    own_rows, other_rows = bring([mamba_rows([0]), mamba_rows([1, 2])], mixing)
    base = lambda s, x, c: s * hs_count + x * 2 + c
    arrived = [
        lax.ppermute(
            mixing,
            ("seq",) + HS,
            [(base(s, x, 1), base(s ^ flip, x ^ 1, 1)) for s in range(seq_count) for x in range(2)]
            + [(base(s, x, 0), base(s ^ flip, x, 0)) for s in range(seq_count) for x in range(2) if flip],
        )
        for flip in range(seq_count - 1, -1, -1)
    ]
    arrived, own_rows, other_rows = lax.optimization_barrier((arrived, own_rows, other_rows))
    line = jnp.where(lax.axis_index("sub") == 0, mixing, 0.0) + paired_sum(arrived)
    mixing = line + crossed(line, "sub", 1)
    gated, state = scan_states(
        mixing,
        conv,
        gate,
        dt_weight,
        dt_bias.reshape(1, -1),
        decay_rate.T,
        skip_gain.reshape(1, -1),
        ssm_state.transpose(0, 2, 1),
        other_rows,
    )
    (last_rows,) = bring([mamba_rows([3])], gated)
    first = project_out([gated], [own_rows], None)
    blocks, last_rows, first = lax.optimization_barrier((crossed_all(gated, HS), last_rows, first))
    partial = project_out(blocks[1:], [other_rows, last_rows], first)
    final = finish(residual, crossed_all(partial, "seq"), requests)
    return final, state.transpose(0, 2, 1)


def solution(mesh):
    return jax.shard_map(
        local,
        mesh=mesh,
        in_specs=(
            P("groups", None, HS),
            P("groups", None, HS, None),
            P("groups", None, HS, None),
            P("groups", None, HS, None),
            P(None, "groups", "seq", HS, None),
            P(None, "groups", HS, "seq"),
            P("groups"),
            P("seq", HS),
            P(HS),
            P(None, HS, "seq"),
            P(("seq",) + HS, None),
            P(("seq",) + HS),
            P("groups", None, ("seq",) + HS),
            P(("seq",) + HS, None),
            P(None, ("seq",) + HS),
            P(("seq",) + HS),
            P(("seq",) + HS, None),
            P(("seq",) + HS),
            P("groups", ("seq",) + HS, None),
            P("seq", HS),
        ),
        out_specs=(P("groups", None, HS), P("groups", ("seq",) + HS, None)),
        check_vma=False,
    )
```

```python
import math

import jax
import jax.numpy as jnp
from jax import lax
from jax.experimental import pallas as pl
from jax.experimental.pallas import tpu as pltpu
from jax.sharding import PartitionSpec as P

BLOCK = 128
EPS = 1e-06
HS = ("head", "sub")
DIRECT = 8
LANES = 128
MIB = 1024 * 1024
PIECES = 4
FLOPS_AHEAD = 20_000_000_000


def shifted(value, axes, hop):
    count = lax.axis_size(axes)
    return lax.ppermute(value, axes, [(i, (i + hop) % count) for i in range(count)])


def paired_sum(terms):
    if len(terms) == 1:
        return terms[0]
    return paired_sum(terms[::2]) + paired_sum(terms[1::2])


def crossed(value, axes, flip):
    return lax.ppermute(value, axes, [(i, i ^ flip) for i in range(lax.axis_size(axes))])


def crossed_all(value, axes):
    count = lax.axis_size(axes)
    far_first = {flip: crossed(value, axes, flip) for flip in range(count - 1, 0, -1)}
    return [value] + [far_first[flip] for flip in range(1, count)]


def everyone(value, axes):
    return [value] + [shifted(value, axes, hop) for hop in range(1, lax.axis_size(axes))]


def sum_over(value, axes, kind=None):
    if lax.axis_size(axes) > DIRECT:
        return lax.psum(value, axes)
    if kind is not None:
        value = lax.optimization_barrier(value.astype(kind))
    return paired_sum([part.astype(jnp.float32) for part in everyone(value, axes)])


def split_pair(value):
    upper = lax.reduce_precision(value, 8, 7)
    return upper, lax.reduce_precision(value - upper, 8, 7)


def rms_unit(values):
    return values * lax.rsqrt(jnp.mean(values * values, axis=-1, keepdims=True) + EPS)


def tile_of(width, limit):
    tile = width
    while tile > limit and tile % 2 == 0 and (tile // 2) % 128 == 0:
        tile //= 2
    return tile


def whole(count):
    return [pl.BlockSpec(memory_space=pltpu.VMEM)] * count


def in_pieces(source, target):
    rows = target.shape[0] // PIECES
    return [(source.at[k * rows : (k + 1) * rows], target.at[k * rows : (k + 1) * rows]) for k in range(PIECES)]


def hs_position():
    return lax.axis_index("head") * lax.axis_size("sub") + lax.axis_index("sub")


def whole_job(weight):
    return weight, weight.shape, in_pieces, PIECES


def block_job(weight, own_width, flip):
    def views(source, target):
        columns = pl.ds(pl.multiple_of((hs_position() ^ flip) * own_width, own_width), own_width)
        return [
            pair for part in range(2) for pair in in_pieces(source.at[part, :, columns], target.at[part])
        ]

    return weight, (2, weight.shape[1], own_width), views, 2 * PIECES


def job_shapes(jobs):
    return [pltpu.VMEM(job[1], job[0].dtype) for job in jobs]


def job_inputs(jobs):
    return [pltpu.with_memory_space_constraint(job[0], pltpu.HBM) for job in jobs]


def job_bytes(jobs):
    return sum(2 * math.prod(job[1]) * job[0].dtype.itemsize for job in jobs)


def job_sems(jobs):
    count = sum(job[3] for job in jobs)
    return [pltpu.SemaphoreType.DMA((count,))] if jobs else []


def start_jobs(jobs, sources, targets, ready):
    pairs = []
    for job, source, target in zip(jobs, sources, targets):
        pairs += job[2](source, target)
    copies = [pltpu.make_async_copy(source, target, ready.at[k]) for k, (source, target) in enumerate(pairs)]
    for copy in copies:
        copy.start()
    return copies


def anywhere(count):
    return [pl.BlockSpec(memory_space=pl.ANY)] * count


def bring(jobs, after):
    count = len(jobs)

    def kernel(*refs):
        for copy in start_jobs(jobs, refs[:count], refs[count + 1 : -1], refs[-1]):
            copy.wait()

    return pl.pallas_call(
        kernel,
        out_shape=tuple(job_shapes(jobs)),
        in_specs=anywhere(count + 1),
        out_specs=tuple(whole(count)),
        scratch_shapes=job_sems(jobs),
        compiler_params=pltpu.CompilerParams(vmem_limit_bytes=2 * MIB),
        cost_estimate=pl.CostEstimate(flops=0, bytes_accessed=job_bytes(jobs), transcendentals=0),
    )(*job_inputs(jobs), after)


def attention(query, key_new, value_new, kv_cache, kv_scale, context_len, jobs):
    requests, steps, heads, dim = query.shape
    kv_heads = key_new.shape[2]
    group = heads // kv_heads
    cache_len = kv_cache.shape[2]
    width = cache_len * kv_heads
    blocks = kv_scale.shape[3]
    inv_root = 1.0 / math.sqrt(dim)
    lines = steps * heads
    total_rows = requests * lines
    news = steps * kv_heads

    def kernel(*refs):
        count = len(jobs)
        sources, job_sources, refs = refs[:6], refs[6 : 6 + count], refs[6 + count :]
        out_ref, targets, held, ready = refs[0], refs[1 : 1 + count], refs[1 + count : 7 + count], refs[7 + count]
        length_ref, scale_ref, query_ref, key_ref, value_ref, cache_ref = held
        copies = [
            pltpu.make_async_copy(sources[k], held[k], ready.at[k]) for k in range(5)
        ] + [
            pltpu.make_async_copy(sources[5].at[:, k], cache_ref.at[:, k], ready.at[5 + k])
            for k in range(requests)
        ]
        for copy in copies:
            copy.start()
        job_copies = start_jobs(jobs, job_sources, targets, refs[-1])
        shard = lax.axis_index("seq")
        row = lax.broadcasted_iota(jnp.int32, (lines, width), 0)
        column = lax.broadcasted_iota(jnp.int32, (lines, width), 1)
        same = (row % heads) // group == column % kv_heads
        place = shard * cache_len + column // kv_heads
        new_row = lax.broadcasted_iota(jnp.int32, (lines, news), 0)
        new_column = lax.broadcasted_iota(jnp.int32, (lines, news), 1)
        new_live = (
            ((new_row % heads) // group == new_column % kv_heads)
            & (new_column // kv_heads <= new_row // heads)
            & (shard == 0)
        )
        parity = lax.broadcasted_iota(jnp.int32, (1, kv_heads * BLOCK), 1) % kv_heads

        def spread(which, request):
            pieces = []
            for block in range(blocks):
                piece = jnp.zeros((1, kv_heads * BLOCK), jnp.float32)
                for head in range(kv_heads):
                    piece = jnp.where(
                        parity == head, scale_ref[which, head, block : block + 1, request : request + 1], piece
                    )
                pieces.append(piece)
            return jnp.concatenate(pieces, axis=1)

        tops, totals = [], []
        for copy in copies[:5]:
            copy.wait()
        for request in range(requests):
            asked = query_ref[request]
            live = same & (place < length_ref[:, request : request + 1])
            copies[5 + request].wait()
            scores = lax.dot_general(
                asked, cache_ref[0, request], (((1,), (1,)), ((), ())), preferred_element_type=jnp.float32
            )
            scores = jnp.where(live, scores * spread(0, request) * inv_root, -1e30)
            recent = lax.dot_general(
                asked, key_ref[request], (((1,), (1,)), ((), ())), preferred_element_type=jnp.float32
            )
            recent = jnp.where(new_live, recent * inv_root, -1e30)
            top = jnp.maximum(
                jnp.max(scores, axis=1, keepdims=True), jnp.max(recent, axis=1, keepdims=True)
            )
            weight = jnp.where(live, jnp.exp(scores - top), 0.0)
            new_weight = jnp.where(new_live, jnp.exp(recent - top), 0.0)
            total = jnp.sum(weight, axis=1, keepdims=True) + jnp.sum(new_weight, axis=1, keepdims=True)
            mix = jnp.dot(
                (weight * spread(1, request)).astype(jnp.bfloat16),
                cache_ref[1, request],
                preferred_element_type=jnp.float32,
            ) + jnp.dot(
                new_weight.astype(jnp.bfloat16), value_ref[request], preferred_element_type=jnp.float32
            )
            for step in range(steps):
                start = (step * requests + request) * heads
                out_ref[start : start + heads, :] = mix[step * heads : (step + 1) * heads].astype(jnp.bfloat16)
            tops.append(top)
            totals.append(total)

        def by_step(values):
            return jnp.concatenate(
                [value[step * heads : (step + 1) * heads] for step in range(steps) for value in values], axis=0
            )

        lane = lax.broadcasted_iota(jnp.int32, (total_rows, LANES), 1)
        table = jnp.zeros((total_rows, LANES), jnp.float32)
        for start, value in ((0, by_step(tops)), (3, by_step(totals))):
            for k in range(3):
                piece = value.astype(jnp.bfloat16).astype(jnp.float32)
                table = jnp.where(lane == start + k, piece, table)
                value = value - piece
        turned = jnp.transpose(table)[:8]
        out_ref[total_rows:, :] = jnp.concatenate(
            [turned[:, k * LANES : (k + 1) * LANES] for k in range(total_rows // LANES)], axis=0
        ).astype(jnp.bfloat16)
        for copy in job_copies:
            copy.wait()

    given_all = (
        context_len.reshape(1, requests),
        kv_scale.transpose(0, 2, 3, 1),
        query.reshape(requests, lines, dim),
        key_new.reshape(requests, news, dim),
        value_new.reshape(requests, news, dim),
        kv_cache.reshape(2, requests, width, dim),
    )
    return pl.pallas_call(
        kernel,
        out_shape=tuple(
            [jax.ShapeDtypeStruct((total_rows + total_rows // 16, dim), jnp.bfloat16)] + job_shapes(jobs)
        ),
        in_specs=anywhere(6 + len(jobs)),
        out_specs=tuple(whole(1 + len(jobs))),
        scratch_shapes=[pltpu.VMEM(given.shape, given.dtype) for given in given_all]
        + [pltpu.SemaphoreType.DMA((5 + requests,))]
        + job_sems(jobs),
        compiler_params=pltpu.CompilerParams(vmem_limit_bytes=8 * MIB),
        cost_estimate=cost(1_000_000_000),
    )(*[pltpu.with_memory_space_constraint(given, pltpu.HBM) for given in given_all], *job_inputs(jobs))


def cost(flops):
    return pl.CostEstimate(flops=flops, bytes_accessed=0, transcendentals=0)


def merge_project(parts, weight, rows, heads, dim):
    lines = rows * heads
    count = len(parts)
    depth, width = weight.shape
    tile = tile_of(width, 512)

    def kernel(*refs):
        part_refs, weight_ref, out_ref, mixed, chosen = refs[:count], refs[count], refs[-3], refs[-2], refs[-1]
        tops, totals = [], []
        for ref in part_refs:
            stats = ref[lines:, :].astype(jnp.float32)
            wide = jnp.concatenate([stats[k * 8 : (k + 1) * 8] for k in range(lines // LANES)], axis=1)
            table = jnp.transpose(jnp.concatenate([wide, jnp.zeros((LANES - 8, lines), jnp.float32)], axis=0))
            tops.append(table[:, 0:1] + table[:, 1:2] + table[:, 2:3])
            totals.append(table[:, 3:4] + table[:, 4:5] + table[:, 5:6])
        best = tops[0]
        for top in tops[1:]:
            best = jnp.maximum(best, top)
        factors = [jnp.exp(top - best) for top in tops]
        summed = paired_sum([total * factor for total, factor in zip(totals, factors)])
        mixed[...] = (
            paired_sum([ref[:lines, :].astype(jnp.float32) * factor for ref, factor in zip(part_refs, factors)])
            / summed
        )
        for head in range(heads):
            chosen[:, head * dim : (head + 1) * dim] = mixed[pl.ds(head, rows, stride=heads), :].astype(
                jnp.bfloat16
            )
        for start in range(0, width, tile):
            out_ref[:, start : start + tile] = jnp.dot(
                chosen[...], weight_ref[:, start : start + tile], preferred_element_type=jnp.float32
            ).astype(out_ref.dtype)

    return pl.pallas_call(
        kernel,
        out_shape=jax.ShapeDtypeStruct((rows, width), jnp.bfloat16),
        in_specs=whole(count + 1),
        out_specs=whole(1)[0],
        scratch_shapes=[pltpu.VMEM((lines, dim), jnp.float32), pltpu.VMEM((rows, heads * dim), jnp.bfloat16)],
        compiler_params=pltpu.CompilerParams(vmem_limit_bytes=4 * MIB),
        cost_estimate=cost(FLOPS_AHEAD),
    )(*parts, weight)


def in_three(left):
    rows = left.shape[0]
    lane = lax.broadcasted_iota(jnp.int32, (rows, LANES), 1)
    table = jnp.zeros((rows, LANES), jnp.float32)
    for k in range(3):
        piece = left.astype(jnp.bfloat16).astype(jnp.float32)
        table = jnp.where(lane == k, piece, table)
        left = left - piece
    return table.astype(jnp.bfloat16)


def add_residual(hidden, parts, gain):
    requests, steps, width = hidden.shape
    rows = requests * steps

    def kernel(hidden_ref, gain_ref, *refs):
        part_refs, (residual_ref, gained_ref, stats_ref) = refs[:-3], refs[-3:]
        wide = [hidden_ref[request].astype(jnp.float32) for request in range(requests)]
        by_step = jnp.concatenate([part[step : step + 1] for step in range(steps) for part in wide], axis=0)
        residual = by_step + paired_sum(
            [ref[...].astype(jnp.float32) for ref in part_refs]
        )
        residual_ref[...] = residual
        gained_ref[...] = (residual * gain_ref[...]).astype(jnp.bfloat16)
        stats_ref[...] = in_three(jnp.sum(residual * residual, axis=1, keepdims=True))

    return pl.pallas_call(
        kernel,
        out_shape=(
            jax.ShapeDtypeStruct((rows, width), jnp.float32),
            jax.ShapeDtypeStruct((rows, width), jnp.bfloat16),
            jax.ShapeDtypeStruct((rows, LANES), jnp.bfloat16),
        ),
        in_specs=whole(2 + len(parts)),
        out_specs=tuple(whole(3)),
        compiler_params=pltpu.CompilerParams(vmem_limit_bytes=4 * MIB),
        cost_estimate=cost(rows * width * 8),
    )(hidden, gain.reshape(1, width), *parts)


def project_block(gained, weight, own_width, kind, stats):
    rows, depth = gained.shape
    width = 2 * own_width
    tile = tile_of(own_width, 512)
    riders = () if stats is None else (stats,)

    def kernel(gained_ref, weight_ref, *refs):
        out_ref = refs[-1]
        for part in range(2):
            for start in range(0, own_width, tile):
                out_ref[:, part * own_width + start : part * own_width + start + tile] = jnp.dot(
                    gained_ref[...], weight_ref[part, :, start : start + tile], preferred_element_type=jnp.float32
                ).astype(kind)
        if riders:
            out_ref[:, width:] = refs[0][...]

    return pl.pallas_call(
        kernel,
        out_shape=jax.ShapeDtypeStruct((rows, width + (LANES if riders else 0)), kind),
        in_specs=whole(2 + len(riders)),
        out_specs=whole(1)[0],
        compiler_params=pltpu.CompilerParams(vmem_limit_bytes=4 * MIB),
        cost_estimate=cost(2 * rows * depth * width),
    )(gained, weight, *riders)


def relay(block, arrived, stats):
    rows, width = block.shape

    def kernel(block_ref, arrived_ref, stats_ref, out_ref):
        out_ref[:, :width] = (block_ref[...] + arrived_ref[:, :width].astype(jnp.float32)).astype(jnp.bfloat16)
        both = stats_ref[...].astype(jnp.float32) + arrived_ref[:, width:].astype(jnp.float32)
        out_ref[:, width:] = in_three(jnp.sum(both, axis=1, keepdims=True))

    return pl.pallas_call(
        kernel,
        out_shape=jax.ShapeDtypeStruct((rows, width + LANES), jnp.bfloat16),
        in_specs=whole(3),
        out_specs=whole(1)[0],
        compiler_params=pltpu.CompilerParams(vmem_limit_bytes=4 * MIB),
        cost_estimate=cost(rows * width * 8),
    )(block, arrived, stats)


def convolve(own, near, received, squares, state, taps, bias, weight, features):
    rows, width = own.shape
    own_width = width // 2
    requests = state.shape[1]
    taps_count = taps.shape[0]
    mixed_width = weight.shape[0]
    count = len(squares)

    def kernel(own_ref, near_ref, received_ref, state_ref, taps_ref, bias_ref, weight_ref, *refs):
        squares_refs, (conv_ref, gate_ref, mixing_ref) = refs[:count], refs[count:]
        pieces = received_ref[:, width:].astype(jnp.float32)
        for ref in squares_refs:
            pieces = pieces + ref[:, ref.shape[1] - LANES :].astype(jnp.float32)
        channels = (own_ref[...] + near_ref[...].astype(jnp.float32)) + received_ref[:, :width].astype(jnp.float32)
        squares = jnp.sum(pieces, axis=1, keepdims=True)
        channels = (channels * lax.rsqrt(squares / features + EPS)).astype(jnp.bfloat16)
        gate_ref[...] = channels[:, own_width:]
        window = jnp.concatenate(
            [state_ref[k].astype(jnp.float32) for k in range(taps_count - 1)]
            + [channels[:, :own_width].astype(jnp.float32)],
            axis=0,
        )
        total = bias_ref[...]
        for tap in range(taps_count):
            total = total + taps_ref[tap : tap + 1, :].astype(jnp.float32) * window[
                tap * requests : tap * requests + rows
            ]
        conv = (total * jax.nn.sigmoid(total)).astype(jnp.bfloat16)
        conv_ref[...] = conv
        mixing_ref[...] = lax.dot_general(
            conv, weight_ref[...], (((1,), (1,)), ((), ())), preferred_element_type=jnp.float32
        )

    return pl.pallas_call(
        kernel,
        out_shape=(
            jax.ShapeDtypeStruct((rows, own_width), jnp.bfloat16),
            jax.ShapeDtypeStruct((rows, own_width), jnp.bfloat16),
            jax.ShapeDtypeStruct((rows, mixed_width), jnp.float32),
        ),
        in_specs=whole(7 + count),
        out_specs=tuple(whole(3)),
        compiler_params=pltpu.CompilerParams(vmem_limit_bytes=8 * MIB),
        cost_estimate=cost(FLOPS_AHEAD//2),
    )(own, near, received, state, taps, bias, weight, *squares)


def scan_states(mixing, conv, gate, dt_weight, dt_bias, decay, skip, state):
    rows, own_width = conv.shape
    requests, state_width = state.shape[:2]
    low_width = dt_weight.shape[0]

    def kernel(mixing_ref, conv_ref, gate_ref, dt_ref, bias_ref, decay_ref, skip_ref, state_ref, *refs):
        gated_ref, next_ref, out = refs
        low = mixing_ref[:, :low_width]
        low_rank = (low * lax.rsqrt(jnp.mean(low * low, axis=1, keepdims=True) + EPS)).astype(jnp.bfloat16)
        step_size = jnp.dot(low_rank, dt_ref[...], preferred_element_type=jnp.float32) + bias_ref[...]
        step_size = jnp.maximum(step_size, 0.0) + jnp.log1p(jnp.exp(-jnp.abs(step_size)))
        mats = mixing_ref[:, low_width : low_width + 2 * state_width]
        lane = lax.broadcasted_iota(jnp.int32, mats.shape, 1)
        power = mats * mats
        first = jnp.sum(jnp.where(lane < state_width, power, 0.0), axis=1, keepdims=True)
        second = jnp.sum(jnp.where(lane < state_width, 0.0, power), axis=1, keepdims=True)
        mats = mats * lax.rsqrt(jnp.where(lane < state_width, first, second) / state_width + EPS)
        mats = jnp.concatenate([mats, jnp.zeros((rows, LANES - 2 * state_width), jnp.float32)], axis=1)
        turned = jnp.transpose(jnp.concatenate([mats, jnp.zeros((LANES - rows, LANES), jnp.float32)], axis=0))
        signal = conv_ref[...].astype(jnp.float32)
        drive = step_size * signal
        decay = decay_ref[...]
        for request in range(requests):
            memory = state_ref[request]
            for row in range(request, rows, requests):
                memory = (
                    jnp.exp(-step_size[row : row + 1] * decay) * memory
                    + drive[row : row + 1] * turned[:state_width, row : row + 1]
                )
                out[row : row + 1, :] = jnp.sum(
                    memory * turned[state_width : 2 * state_width, row : row + 1], axis=0, keepdims=True
                )
            next_ref[request] = memory
        gate = gate_ref[...].astype(jnp.float32)
        gated_ref[...] = ((out[...] + skip_ref[...] * signal) * (gate * jax.nn.sigmoid(gate))).astype(
            jnp.bfloat16
        )

    return pl.pallas_call(
        kernel,
        out_shape=(
            jax.ShapeDtypeStruct((rows, own_width), jnp.bfloat16),
            jax.ShapeDtypeStruct(state.shape, jnp.float32),
        ),
        in_specs=whole(8),
        out_specs=tuple(whole(2)),
        scratch_shapes=[pltpu.VMEM((rows, own_width), jnp.float32)],
        compiler_params=pltpu.CompilerParams(vmem_limit_bytes=8 * MIB),
        cost_estimate=cost(FLOPS_AHEAD//2),
    )(mixing, conv, gate, dt_weight, dt_bias, decay, skip, state)


def project_out(blocks, flips, weight, before):
    rows, own_width = blocks[0].shape
    width = weight.shape[1]
    count = len(blocks)
    tile = tile_of(width, 512)
    kind = jnp.float32 if before is None else jnp.bfloat16

    def kernel(*refs):
        block_refs, weight_ref, out_ref = refs[:count], refs[count], refs[-1]
        for start in range(0, width, tile):
            columns = slice(start, start + tile)
            total = None if before is None else refs[count + 1][:, columns]
            for ref, flip in zip(block_refs, flips):
                base = pl.multiple_of((hs_position() ^ flip) * own_width, own_width)
                term = jnp.dot(
                    ref[...], weight_ref[pl.ds(base, own_width), columns], preferred_element_type=jnp.float32
                )
                total = term if total is None else total + term
            out_ref[:, columns] = total.astype(kind)

    extra = () if before is None else (before,)
    return pl.pallas_call(
        kernel,
        out_shape=jax.ShapeDtypeStruct((rows, width), kind),
        in_specs=whole(count + 1 + len(extra)),
        out_specs=whole(1)[0],
        compiler_params=pltpu.CompilerParams(vmem_limit_bytes=4 * MIB),
        cost_estimate=cost(2 * rows * own_width * width * count),
    )(*blocks, weight, *extra)


def finish(residual, parts, requests):
    rows, width = residual.shape
    steps = rows // requests

    def kernel(residual_ref, *refs):
        part_refs, out_ref, total = refs[:-2], refs[-2], refs[-1]
        total[...] = residual_ref[...] + paired_sum([ref[...].astype(jnp.float32) for ref in part_refs])
        for request in range(requests):
            out_ref[request] = jnp.concatenate(
                [total[step * requests + request : step * requests + request + 1, :] for step in range(steps)],
                axis=0,
            ).astype(jnp.bfloat16)

    return pl.pallas_call(
        kernel,
        out_shape=jax.ShapeDtypeStruct((requests, steps, width), jnp.bfloat16),
        in_specs=whole(1 + len(parts)),
        out_specs=whole(1)[0],
        scratch_shapes=[pltpu.VMEM((rows, width), jnp.float32)],
        compiler_params=pltpu.CompilerParams(vmem_limit_bytes=4 * MIB),
        cost_estimate=cost(rows * width * 8),
    )(residual, *parts)


def plain_attention(query, key_new, value_new, kv_cache, kv_scale, context_len):
    requests, steps, heads, dim = query.shape
    kv_heads = key_new.shape[2]
    group = heads // kv_heads
    cache_len = kv_cache.shape[2]
    width = cache_len * kv_heads
    inv_root = 1.0 / math.sqrt(dim)
    first = lax.axis_index("seq") == 0
    flat_query = query.reshape(requests, steps * heads, dim)
    flat_cache = kv_cache.reshape(2, requests, width, dim)
    column = jnp.arange(width, dtype=jnp.int32)
    row = jnp.arange(steps * heads, dtype=jnp.int32)
    row_kv = (row % heads) // group
    same = row_kv[:, None] == (column % kv_heads)[None, :]
    place = lax.axis_index("seq") * cache_len + column // kv_heads
    live = same[None] & (place[None, :] < context_len[:, None])[:, None, :]
    spread = jnp.repeat(kv_scale.transpose(0, 1, 3, 2), BLOCK, axis=2).reshape(2, requests, width)
    scores = jnp.einsum("rqd,rpd->rqp", flat_query, flat_cache[0], preferred_element_type=jnp.float32)
    scores = jnp.where(live, scores * spread[0][:, None, :] * inv_root, -1e30)
    flat_new_k = key_new.reshape(requests, steps * kv_heads, dim)
    flat_new_v = value_new.reshape(requests, steps * kv_heads, dim)
    new_column = jnp.arange(steps * kv_heads, dtype=jnp.int32)
    new_live = (
        (row_kv[:, None] == (new_column % kv_heads)[None, :])
        & ((new_column // kv_heads)[None, :] <= (row // heads)[:, None])
        & first
    )[None]
    recent = jnp.einsum("rqd,rjd->rqj", flat_query, flat_new_k, preferred_element_type=jnp.float32)
    recent = jnp.where(new_live, recent * inv_root, -1e30)
    top = jnp.maximum(jnp.max(scores, axis=-1), jnp.max(recent, axis=-1))
    weight = jnp.where(live, jnp.exp(scores - top[..., None]), 0.0)
    new_weight = jnp.where(new_live, jnp.exp(recent - top[..., None]), 0.0)
    total = jnp.sum(weight, axis=-1) + jnp.sum(new_weight, axis=-1)
    scaled = (weight * spread[1][:, None, :]).astype(jnp.bfloat16)
    mix = jnp.einsum("rqp,rpd->rqd", scaled, flat_cache[1], preferred_element_type=jnp.float32)
    mix = mix + jnp.einsum(
        "rqj,rjd->rqd", new_weight.astype(jnp.bfloat16), flat_new_v, preferred_element_type=jnp.float32
    )
    rows = requests * steps
    return mix.reshape(rows, heads, dim), top.reshape(rows, heads), total.reshape(rows, heads)


def merge(mixes, tops, totals):
    best = tops[0]
    for top in tops[1:]:
        best = jnp.maximum(best, top)
    factors = [jnp.exp(top - best) for top in tops]
    summed = paired_sum([total * factor for total, factor in zip(totals, factors)])
    mixed = paired_sum(
        [mix.astype(jnp.float32) * factor[..., None] for mix, factor in zip(mixes, factors)]
    )
    return (mixed / summed[..., None]).astype(jnp.bfloat16)


def plain(
    hidden,
    query,
    key_new,
    value_new,
    kv_cache,
    kv_scale,
    context_len,
    attn_out_weight,
    norm_gain,
    in_weight,
    conv_weight,
    conv_bias,
    conv_state,
    xproj_weight,
    dt_weight,
    dt_bias,
    decay_rate,
    skip_gain,
    ssm_state,
    mamba_out_weight,
):
    requests, steps = hidden.shape[:2]
    rows = requests * steps
    seq_count = lax.axis_size("seq")
    hs_count = lax.axis_size(HS)
    hs_index = lax.axis_index(HS)
    heads = query.shape[2]
    dim = query.shape[3]
    mix, top, total = plain_attention(query, key_new, value_new, kv_cache, kv_scale, context_len)
    mixes, tops, totals = (lax.all_gather(part, "seq") for part in (mix, top, total))
    every = range(seq_count)
    own_heads = merge([mixes[k] for k in every], [tops[k] for k in every], [totals[k] for k in every])
    every_head = lax.all_gather(own_heads.reshape(rows, heads * dim), HS, axis=1, tiled=True)
    width_in = attn_out_weight.shape[0]
    chosen = lax.dynamic_slice_in_dim(every_head, lax.axis_index("seq") * width_in, width_in, 1)
    attended = sum_over(
        jnp.dot(chosen, attn_out_weight, preferred_element_type=jnp.float32), "seq", jnp.bfloat16
    )
    residual = hidden.astype(jnp.float32).reshape(rows, -1) + attended
    features = residual.shape[1] * hs_count
    squares = jnp.sum(residual * residual, axis=-1, keepdims=True)
    gained = (residual * norm_gain).astype(jnp.bfloat16)
    projected = jnp.einsum("nd,cde->nce", gained, in_weight, preferred_element_type=jnp.float32)
    own_width = conv_weight.shape[0]
    upper, lower = split_pair(squares)

    def block_for(index):
        block = lax.dynamic_slice_in_dim(projected, index * own_width, own_width, 2)
        return block.reshape(rows, 2 * own_width)

    channels = block_for(hs_index)
    for hop in range(1, hs_count):
        block = jnp.concatenate([block_for((hs_index + hop) % hs_count), upper, lower], axis=1)
        part = shifted(block.astype(jnp.bfloat16), HS, hop).astype(jnp.float32)
        channels = channels + part[:, : 2 * own_width]
        squares = squares + part[:, 2 * own_width : 2 * own_width + 1] + part[:, 2 * own_width + 1 :]
    channels = channels * lax.rsqrt(squares / features + EPS)
    conv_in = channels[:, :own_width].astype(jnp.bfloat16)
    gate_in = channels[:, own_width:].astype(jnp.bfloat16)
    window = jnp.concatenate(
        [
            conv_state.astype(jnp.float32),
            conv_in.astype(jnp.float32).reshape(requests, steps, own_width),
        ],
        axis=1,
    )
    conv_sum = jnp.zeros((requests, steps, own_width), jnp.float32) + conv_bias
    for tap in range(conv_weight.shape[1]):
        conv_sum = conv_sum + conv_weight[:, tap].astype(jnp.float32) * window[:, tap : tap + steps, :]
    conv_out = jax.nn.silu(conv_sum).astype(jnp.bfloat16).reshape(rows, own_width)
    mixing = jnp.dot(conv_out, xproj_weight, preferred_element_type=jnp.float32)
    mixing = sum_over(sum_over(mixing, HS), "seq")
    low_width = dt_weight.shape[0]
    state_width = decay_rate.shape[1]
    low_rank = rms_unit(mixing[:, :low_width]).astype(jnp.bfloat16)
    input_mat = rms_unit(mixing[:, low_width : low_width + state_width]).reshape(
        requests, steps, state_width
    )
    output_mat = rms_unit(mixing[:, low_width + state_width :]).reshape(requests, steps, state_width)
    delta = jax.nn.softplus(
        jnp.dot(low_rank, dt_weight, preferred_element_type=jnp.float32) + dt_bias
    ).reshape(requests, steps, own_width)
    signal = conv_out.astype(jnp.float32).reshape(requests, steps, own_width)
    memory = ssm_state
    outputs = []
    for moment in range(steps):
        step_now = delta[:, moment]
        memory = (
            jnp.exp(-step_now[..., None] * decay_rate) * memory
            + (step_now * signal[:, moment])[..., None] * input_mat[:, moment][:, None, :]
        )
        outputs.append(
            jnp.sum(memory * output_mat[:, moment][:, None, :], axis=-1)
            + skip_gain * signal[:, moment]
        )
    stacked = jnp.stack(outputs, axis=1).reshape(rows, own_width)
    gated_out = (stacked * jax.nn.silu(gate_in.astype(jnp.float32))).astype(jnp.bfloat16)
    gated_block = lax.all_gather(gated_out, HS, axis=1, tiled=True)
    mamba_part = sum_over(
        jnp.dot(gated_block, mamba_out_weight, preferred_element_type=jnp.float32), "seq", jnp.bfloat16
    )
    final = (residual + mamba_part).astype(jnp.bfloat16).reshape(requests, steps, -1)
    return (final, memory)


def local(
    hidden,
    query,
    key_new,
    value_new,
    kv_cache,
    kv_scale,
    context_len,
    attn_out_weight,
    norm_gain,
    in_weight,
    conv_weight,
    conv_bias,
    conv_state,
    xproj_weight,
    dt_weight,
    dt_bias,
    decay_rate,
    skip_gain,
    ssm_state,
    mamba_out_weight,
):
    requests, steps = hidden.shape[:2]
    rows = requests * steps
    seq_count = lax.axis_size("seq")
    hs_count = lax.axis_size(HS)
    heads, dim = query.shape[2:]
    own_width = conv_weight.shape[0]
    if (
        lax.axis_size("head") != 2
        or lax.axis_size("sub") != 2
        or seq_count != hs_count
        or own_width % LANES
        or dim != LANES
        or (rows * heads) % LANES
        or rows % 16
    ):
        return plain(
            hidden,
            query,
            key_new,
            value_new,
            kv_cache,
            kv_scale,
            context_len,
            attn_out_weight,
            norm_gain,
            in_weight,
            conv_weight,
            conv_bias,
            conv_state,
            xproj_weight,
            dt_weight,
            dt_bias,
            decay_rate,
            skip_gain,
            ssm_state,
            mamba_out_weight,
        )
    part, out_rows = attention(
        query, key_new, value_new, kv_cache, kv_scale, context_len, [whole_job(attn_out_weight)]
    )
    columns = lambda flip: block_job(in_weight, own_width, flip)
    far_columns, chip_columns = bring([columns(3), columns(2)], part)
    place = range(hs_count)
    parts = [
        lax.ppermute(
            part,
            ("seq",) + HS,
            [
                (s * hs_count + j, j * hs_count + ((s // 2 + turn) % 2) * 2 + s % 2)
                for s in range(seq_count)
                for j in place
            ],
        )
        for turn in range(2)
    ]
    parts, far_columns, chip_columns = lax.optimization_barrier((parts, far_columns, chip_columns))
    parts = parts + [crossed(arrived, "sub", 1) for arrived in parts]
    partial = merge_project(parts, out_rows, rows, heads, dim)
    core_columns, own_columns = bring([columns(1), columns(0)], partial)
    terms, core_columns, own_columns = lax.optimization_barrier(
        (crossed_all(partial, "seq"), core_columns, own_columns)
    )
    residual, gained, stats = add_residual(hidden, terms, norm_gain)
    features = residual.shape[1] * hs_count
    for_far = crossed(project_block(gained, far_columns, own_width, jnp.bfloat16, stats), "sub", 1)
    block = relay(project_block(gained, chip_columns, own_width, jnp.float32, None), for_far, stats)
    received = crossed(block, "head", 1)
    late, block = lax.optimization_barrier((gained, block))
    near = crossed(project_block(late, core_columns, own_width, jnp.bfloat16, None), "sub", 1)
    own = project_block(late, own_columns, own_width, jnp.float32, None)
    conv, gate, mixing = convolve(
        own,
        near,
        received,
        [stats, for_far],
        conv_state.transpose(1, 0, 2),
        conv_weight.T,
        conv_bias.reshape(1, -1),
        xproj_weight.T,
        features,
    )
    mixing = mixing + crossed(mixing, "sub", 1)
    base = lambda s, x, c: s * hs_count + x * 2 + c
    arrived = [
        lax.ppermute(
            mixing,
            ("seq",) + HS,
            [(base(s, x, 1), base(s ^ flip, x ^ 1, 1)) for s in range(seq_count) for x in range(2)]
            + [(base(s, x, 0), base(s ^ flip, x, 0)) for s in range(seq_count) for x in range(2) if flip],
        )
        for flip in range(seq_count - 1, -1, -1)
    ]
    line = jnp.where(lax.axis_index("sub") == 0, mixing, 0.0) + paired_sum(arrived)
    mixing = line + crossed(line, "sub", 1)
    gated, state = scan_states(
        mixing,
        conv,
        gate,
        dt_weight,
        dt_bias.reshape(1, -1),
        decay_rate.T,
        skip_gain.reshape(1, -1),
        ssm_state.transpose(0, 2, 1),
    )
    first = project_out([gated], [0], mamba_out_weight, None)
    blocks, first = lax.optimization_barrier((crossed_all(gated, HS), first))
    partial = project_out(blocks[1:], list(place)[1:], mamba_out_weight, first)
    final = finish(residual, crossed_all(partial, "seq"), requests)
    return final, state.transpose(0, 2, 1)


def solution(mesh):
    return jax.shard_map(
        local,
        mesh=mesh,
        in_specs=(
            P("groups", None, HS),
            P("groups", None, HS, None),
            P("groups", None, HS, None),
            P("groups", None, HS, None),
            P(None, "groups", "seq", HS, None),
            P(None, "groups", HS, "seq"),
            P("groups"),
            P("seq", HS),
            P(HS),
            P(None, HS, "seq"),
            P(("seq",) + HS, None),
            P(("seq",) + HS),
            P("groups", None, ("seq",) + HS),
            P(("seq",) + HS, None),
            P(None, ("seq",) + HS),
            P(("seq",) + HS),
            P(("seq",) + HS, None),
            P(("seq",) + HS),
            P("groups", ("seq",) + HS, None),
            P("seq", HS),
        ),
        out_specs=(P("groups", None, HS), P("groups", ("seq",) + HS, None)),
        check_vma=False,
    )
```

```python
import math

import jax
import jax.numpy as jnp
from jax import lax
from jax.experimental import pallas as pl
from jax.experimental.pallas import tpu as pltpu
from jax.sharding import PartitionSpec as P

BLOCK = 128
EPS = 1e-06
HS = ("head", "sub")
DIRECT = 8
LANES = 128
MIB = 1024 * 1024
PIECES = 4
FLOPS_AHEAD = 20_000_000_000


def shifted(value, axes, hop):
    count = lax.axis_size(axes)
    return lax.ppermute(value, axes, [(i, (i + hop) % count) for i in range(count)])


def paired_sum(terms):
    if len(terms) == 1:
        return terms[0]
    return paired_sum(terms[::2]) + paired_sum(terms[1::2])


def crossed(value, axes, flip):
    return lax.ppermute(value, axes, [(i, i ^ flip) for i in range(lax.axis_size(axes))])


def crossed_all(value, axes):
    count = lax.axis_size(axes)
    far_first = {flip: crossed(value, axes, flip) for flip in range(count - 1, 0, -1)}
    return [value] + [far_first[flip] for flip in range(1, count)]


def everyone(value, axes):
    return [value] + [shifted(value, axes, hop) for hop in range(1, lax.axis_size(axes))]


def sum_over(value, axes, kind=None):
    if lax.axis_size(axes) > DIRECT:
        return lax.psum(value, axes)
    if kind is not None:
        value = lax.optimization_barrier(value.astype(kind))
    return paired_sum([part.astype(jnp.float32) for part in everyone(value, axes)])


def split_pair(value):
    upper = lax.reduce_precision(value, 8, 7)
    return upper, lax.reduce_precision(value - upper, 8, 7)


def rms_unit(values):
    return values * lax.rsqrt(jnp.mean(values * values, axis=-1, keepdims=True) + EPS)


def tile_of(width, limit):
    tile = width
    while tile > limit and tile % 2 == 0 and (tile // 2) % 128 == 0:
        tile //= 2
    return tile


def whole(count):
    return [pl.BlockSpec(memory_space=pltpu.VMEM)] * count


def in_pieces(source, target):
    rows = target.shape[0] // PIECES
    return [(source.at[k * rows : (k + 1) * rows], target.at[k * rows : (k + 1) * rows]) for k in range(PIECES)]


def hs_position():
    return lax.axis_index("head") * lax.axis_size("sub") + lax.axis_index("sub")


def whole_job(weight):
    return weight, weight.shape, in_pieces, PIECES


def block_job(weight, own_width, flip):
    def views(source, target):
        columns = pl.ds(pl.multiple_of((hs_position() ^ flip) * own_width, own_width), own_width)
        return [
            pair for part in range(2) for pair in in_pieces(source.at[part, :, columns], target.at[part])
        ]

    return weight, (2, weight.shape[1], own_width), views, 2 * PIECES


def job_shapes(jobs):
    return [pltpu.VMEM(job[1], job[0].dtype) for job in jobs]


def job_inputs(jobs):
    return [pltpu.with_memory_space_constraint(job[0], pltpu.HBM) for job in jobs]


def job_bytes(jobs):
    return sum(2 * math.prod(job[1]) * job[0].dtype.itemsize for job in jobs)


def job_sems(jobs):
    count = sum(job[3] for job in jobs)
    return [pltpu.SemaphoreType.DMA((count,))] if jobs else []


def start_jobs(jobs, sources, targets, ready):
    pairs = []
    for job, source, target in zip(jobs, sources, targets):
        pairs += job[2](source, target)
    copies = [pltpu.make_async_copy(source, target, ready.at[k]) for k, (source, target) in enumerate(pairs)]
    for copy in copies:
        copy.start()
    return copies


def anywhere(count):
    return [pl.BlockSpec(memory_space=pl.ANY)] * count


def bring(jobs, after):
    count = len(jobs)

    def kernel(*refs):
        for copy in start_jobs(jobs, refs[:count], refs[count + 1 : -1], refs[-1]):
            copy.wait()

    return pl.pallas_call(
        kernel,
        out_shape=tuple(job_shapes(jobs)),
        in_specs=anywhere(count + 1),
        out_specs=tuple(whole(count)),
        scratch_shapes=job_sems(jobs),
        compiler_params=pltpu.CompilerParams(vmem_limit_bytes=2 * MIB),
        cost_estimate=pl.CostEstimate(flops=0, bytes_accessed=job_bytes(jobs), transcendentals=0),
    )(*job_inputs(jobs), after)


def attention(query, key_new, value_new, kv_cache, kv_scale, context_len, jobs):
    requests, steps, heads, dim = query.shape
    kv_heads = key_new.shape[2]
    group = heads // kv_heads
    cache_len = kv_cache.shape[2]
    width = cache_len * kv_heads
    blocks = kv_scale.shape[3]
    inv_root = 1.0 / math.sqrt(dim)
    lines = steps * heads
    total_rows = requests * lines
    news = steps * kv_heads

    def kernel(*refs):
        count = len(jobs)
        sources, job_sources, refs = refs[:6], refs[6 : 6 + count], refs[6 + count :]
        out_ref, targets, held, ready = refs[0], refs[1 : 1 + count], refs[1 + count : 7 + count], refs[7 + count]
        length_ref, scale_ref, query_ref, key_ref, value_ref, cache_ref = held
        copies = [
            pltpu.make_async_copy(sources[k], held[k], ready.at[k]) for k in range(5)
        ] + [
            pltpu.make_async_copy(sources[5].at[:, k], cache_ref.at[:, k], ready.at[5 + k])
            for k in range(requests)
        ]
        for copy in copies:
            copy.start()
        job_copies = start_jobs(jobs, job_sources, targets, refs[-1])
        shard = lax.axis_index("seq")
        row = lax.broadcasted_iota(jnp.int32, (lines, width), 0)
        column = lax.broadcasted_iota(jnp.int32, (lines, width), 1)
        same = (row % heads) // group == column % kv_heads
        place = shard * cache_len + column // kv_heads
        new_row = lax.broadcasted_iota(jnp.int32, (lines, news), 0)
        new_column = lax.broadcasted_iota(jnp.int32, (lines, news), 1)
        new_live = (
            ((new_row % heads) // group == new_column % kv_heads)
            & (new_column // kv_heads <= new_row // heads)
            & (shard == 0)
        )
        parity = lax.broadcasted_iota(jnp.int32, (1, kv_heads * BLOCK), 1) % kv_heads

        def spread(which, request):
            pieces = []
            for block in range(blocks):
                piece = jnp.zeros((1, kv_heads * BLOCK), jnp.float32)
                for head in range(kv_heads):
                    piece = jnp.where(
                        parity == head, scale_ref[which, head, block : block + 1, request : request + 1], piece
                    )
                pieces.append(piece)
            return jnp.concatenate(pieces, axis=1)

        tops, totals = [], []
        for copy in copies[:5]:
            copy.wait()
        for request in range(requests):
            asked = query_ref[request]
            live = same & (place < length_ref[:, request : request + 1])
            copies[5 + request].wait()
            scores = lax.dot_general(
                asked, cache_ref[0, request], (((1,), (1,)), ((), ())), preferred_element_type=jnp.float32
            )
            scores = jnp.where(live, scores * spread(0, request) * inv_root, -1e30)
            recent = lax.dot_general(
                asked, key_ref[request], (((1,), (1,)), ((), ())), preferred_element_type=jnp.float32
            )
            recent = jnp.where(new_live, recent * inv_root, -1e30)
            top = jnp.maximum(
                jnp.max(scores, axis=1, keepdims=True), jnp.max(recent, axis=1, keepdims=True)
            )
            weight = jnp.where(live, jnp.exp(scores - top), 0.0)
            new_weight = jnp.where(new_live, jnp.exp(recent - top), 0.0)
            total = jnp.sum(weight, axis=1, keepdims=True) + jnp.sum(new_weight, axis=1, keepdims=True)
            mix = jnp.dot(
                (weight * spread(1, request)).astype(jnp.bfloat16),
                cache_ref[1, request],
                preferred_element_type=jnp.float32,
            ) + jnp.dot(
                new_weight.astype(jnp.bfloat16), value_ref[request], preferred_element_type=jnp.float32
            )
            for step in range(steps):
                start = (step * requests + request) * heads
                out_ref[start : start + heads, :] = mix[step * heads : (step + 1) * heads].astype(jnp.bfloat16)
            tops.append(top)
            totals.append(total)

        def by_step(values):
            return jnp.concatenate(
                [value[step * heads : (step + 1) * heads] for step in range(steps) for value in values], axis=0
            )

        lane = lax.broadcasted_iota(jnp.int32, (total_rows, LANES), 1)
        table = jnp.zeros((total_rows, LANES), jnp.float32)
        for start, value in ((0, by_step(tops)), (3, by_step(totals))):
            for k in range(3):
                piece = value.astype(jnp.bfloat16).astype(jnp.float32)
                table = jnp.where(lane == start + k, piece, table)
                value = value - piece
        turned = jnp.transpose(table)[:8]
        out_ref[total_rows:, :] = jnp.concatenate(
            [turned[:, k * LANES : (k + 1) * LANES] for k in range(total_rows // LANES)], axis=0
        ).astype(jnp.bfloat16)
        for copy in job_copies:
            copy.wait()

    given_all = (
        context_len.reshape(1, requests),
        kv_scale.transpose(0, 2, 3, 1),
        query.reshape(requests, lines, dim),
        key_new.reshape(requests, news, dim),
        value_new.reshape(requests, news, dim),
        kv_cache.reshape(2, requests, width, dim),
    )
    return pl.pallas_call(
        kernel,
        out_shape=tuple(
            [jax.ShapeDtypeStruct((total_rows + total_rows // 16, dim), jnp.bfloat16)] + job_shapes(jobs)
        ),
        in_specs=anywhere(6 + len(jobs)),
        out_specs=tuple(whole(1 + len(jobs))),
        scratch_shapes=[pltpu.VMEM(given.shape, given.dtype) for given in given_all]
        + [pltpu.SemaphoreType.DMA((5 + requests,))]
        + job_sems(jobs),
        compiler_params=pltpu.CompilerParams(vmem_limit_bytes=8 * MIB),
        cost_estimate=cost(1_000_000_000),
    )(*[pltpu.with_memory_space_constraint(given, pltpu.HBM) for given in given_all], *job_inputs(jobs))


def cost(flops):
    return pl.CostEstimate(flops=flops, bytes_accessed=0, transcendentals=0)


def merge_project(parts, weight, rows, heads, dim):
    lines = rows * heads
    count = len(parts)
    depth, width = weight.shape
    tile = tile_of(width, 512)

    def kernel(*refs):
        part_refs, weight_ref, out_ref, mixed, chosen = refs[:count], refs[count], refs[-3], refs[-2], refs[-1]
        tops, totals = [], []
        for ref in part_refs:
            stats = ref[lines:, :].astype(jnp.float32)
            wide = jnp.concatenate([stats[k * 8 : (k + 1) * 8] for k in range(lines // LANES)], axis=1)
            table = jnp.transpose(jnp.concatenate([wide, jnp.zeros((LANES - 8, lines), jnp.float32)], axis=0))
            tops.append(table[:, 0:1] + table[:, 1:2] + table[:, 2:3])
            totals.append(table[:, 3:4] + table[:, 4:5] + table[:, 5:6])
        best = tops[0]
        for top in tops[1:]:
            best = jnp.maximum(best, top)
        factors = [jnp.exp(top - best) for top in tops]
        summed = paired_sum([total * factor for total, factor in zip(totals, factors)])
        mixed[...] = (
            paired_sum([ref[:lines, :].astype(jnp.float32) * factor for ref, factor in zip(part_refs, factors)])
            / summed
        )
        for head in range(heads):
            chosen[:, head * dim : (head + 1) * dim] = mixed[pl.ds(head, rows, stride=heads), :].astype(
                jnp.bfloat16
            )
        for start in range(0, width, tile):
            out_ref[:, start : start + tile] = jnp.dot(
                chosen[...], weight_ref[:, start : start + tile], preferred_element_type=jnp.float32
            ).astype(out_ref.dtype)

    return pl.pallas_call(
        kernel,
        out_shape=jax.ShapeDtypeStruct((rows, width), jnp.bfloat16),
        in_specs=whole(count + 1),
        out_specs=whole(1)[0],
        scratch_shapes=[pltpu.VMEM((lines, dim), jnp.float32), pltpu.VMEM((rows, heads * dim), jnp.bfloat16)],
        compiler_params=pltpu.CompilerParams(vmem_limit_bytes=4 * MIB),
        cost_estimate=cost(FLOPS_AHEAD),
    )(*parts, weight)


def in_three(left):
    rows = left.shape[0]
    lane = lax.broadcasted_iota(jnp.int32, (rows, LANES), 1)
    table = jnp.zeros((rows, LANES), jnp.float32)
    for k in range(3):
        piece = left.astype(jnp.bfloat16).astype(jnp.float32)
        table = jnp.where(lane == k, piece, table)
        left = left - piece
    return table.astype(jnp.bfloat16)


def add_residual(hidden, parts, gain):
    requests, steps, width = hidden.shape
    rows = requests * steps

    def kernel(hidden_ref, gain_ref, *refs):
        part_refs, (residual_ref, gained_ref, stats_ref) = refs[:-3], refs[-3:]
        wide = [hidden_ref[request].astype(jnp.float32) for request in range(requests)]
        by_step = jnp.concatenate([part[step : step + 1] for step in range(steps) for part in wide], axis=0)
        residual = by_step + paired_sum(
            [ref[...].astype(jnp.float32) for ref in part_refs]
        )
        residual_ref[...] = residual
        gained_ref[...] = (residual * gain_ref[...]).astype(jnp.bfloat16)
        stats_ref[...] = in_three(jnp.sum(residual * residual, axis=1, keepdims=True))

    return pl.pallas_call(
        kernel,
        out_shape=(
            jax.ShapeDtypeStruct((rows, width), jnp.float32),
            jax.ShapeDtypeStruct((rows, width), jnp.bfloat16),
            jax.ShapeDtypeStruct((rows, LANES), jnp.bfloat16),
        ),
        in_specs=whole(2 + len(parts)),
        out_specs=tuple(whole(3)),
        compiler_params=pltpu.CompilerParams(vmem_limit_bytes=4 * MIB),
        cost_estimate=cost(rows * width * 8),
    )(hidden, gain.reshape(1, width), *parts)


def project_block(gained, weight, own_width, kind, stats):
    rows, depth = gained.shape
    width = 2 * own_width
    tile = tile_of(own_width, 512)
    riders = () if stats is None else (stats,)

    def kernel(gained_ref, weight_ref, *refs):
        out_ref = refs[-1]
        for part in range(2):
            for start in range(0, own_width, tile):
                out_ref[:, part * own_width + start : part * own_width + start + tile] = jnp.dot(
                    gained_ref[...], weight_ref[part, :, start : start + tile], preferred_element_type=jnp.float32
                ).astype(kind)
        if riders:
            out_ref[:, width:] = refs[0][...]

    return pl.pallas_call(
        kernel,
        out_shape=jax.ShapeDtypeStruct((rows, width + (LANES if riders else 0)), kind),
        in_specs=whole(2 + len(riders)),
        out_specs=whole(1)[0],
        compiler_params=pltpu.CompilerParams(vmem_limit_bytes=4 * MIB),
        cost_estimate=cost(2 * rows * depth * width),
    )(gained, weight, *riders)


def relay(block, arrived, stats):
    rows, width = block.shape

    def kernel(block_ref, arrived_ref, stats_ref, out_ref):
        out_ref[:, :width] = (block_ref[...] + arrived_ref[:, :width].astype(jnp.float32)).astype(jnp.bfloat16)
        both = stats_ref[...].astype(jnp.float32) + arrived_ref[:, width:].astype(jnp.float32)
        out_ref[:, width:] = in_three(jnp.sum(both, axis=1, keepdims=True))

    return pl.pallas_call(
        kernel,
        out_shape=jax.ShapeDtypeStruct((rows, width + LANES), jnp.bfloat16),
        in_specs=whole(3),
        out_specs=whole(1)[0],
        compiler_params=pltpu.CompilerParams(vmem_limit_bytes=4 * MIB),
        cost_estimate=cost(rows * width * 8),
    )(block, arrived, stats)


def convolve(own, near, received, squares, state, taps, bias, weight, features):
    rows, width = own.shape
    own_width = width // 2
    requests = state.shape[1]
    taps_count = taps.shape[0]
    mixed_width = weight.shape[0]
    count = len(squares)

    def kernel(own_ref, near_ref, received_ref, state_ref, taps_ref, bias_ref, weight_ref, *refs):
        squares_refs, (conv_ref, gate_ref, mixing_ref) = refs[:count], refs[count:]
        pieces = received_ref[:, width:].astype(jnp.float32)
        for ref in squares_refs:
            pieces = pieces + ref[:, ref.shape[1] - LANES :].astype(jnp.float32)
        channels = (own_ref[...] + near_ref[...].astype(jnp.float32)) + received_ref[:, :width].astype(jnp.float32)
        squares = jnp.sum(pieces, axis=1, keepdims=True)
        channels = (channels * lax.rsqrt(squares / features + EPS)).astype(jnp.bfloat16)
        gate_ref[...] = channels[:, own_width:]
        window = jnp.concatenate(
            [state_ref[k].astype(jnp.float32) for k in range(taps_count - 1)]
            + [channels[:, :own_width].astype(jnp.float32)],
            axis=0,
        )
        total = bias_ref[...]
        for tap in range(taps_count):
            total = total + taps_ref[tap : tap + 1, :].astype(jnp.float32) * window[
                tap * requests : tap * requests + rows
            ]
        conv = (total * jax.nn.sigmoid(total)).astype(jnp.bfloat16)
        conv_ref[...] = conv
        mixing_ref[...] = lax.dot_general(
            conv, weight_ref[...], (((1,), (1,)), ((), ())), preferred_element_type=jnp.float32
        )

    return pl.pallas_call(
        kernel,
        out_shape=(
            jax.ShapeDtypeStruct((rows, own_width), jnp.bfloat16),
            jax.ShapeDtypeStruct((rows, own_width), jnp.bfloat16),
            jax.ShapeDtypeStruct((rows, mixed_width), jnp.float32),
        ),
        in_specs=whole(7 + count),
        out_specs=tuple(whole(3)),
        compiler_params=pltpu.CompilerParams(vmem_limit_bytes=8 * MIB),
        cost_estimate=cost(FLOPS_AHEAD//2),
    )(own, near, received, state, taps, bias, weight, *squares)


def scan_states(mixing, conv, gate, dt_weight, dt_bias, decay, skip, state):
    rows, own_width = conv.shape
    requests, state_width = state.shape[:2]
    low_width = dt_weight.shape[0]

    def kernel(mixing_ref, conv_ref, gate_ref, dt_ref, bias_ref, decay_ref, skip_ref, state_ref, *refs):
        gated_ref, next_ref, out = refs
        low = mixing_ref[:, :low_width]
        low_rank = (low * lax.rsqrt(jnp.mean(low * low, axis=1, keepdims=True) + EPS)).astype(jnp.bfloat16)
        step_size = jnp.dot(low_rank, dt_ref[...], preferred_element_type=jnp.float32) + bias_ref[...]
        step_size = jnp.maximum(step_size, 0.0) + jnp.log1p(jnp.exp(-jnp.abs(step_size)))
        mats = mixing_ref[:, low_width : low_width + 2 * state_width]
        lane = lax.broadcasted_iota(jnp.int32, mats.shape, 1)
        power = mats * mats
        first = jnp.sum(jnp.where(lane < state_width, power, 0.0), axis=1, keepdims=True)
        second = jnp.sum(jnp.where(lane < state_width, 0.0, power), axis=1, keepdims=True)
        mats = mats * lax.rsqrt(jnp.where(lane < state_width, first, second) / state_width + EPS)
        mats = jnp.concatenate([mats, jnp.zeros((rows, LANES - 2 * state_width), jnp.float32)], axis=1)
        turned = jnp.transpose(jnp.concatenate([mats, jnp.zeros((LANES - rows, LANES), jnp.float32)], axis=0))
        signal = conv_ref[...].astype(jnp.float32)
        drive = step_size * signal
        decay = decay_ref[...]
        for request in range(requests):
            memory = state_ref[request]
            for row in range(request, rows, requests):
                memory = (
                    jnp.exp(-step_size[row : row + 1] * decay) * memory
                    + drive[row : row + 1] * turned[:state_width, row : row + 1]
                )
                out[row : row + 1, :] = jnp.sum(
                    memory * turned[state_width : 2 * state_width, row : row + 1], axis=0, keepdims=True
                )
            next_ref[request] = memory
        gate = gate_ref[...].astype(jnp.float32)
        gated_ref[...] = ((out[...] + skip_ref[...] * signal) * (gate * jax.nn.sigmoid(gate))).astype(
            jnp.bfloat16
        )

    return pl.pallas_call(
        kernel,
        out_shape=(
            jax.ShapeDtypeStruct((rows, own_width), jnp.bfloat16),
            jax.ShapeDtypeStruct(state.shape, jnp.float32),
        ),
        in_specs=whole(8),
        out_specs=tuple(whole(2)),
        scratch_shapes=[pltpu.VMEM((rows, own_width), jnp.float32)],
        compiler_params=pltpu.CompilerParams(vmem_limit_bytes=8 * MIB),
        cost_estimate=cost(FLOPS_AHEAD//4),
    )(mixing, conv, gate, dt_weight, dt_bias, decay, skip, state)


def add_up(terms, flops):
    def kernel(*refs):
        total = refs[0][...]
        for ref in refs[1:-1]:
            total = total + ref[...]
        refs[-1][...] = total

    return pl.pallas_call(
        kernel,
        out_shape=jax.ShapeDtypeStruct(terms[0].shape, terms[0].dtype),
        in_specs=whole(len(terms)),
        out_specs=whole(1)[0],
        compiler_params=pltpu.CompilerParams(vmem_limit_bytes=4 * MIB),
        cost_estimate=cost(flops),
    )(*terms)


def project_out(blocks, flips, weight, before):
    rows, own_width = blocks[0].shape
    width = weight.shape[1]
    count = len(blocks)
    tile = tile_of(width, 512)
    kind = jnp.float32 if before is None else jnp.bfloat16

    def kernel(*refs):
        block_refs, weight_ref, out_ref = refs[:count], refs[count], refs[-1]
        for start in range(0, width, tile):
            columns = slice(start, start + tile)
            total = None if before is None else refs[count + 1][:, columns]
            for ref, flip in zip(block_refs, flips):
                base = pl.multiple_of((hs_position() ^ flip) * own_width, own_width)
                term = jnp.dot(
                    ref[...], weight_ref[pl.ds(base, own_width), columns], preferred_element_type=jnp.float32
                )
                total = term if total is None else total + term
            out_ref[:, columns] = total.astype(kind)

    extra = () if before is None else (before,)
    return pl.pallas_call(
        kernel,
        out_shape=jax.ShapeDtypeStruct((rows, width), kind),
        in_specs=whole(count + 1 + len(extra)),
        out_specs=whole(1)[0],
        compiler_params=pltpu.CompilerParams(vmem_limit_bytes=4 * MIB),
        cost_estimate=cost(2 * rows * own_width * width * count),
    )(*blocks, weight, *extra)


def finish(residual, parts, requests):
    rows, width = residual.shape
    steps = rows // requests

    def kernel(residual_ref, *refs):
        part_refs, out_ref, total = refs[:-2], refs[-2], refs[-1]
        total[...] = residual_ref[...] + paired_sum([ref[...].astype(jnp.float32) for ref in part_refs])
        for request in range(requests):
            out_ref[request] = jnp.concatenate(
                [total[step * requests + request : step * requests + request + 1, :] for step in range(steps)],
                axis=0,
            ).astype(jnp.bfloat16)

    return pl.pallas_call(
        kernel,
        out_shape=jax.ShapeDtypeStruct((requests, steps, width), jnp.bfloat16),
        in_specs=whole(1 + len(parts)),
        out_specs=whole(1)[0],
        scratch_shapes=[pltpu.VMEM((rows, width), jnp.float32)],
        compiler_params=pltpu.CompilerParams(vmem_limit_bytes=4 * MIB),
        cost_estimate=cost(rows * width * 8),
    )(residual, *parts)


def plain_attention(query, key_new, value_new, kv_cache, kv_scale, context_len):
    requests, steps, heads, dim = query.shape
    kv_heads = key_new.shape[2]
    group = heads // kv_heads
    cache_len = kv_cache.shape[2]
    width = cache_len * kv_heads
    inv_root = 1.0 / math.sqrt(dim)
    first = lax.axis_index("seq") == 0
    flat_query = query.reshape(requests, steps * heads, dim)
    flat_cache = kv_cache.reshape(2, requests, width, dim)
    column = jnp.arange(width, dtype=jnp.int32)
    row = jnp.arange(steps * heads, dtype=jnp.int32)
    row_kv = (row % heads) // group
    same = row_kv[:, None] == (column % kv_heads)[None, :]
    place = lax.axis_index("seq") * cache_len + column // kv_heads
    live = same[None] & (place[None, :] < context_len[:, None])[:, None, :]
    spread = jnp.repeat(kv_scale.transpose(0, 1, 3, 2), BLOCK, axis=2).reshape(2, requests, width)
    scores = jnp.einsum("rqd,rpd->rqp", flat_query, flat_cache[0], preferred_element_type=jnp.float32)
    scores = jnp.where(live, scores * spread[0][:, None, :] * inv_root, -1e30)
    flat_new_k = key_new.reshape(requests, steps * kv_heads, dim)
    flat_new_v = value_new.reshape(requests, steps * kv_heads, dim)
    new_column = jnp.arange(steps * kv_heads, dtype=jnp.int32)
    new_live = (
        (row_kv[:, None] == (new_column % kv_heads)[None, :])
        & ((new_column // kv_heads)[None, :] <= (row // heads)[:, None])
        & first
    )[None]
    recent = jnp.einsum("rqd,rjd->rqj", flat_query, flat_new_k, preferred_element_type=jnp.float32)
    recent = jnp.where(new_live, recent * inv_root, -1e30)
    top = jnp.maximum(jnp.max(scores, axis=-1), jnp.max(recent, axis=-1))
    weight = jnp.where(live, jnp.exp(scores - top[..., None]), 0.0)
    new_weight = jnp.where(new_live, jnp.exp(recent - top[..., None]), 0.0)
    total = jnp.sum(weight, axis=-1) + jnp.sum(new_weight, axis=-1)
    scaled = (weight * spread[1][:, None, :]).astype(jnp.bfloat16)
    mix = jnp.einsum("rqp,rpd->rqd", scaled, flat_cache[1], preferred_element_type=jnp.float32)
    mix = mix + jnp.einsum(
        "rqj,rjd->rqd", new_weight.astype(jnp.bfloat16), flat_new_v, preferred_element_type=jnp.float32
    )
    rows = requests * steps
    return mix.reshape(rows, heads, dim), top.reshape(rows, heads), total.reshape(rows, heads)


def merge(mixes, tops, totals):
    best = tops[0]
    for top in tops[1:]:
        best = jnp.maximum(best, top)
    factors = [jnp.exp(top - best) for top in tops]
    summed = paired_sum([total * factor for total, factor in zip(totals, factors)])
    mixed = paired_sum(
        [mix.astype(jnp.float32) * factor[..., None] for mix, factor in zip(mixes, factors)]
    )
    return (mixed / summed[..., None]).astype(jnp.bfloat16)


def plain(
    hidden,
    query,
    key_new,
    value_new,
    kv_cache,
    kv_scale,
    context_len,
    attn_out_weight,
    norm_gain,
    in_weight,
    conv_weight,
    conv_bias,
    conv_state,
    xproj_weight,
    dt_weight,
    dt_bias,
    decay_rate,
    skip_gain,
    ssm_state,
    mamba_out_weight,
):
    requests, steps = hidden.shape[:2]
    rows = requests * steps
    seq_count = lax.axis_size("seq")
    hs_count = lax.axis_size(HS)
    hs_index = lax.axis_index(HS)
    heads = query.shape[2]
    dim = query.shape[3]
    mix, top, total = plain_attention(query, key_new, value_new, kv_cache, kv_scale, context_len)
    mixes, tops, totals = (lax.all_gather(part, "seq") for part in (mix, top, total))
    every = range(seq_count)
    own_heads = merge([mixes[k] for k in every], [tops[k] for k in every], [totals[k] for k in every])
    every_head = lax.all_gather(own_heads.reshape(rows, heads * dim), HS, axis=1, tiled=True)
    width_in = attn_out_weight.shape[0]
    chosen = lax.dynamic_slice_in_dim(every_head, lax.axis_index("seq") * width_in, width_in, 1)
    attended = sum_over(
        jnp.dot(chosen, attn_out_weight, preferred_element_type=jnp.float32), "seq", jnp.bfloat16
    )
    residual = hidden.astype(jnp.float32).reshape(rows, -1) + attended
    features = residual.shape[1] * hs_count
    squares = jnp.sum(residual * residual, axis=-1, keepdims=True)
    gained = (residual * norm_gain).astype(jnp.bfloat16)
    projected = jnp.einsum("nd,cde->nce", gained, in_weight, preferred_element_type=jnp.float32)
    own_width = conv_weight.shape[0]
    upper, lower = split_pair(squares)

    def block_for(index):
        block = lax.dynamic_slice_in_dim(projected, index * own_width, own_width, 2)
        return block.reshape(rows, 2 * own_width)

    channels = block_for(hs_index)
    for hop in range(1, hs_count):
        block = jnp.concatenate([block_for((hs_index + hop) % hs_count), upper, lower], axis=1)
        part = shifted(block.astype(jnp.bfloat16), HS, hop).astype(jnp.float32)
        channels = channels + part[:, : 2 * own_width]
        squares = squares + part[:, 2 * own_width : 2 * own_width + 1] + part[:, 2 * own_width + 1 :]
    channels = channels * lax.rsqrt(squares / features + EPS)
    conv_in = channels[:, :own_width].astype(jnp.bfloat16)
    gate_in = channels[:, own_width:].astype(jnp.bfloat16)
    window = jnp.concatenate(
        [
            conv_state.astype(jnp.float32),
            conv_in.astype(jnp.float32).reshape(requests, steps, own_width),
        ],
        axis=1,
    )
    conv_sum = jnp.zeros((requests, steps, own_width), jnp.float32) + conv_bias
    for tap in range(conv_weight.shape[1]):
        conv_sum = conv_sum + conv_weight[:, tap].astype(jnp.float32) * window[:, tap : tap + steps, :]
    conv_out = jax.nn.silu(conv_sum).astype(jnp.bfloat16).reshape(rows, own_width)
    mixing = jnp.dot(conv_out, xproj_weight, preferred_element_type=jnp.float32)
    mixing = sum_over(sum_over(mixing, HS), "seq")
    low_width = dt_weight.shape[0]
    state_width = decay_rate.shape[1]
    low_rank = rms_unit(mixing[:, :low_width]).astype(jnp.bfloat16)
    input_mat = rms_unit(mixing[:, low_width : low_width + state_width]).reshape(
        requests, steps, state_width
    )
    output_mat = rms_unit(mixing[:, low_width + state_width :]).reshape(requests, steps, state_width)
    delta = jax.nn.softplus(
        jnp.dot(low_rank, dt_weight, preferred_element_type=jnp.float32) + dt_bias
    ).reshape(requests, steps, own_width)
    signal = conv_out.astype(jnp.float32).reshape(requests, steps, own_width)
    memory = ssm_state
    outputs = []
    for moment in range(steps):
        step_now = delta[:, moment]
        memory = (
            jnp.exp(-step_now[..., None] * decay_rate) * memory
            + (step_now * signal[:, moment])[..., None] * input_mat[:, moment][:, None, :]
        )
        outputs.append(
            jnp.sum(memory * output_mat[:, moment][:, None, :], axis=-1)
            + skip_gain * signal[:, moment]
        )
    stacked = jnp.stack(outputs, axis=1).reshape(rows, own_width)
    gated_out = (stacked * jax.nn.silu(gate_in.astype(jnp.float32))).astype(jnp.bfloat16)
    gated_block = lax.all_gather(gated_out, HS, axis=1, tiled=True)
    mamba_part = sum_over(
        jnp.dot(gated_block, mamba_out_weight, preferred_element_type=jnp.float32), "seq", jnp.bfloat16
    )
    final = (residual + mamba_part).astype(jnp.bfloat16).reshape(requests, steps, -1)
    return (final, memory)


def local(
    hidden,
    query,
    key_new,
    value_new,
    kv_cache,
    kv_scale,
    context_len,
    attn_out_weight,
    norm_gain,
    in_weight,
    conv_weight,
    conv_bias,
    conv_state,
    xproj_weight,
    dt_weight,
    dt_bias,
    decay_rate,
    skip_gain,
    ssm_state,
    mamba_out_weight,
):
    requests, steps = hidden.shape[:2]
    rows = requests * steps
    seq_count = lax.axis_size("seq")
    hs_count = lax.axis_size(HS)
    heads, dim = query.shape[2:]
    own_width = conv_weight.shape[0]
    if (
        lax.axis_size("head") != 2
        or lax.axis_size("sub") != 2
        or seq_count != hs_count
        or own_width % LANES
        or dim != LANES
        or (rows * heads) % LANES
        or rows % 16
    ):
        return plain(
            hidden,
            query,
            key_new,
            value_new,
            kv_cache,
            kv_scale,
            context_len,
            attn_out_weight,
            norm_gain,
            in_weight,
            conv_weight,
            conv_bias,
            conv_state,
            xproj_weight,
            dt_weight,
            dt_bias,
            decay_rate,
            skip_gain,
            ssm_state,
            mamba_out_weight,
        )
    part, out_rows = attention(
        query, key_new, value_new, kv_cache, kv_scale, context_len, [whole_job(attn_out_weight)]
    )
    columns = lambda flip: block_job(in_weight, own_width, flip)
    far_columns, chip_columns = bring([columns(3), columns(2)], part)
    place = range(hs_count)
    parts = [
        lax.ppermute(
            part,
            ("seq",) + HS,
            [
                (s * hs_count + j, j * hs_count + ((s // 2 + turn) % 2) * 2 + s % 2)
                for s in range(seq_count)
                for j in place
            ],
        )
        for turn in range(2)
    ]
    parts, far_columns, chip_columns = lax.optimization_barrier((parts, far_columns, chip_columns))
    parts = parts + [crossed(arrived, "sub", 1) for arrived in parts]
    partial = merge_project(parts, out_rows, rows, heads, dim)
    core_columns, own_columns = bring([columns(1), columns(0)], partial)
    terms, core_columns, own_columns = lax.optimization_barrier(
        (crossed_all(partial, "seq"), core_columns, own_columns)
    )
    residual, gained, stats = add_residual(hidden, terms, norm_gain)
    features = residual.shape[1] * hs_count
    for_far = crossed(project_block(gained, far_columns, own_width, jnp.bfloat16, stats), "sub", 1)
    block = relay(project_block(gained, chip_columns, own_width, jnp.float32, None), for_far, stats)
    received = crossed(block, "head", 1)
    late, block = lax.optimization_barrier((gained, block))
    near = crossed(project_block(late, core_columns, own_width, jnp.bfloat16, None), "sub", 1)
    own = project_block(late, own_columns, own_width, jnp.float32, None)
    conv, gate, mixing = convolve(
        own,
        near,
        received,
        [stats, for_far],
        conv_state.transpose(1, 0, 2),
        conv_weight.T,
        conv_bias.reshape(1, -1),
        xproj_weight.T,
        features,
    )
    mixing = add_up([mixing, crossed(mixing, "sub", 1)], 1_000_000)
    base = lambda s, x, c: s * hs_count + x * 2 + c
    arrived = [
        lax.ppermute(
            mixing,
            ("seq",) + HS,
            [(base(s, x, 1), base(s ^ flip, x ^ 1, 1)) for s in range(seq_count) for x in range(2)]
            + [(base(s, x, 0), base(s ^ flip, x, 0)) for s in range(seq_count) for x in range(2) if flip],
        )
        for flip in range(seq_count - 1, -1, -1)
    ]
    line = add_up([jnp.where(lax.axis_index("sub") == 0, mixing, 0.0)] + arrived, FLOPS_AHEAD//4)
    mixing = add_up([line, crossed(line, "sub", 1)], 1_000_000)
    gated, state = scan_states(
        mixing,
        conv,
        gate,
        dt_weight,
        dt_bias.reshape(1, -1),
        decay_rate.T,
        skip_gain.reshape(1, -1),
        ssm_state.transpose(0, 2, 1),
    )
    first = project_out([gated], [0], mamba_out_weight, None)
    blocks, first = lax.optimization_barrier((crossed_all(gated, HS), first))
    partial = project_out(blocks[1:], list(place)[1:], mamba_out_weight, first)
    final = finish(residual, crossed_all(partial, "seq"), requests)
    return final, state.transpose(0, 2, 1)


def solution(mesh):
    return jax.shard_map(
        local,
        mesh=mesh,
        in_specs=(
            P("groups", None, HS),
            P("groups", None, HS, None),
            P("groups", None, HS, None),
            P("groups", None, HS, None),
            P(None, "groups", "seq", HS, None),
            P(None, "groups", HS, "seq"),
            P("groups"),
            P("seq", HS),
            P(HS),
            P(None, HS, "seq"),
            P(("seq",) + HS, None),
            P(("seq",) + HS),
            P("groups", None, ("seq",) + HS),
            P(("seq",) + HS, None),
            P(None, ("seq",) + HS),
            P(("seq",) + HS),
            P(("seq",) + HS, None),
            P(("seq",) + HS),
            P("groups", ("seq",) + HS, None),
            P("seq", HS),
        ),
        out_specs=(P("groups", None, HS), P("groups", ("seq",) + HS, None)),
        check_vma=False,
    )
```
